512 devices in a mesh: gz: 16 (over x, y), ta: 32 (over z, core).
Axes of the slice: x: 4, y: 4, z: 16, core: 2. Of those that a mesh axis runs over, the one named last changes fastest.
Arguments:
- links: float32 [4, 18, 32, 32, 1024], P(None, None, 'gz', 'ta'), may hold values from -1 to 1, as said below
Outputs:
- fixed_links: float32 [4, 18, 32, 32, 1024], P(None, None, 'gz', 'ta')
The draws below stay inside these ranges and needn't reach their ends.
Inputs may be any that keep to these rules, and one draw needn't show every extreme that they name: `links`: every link is a special unitary 3 by 3 matrix.
All inputs are finite; a program needn't handle non-finite values.
Results may differ from the reference program's by a relative error of at most 0.0001.
Values sent between devices are 32-bit elements; how exact they have to be, the bound alone decides.
A program may use at most 64 MiB of HBM per device.

```python
import jax
import jax.numpy as jnp
from jax import lax

LX = 32
LY = 32
ITERS = 2
NZ = 32
NT = 32


def row_normalized(vec_real, vec_imag):
    scale = lax.rsqrt(jnp.sum(vec_real * vec_real + vec_imag * vec_imag, axis=0))
    return (vec_real * scale, vec_imag * scale)


def orthonormal_rows(p_real, p_imag):
    first_real, first_imag = row_normalized(p_real[0], p_imag[0])
    inner_real = jnp.sum(first_real * p_real[1] + first_imag * p_imag[1], axis=0)
    inner_imag = jnp.sum(first_real * p_imag[1] - first_imag * p_real[1], axis=0)
    second_real, second_imag = row_normalized(p_real[1] - (inner_real * first_real - inner_imag * first_imag), p_imag[1] - (inner_real * first_imag + inner_imag * first_real))
    third_real = []
    third_imag = []
    for column in range(3):
        next_col = (column + 1) % 3
        last_col = (column + 2) % 3
        cross_real = first_real[next_col] * second_real[last_col] - first_imag[next_col] * second_imag[last_col] - (first_real[last_col] * second_real[next_col] - first_imag[last_col] * second_imag[next_col])
        cross_imag = first_real[next_col] * second_imag[last_col] + first_imag[next_col] * second_real[last_col] - (first_real[last_col] * second_imag[next_col] + first_imag[last_col] * second_real[next_col])
        third_real.append(cross_real)
        third_imag.append(-cross_imag)
    return (jnp.stack([first_real, second_real, jnp.stack(third_real)]), jnp.stack([first_imag, second_imag, jnp.stack(third_imag)]))


def draw_links(key, part):
    key = jax.random.fold_in(key, 7)
    key_real, key_imag = jax.random.split(key)
    draw_shape = (3, 3, 4, NZ, NT, LX * LY)
    noise_real = jax.random.normal(key_real, draw_shape, jnp.float32)
    noise_imag = jax.random.normal(key_imag, draw_shape, jnp.float32)
    spread = 1.5
    unit_matrix = jnp.eye(3, dtype=jnp.float32).reshape(3, 3, 1, 1, 1, 1)
    rows_real, rows_imag = orthonormal_rows(unit_matrix + spread * noise_real, spread * noise_imag)
    stacked = jnp.stack([rows_real, rows_imag], axis=2)
    return jnp.transpose(stacked, (3, 0, 1, 2, 4, 5, 6)).reshape(4, 18, NZ, NT, LX * LY)


def setup_inputs(seed: int = 0) -> dict:
    key_of = jax.random.split(jax.random.key(seed), 2)
    return {
        "links": draw_links(jax.random.fold_in(key_of[1], 71), 0),
    }


STEP_SIZE = 0.08

def unit_like(template):
    return jnp.eye(3, dtype=jnp.float32).reshape((3, 3) + (1,) * (template.ndim - 2))

def mat_product(left_real, left_imag, right_real, right_imag):
    out_real = lax.optimization_barrier(jnp.sum(left_real[:, :, None] * right_real[None], axis=1)) - lax.optimization_barrier(jnp.sum(left_imag[:, :, None] * right_imag[None], axis=1))
    out_imag = lax.optimization_barrier(jnp.sum(left_real[:, :, None] * right_imag[None], axis=1)) + lax.optimization_barrier(jnp.sum(left_imag[:, :, None] * right_real[None], axis=1))
    return (out_real, out_imag)

def antihermitian(delta_real, delta_imag):
    unit_matrix = unit_like(delta_real)
    part_real = 0.5 * (delta_real - jnp.swapaxes(delta_real, 0, 1))
    part_imag = 0.5 * (delta_imag + jnp.swapaxes(delta_imag, 0, 1))
    trace_third = (part_imag[0, 0] + part_imag[1, 1] + part_imag[2, 2]) / 3.0
    return (part_real, part_imag - unit_matrix * trace_third)

def polynomial(a_real, a_imag):
    unit_matrix = unit_like(a_real)
    inner_real = unit_matrix + a_real / 3.0
    inner_imag = a_imag / 3.0
    half_real, half_imag = mat_product(0.5 * a_real, 0.5 * a_imag, inner_real, inner_imag)
    outer_real, outer_imag = mat_product(a_real, a_imag, unit_matrix + half_real, half_imag)
    return (unit_matrix + outer_real, outer_imag)

def normalized(vec_real, vec_imag):
    scale = lax.rsqrt(lax.optimization_barrier(jnp.sum(vec_real * vec_real + vec_imag * vec_imag, axis=0)))
    return (vec_real * scale, vec_imag * scale)

def unitarize(p_real, p_imag):
    first_real, first_imag = normalized(p_real[0], p_imag[0])
    inner_real = lax.optimization_barrier(jnp.sum(first_real * p_real[1] + first_imag * p_imag[1], axis=0))
    inner_imag = lax.optimization_barrier(jnp.sum(first_real * p_imag[1] - first_imag * p_real[1], axis=0))
    second_real, second_imag = normalized(p_real[1] - (inner_real * first_real - inner_imag * first_imag), p_imag[1] - (inner_real * first_imag + inner_imag * first_real))
    third_real = []
    third_imag = []
    for column in range(3):
        next_col = (column + 1) % 3
        last_col = (column + 2) % 3
        cross_real = first_real[next_col] * second_real[last_col] - first_imag[next_col] * second_imag[last_col] - (first_real[last_col] * second_real[next_col] - first_imag[last_col] * second_imag[next_col])
        cross_imag = first_real[next_col] * second_imag[last_col] + first_imag[next_col] * second_real[last_col] - (first_real[last_col] * second_imag[next_col] + first_imag[last_col] * second_real[next_col])
        third_real.append(cross_real)
        third_imag.append(-cross_imag)
    return (jnp.stack([first_real, second_real, jnp.stack(third_real)]), jnp.stack([first_imag, second_imag, jnp.stack(third_imag)]))

def sine_square(length):
    mode_index = jnp.arange(length, dtype=jnp.float32)
    sines = jnp.sin(jnp.pi * mode_index / length)
    return 4.0 * sines * sines

def inverse_momenta():
    total = sine_square(NZ)[:, None, None, None] + sine_square(NT)[None, :, None, None] + (sine_square(LX)[None, None, :, None] + sine_square(LY)[None, None, None, :])
    positive = total > 0.001
    return jnp.where(positive, 16.0 / jnp.where(positive, total, 1.0), 0.0)

def reference(links):
    blocks = links.reshape(4, 3, 3, 2, NZ, NT, LX, LY)
    link_real = blocks[:, :, :, 0]
    link_imag = blocks[:, :, :, 1]
    weights = inverse_momenta()
    lattice_axes = (4, 5, 2, 3)
    for sweep_index in range(ITERS):
        delta_real = jnp.zeros_like(link_real[0])
        delta_imag = jnp.zeros_like(link_imag[0])
        for direction in range(4):
            delta_real = delta_real + jnp.roll(link_real[direction], 1, lattice_axes[direction]) - link_real[direction]
            delta_imag = delta_imag + jnp.roll(link_imag[direction], 1, lattice_axes[direction]) - link_imag[direction]
        anti_real, anti_imag = antihermitian(delta_real, delta_imag)
        spectrum = jnp.fft.fftn(anti_real + 1j * anti_imag, axes=(2, 3, 4, 5))
        smooth = jnp.fft.ifftn(spectrum * weights, axes=(2, 3, 4, 5))
        poly_real, poly_imag = polynomial(STEP_SIZE * smooth.real, STEP_SIZE * smooth.imag)
        gauge_real, gauge_imag = unitarize(poly_real, poly_imag)
        new_real = []
        new_imag = []
        for direction in range(4):
            left_real, left_imag = mat_product(gauge_real, gauge_imag, link_real[direction], link_imag[direction])
            ahead_real = jnp.roll(gauge_real, -1, lattice_axes[direction])
            ahead_imag = jnp.roll(gauge_imag, -1, lattice_axes[direction])
            turned_real, turned_imag = mat_product(left_real, left_imag, jnp.swapaxes(ahead_real, 0, 1), -jnp.swapaxes(ahead_imag, 0, 1))
            new_real.append(turned_real)
            new_imag.append(turned_imag)
        link_real = jnp.stack(new_real)
        link_imag = jnp.stack(new_imag)
    return jnp.stack([link_real, link_imag], axis=3).reshape(4, 18, NZ, NT, LX * LY)
```

```python
import functools
import math

import jax
import jax.numpy as jnp
import numpy as np
from jax import lax
from jax.experimental import pallas as pl
from jax.experimental.pallas import tpu as pltpu
from jax.sharding import PartitionSpec as P

ITERS = 2
STEP_SIZE = 0.08
LINE = 32
GZ = 16
TA = 32
PAIRS = ((0, 1), (0, 2), (1, 2))
LOGICAL = pl.DeviceIdType.LOGICAL
F32 = jnp.float32
BF16 = jnp.bfloat16


def halves(table):
    high = table.astype(jnp.bfloat16)
    return high, (table - high.astype(np.float64)).astype(jnp.bfloat16)


def tables():
    phase = 2.0 * np.pi * (np.outer(np.arange(LINE), np.arange(LINE)) % LINE) / LINE
    plane = np.kron(np.eye(4), (np.cos(phase) + np.sin(phase)) / np.sqrt(LINE))
    sines = 4.0 * np.sin(np.pi * np.arange(LINE) / LINE) ** 2
    row = np.arange(128)
    momenta = sines[row // 8 + 16 * (row % 2)][:, None] + np.tile(sines, 4)[None, :]
    tiles = np.broadcast_to(sines[:, None, None], (LINE, 8, 128))
    return (
        np.concatenate(halves(plane), axis=0),
        momenta.reshape(16, 8, 128).astype(np.float32),
        np.ascontiguousarray(tiles).astype(np.float32),
    )


def times(u, v):
    return (u[0] * v[0] - u[1] * v[1], u[0] * v[1] + u[1] * v[0])


def times_conj(u, v):
    return (u[0] * v[0] + u[1] * v[1], u[1] * v[0] - u[0] * v[1])


def plus(u, v):
    return (u[0] + v[0], u[1] + v[1])


def minus(u, v):
    return (u[0] - v[0], u[1] - v[1])


def conj(u):
    return (u[0], -u[1])


def scaled(u, factor):
    return (u[0] * factor, u[1] * factor)


def total(terms):
    return functools.reduce(plus, terms)


def product(left, right):
    return [[total([times(left[a][j], right[j][b]) for j in range(3)]) for b in range(3)] for a in range(len(left))]


def product_dagger(left, right):
    return [[total([times_conj(left[a][j], right[b][j]) for j in range(3)]) for b in range(3)] for a in range(len(left))]


def cross_conj(u, v):
    row = []
    for c in range(3):
        n, m = (c + 1) % 3, (c + 2) % 3
        row.append(conj(minus(times(u[n], v[m]), times(u[m], v[n]))))
    return row


def each(function, matrix):
    return [[(function(e[0]), function(e[1])) for e in row] for row in matrix]


def lanes(v):
    return lax.broadcasted_iota(jnp.int32, v.shape, v.ndim - 1)


def roll(v, shift, axis):
    return pltpu.roll(v, shift, axis)


def behind_x(v):
    moved = roll(v, 32, v.ndim - 1)
    return jnp.where(lanes(v) < 32, roll(moved, 1, v.ndim - 2), moved)


def ahead_x(v):
    moved = roll(v, 96, v.ndim - 1)
    return jnp.where(lanes(v) >= 96, roll(moved, 7, v.ndim - 2), moved)


def behind_y(v):
    return jnp.where(lanes(v) % 32 == 0, roll(v, 97, v.ndim - 1), roll(v, 1, v.ndim - 1))


def ahead_y(v):
    return jnp.where(lanes(v) % 32 == 31, roll(v, 31, v.ndim - 1), roll(v, 127, v.ndim - 1))


def behind_z(v, edge):
    return jnp.concatenate([edge[None], v[:1]], axis=0)


def ahead_z(v, edge):
    return jnp.concatenate([v[1:], edge[None]], axis=0)


def projected(u):
    third = (u[0][0][1] + u[1][1][1] + u[2][2][1]) * (1.0 / 3.0)
    return (
        [u[a][b][0] - u[b][a][0] for a, b in PAIRS]
        + [u[a][b][1] + u[b][a][1] for a, b in PAIRS]
        + [u[0][0][1] - third, u[1][1][1] - third]
    )


def block_transpose(planes):
    lane = lanes(planes[0])
    axis = planes[0].ndim - 1
    low = lane < 64
    even = (lane // 32) % 2 == 0
    first = [jnp.where(low, planes[p], roll(planes[p + 2], 64, axis)) for p in range(2)]
    second = [jnp.where(low, roll(planes[p], 64, axis), planes[p + 2]) for p in range(2)]
    out = []
    for one, two in (first, second):
        out.append(jnp.where(even, one, roll(two, 32, axis)))
        out.append(jnp.where(even, roll(one, 96, axis), two))
    return out


def rows_of(v):
    return lax.broadcasted_iota(jnp.int32, v.shape, v.ndim - 2)


def bit_exchange(one, two, stride):
    clear = lax.rem(lax.div(rows_of(one), stride), 2) == 0
    return (
        jnp.where(clear, one, roll(two, stride, one.ndim - 2)),
        jnp.where(clear, roll(one, 8 - stride, one.ndim - 2), two),
    )


def middle_exchange(v):
    pair = lax.div(rows_of(v), 2)
    return jnp.where(pair == 1, roll(v, 6, 0), jnp.where(pair == 2, roll(v, 2, 0), v))


def hartley(v):
    size = len(v)
    if size == 1:
        return v
    even, odd = hartley(v[0::2]), hartley(v[1::2])
    half = size // 2
    out = [None] * size
    for k in range(half):
        turned = odd[k]
        if k and 4 * k != size:
            angle = 2.0 * math.pi * k / size
            turned = odd[k] * math.cos(angle) + odd[half - k] * math.sin(angle)
        out[k], out[k + half] = even[k] + turned, even[k] - turned
    return out


def bit_clear(v, stride):
    return lax.rem(lax.div(rows_of(v), stride), 2) == 0


def rotated(v, stride):
    low = bit_clear(v[0], stride)
    out = list(v)
    for k in range(1, 16):
        if k != 8:
            angle = math.pi * k / 16
            out[k] = v[k] * jnp.where(low, 1.0, math.cos(angle)) + v[16 - k] * jnp.where(low, 0.0, math.sin(angle))
    return out


def butterflies(v, stride):
    low = bit_clear(v[0], stride)
    out = []
    for e in v:
        other = roll(e, stride, 0)
        if stride != 4:
            other = jnp.where(low, roll(e, 8 - stride, 0), other)
        out.append(other + jnp.where(low, e, -e))
    return out


def fine_to_coarse(v, stride):
    return butterflies(rotated(hartley(v), stride), stride)


def coarse_to_fine(v, stride):
    return hartley(rotated(butterflies(v, stride), stride))


def tiles_of(matrix):
    return [matrix[8 * i : 8 * i + 8] for i in range(16)]


def plane_forward(fields, table):
    parts = [block_transpose(fields[tl]) for tl in range(2)]
    tiles = [None] * 16
    for b in range(4):
        traded = [bit_exchange(parts[tl][b][0], parts[tl][b][1], 2) for tl in range(2)]
        for bit in range(2):
            tiles[8 * bit + b], tiles[8 * bit + 4 + b] = bit_exchange(traded[0][bit], traded[1][bit], 1)
    tiles = [middle_exchange(v) for v in coarse_to_fine(tiles, 4)]
    return tiles if table is None else right(jnp.concatenate(tiles, axis=0), table)


def plane_inverse(matrix, table):
    tiles = fine_to_coarse([middle_exchange(v) for v in tiles_of(right(matrix, table))], 4)
    blocks = [[None] * 4 for _ in range(2)]
    for b in range(4):
        pairs = [bit_exchange(tiles[8 * bit + b], tiles[8 * bit + 4 + b], 1) for bit in range(2)]
        for tl in range(2):
            blocks[tl][b] = jnp.stack(bit_exchange(pairs[0][tl], pairs[1][tl], 2))
    return [block_transpose(blocks[tl]) for tl in range(2)]


def split(v):
    high = v.astype(BF16)
    return high, (v - high.astype(F32)).astype(BF16)


def right(v, table):
    table_high, table_low = table[pl.ds(0, 128)], table[pl.ds(128, 128)]
    high, low = split(v)
    return jnp.dot(
        jnp.concatenate([high, low, high], axis=1),
        jnp.concatenate([table_high, table_high, table_low], axis=0),
        preferred_element_type=F32,
    )


def store_tiles(ref, tiles):
    for i, tile in enumerate(tiles):
        ref[pl.ds(8 * i, 8)] = tile


def load_tiles(ref):
    return [ref[pl.ds(8 * i, 8)] for i in range(16)]


def inverse_momenta(momenta, tiles):
    row = lax.broadcasted_iota(jnp.int32, (8, 128), 0)
    own = jnp.where(row < 4, tiles[0], tiles[1]) + jnp.where(lax.rem(lax.div(row, 2), 2) == 0, tiles[2], tiles[3])
    squares = momenta + own[None]
    positive = squares > 0.001
    return jnp.where(positive, (16.0 * STEP_SIZE / LINE**3) / jnp.where(positive, squares, 1.0), 0.0).reshape(128, 128)


def normalized(row):
    norm = functools.reduce(jnp.add, [e[0] * e[0] + e[1] * e[1] for e in row])
    scale = lax.rsqrt(norm)
    return [scaled(e, scale) for e in row]


def gauge_rows(fields):
    a, b, c = [(fields[i], fields[3 + i]) for i in range(3)]
    h0, h1 = fields[6], fields[7]
    h2 = -(h0 + h1)
    aa, bb, cc = [e[0] * e[0] + e[1] * e[1] for e in (a, b, c)]
    sixth = 1.0 / 6.0

    def turned(u, h):
        return (-(u[1] * h), u[0] * h)

    s01 = minus(turned(a, -h2), times_conj(b, c))
    s02 = plus(turned(b, -h1), times(a, c))
    s12 = minus(turned(c, -h0), times_conj(b, a))
    d0 = 1.0 - (h0 * h0 + aa + bb) * sixth
    d1 = 1.0 - (h1 * h1 + aa + cc) * sixth
    d2 = 1.0 - (h2 * h2 + bb + cc) * sixth

    def upper(u, s):
        return (0.5 * u[0] + s[0] * sixth, 0.5 * u[1] + s[1] * sixth)

    def lower(u, s):
        return (s[0] * sixth - 0.5 * u[0], 0.5 * u[1] - s[1] * sixth)

    inner = [
        [(d0, 0.5 * h0), upper(a, s01), upper(b, s02)],
        [lower(a, s01), (d1, 0.5 * h1), upper(c, s12)],
        [lower(b, s02), lower(c, s12), (d2, 0.5 * h2)],
    ]
    minus_a = (-a[0], a[1])
    p0 = [total([turned(inner[0][j], h0), times(a, inner[1][j]), times(b, inner[2][j])]) for j in range(3)]
    p1 = [total([times(minus_a, inner[0][j]), turned(inner[1][j], h1), times(c, inner[2][j])]) for j in range(3)]
    p0[0] = (p0[0][0] + 1.0, p0[0][1])
    p1[1] = (p1[1][0] + 1.0, p1[1][1])
    row0 = normalized(p0)
    overlap = total([times_conj(p1[j], row0[j]) for j in range(3)])
    row1 = normalized([minus(p1[j], times(overlap, row0[j])) for j in range(3)])
    return [row0, row1]


def completed(rows):
    return rows + [cross_conj(rows[0], rows[1])]


def load_matrix(ref):
    return [[(ref[2 * (3 * a + b)], ref[2 * (3 * a + b) + 1]) for b in range(3)] for a in range(3)]


def store_matrix(ref, matrix):
    for a, row in enumerate(matrix):
        for b, entry in enumerate(row):
            ref[2 * (3 * a + b)] = entry[0]
            ref[2 * (3 * a + b) + 1] = entry[1]


def load_rows(ref):
    return [[(ref[2 * (3 * a + b)], ref[2 * (3 * a + b) + 1]) for b in range(3)] for a in range(2)]


def kernel(
    links, table_hbm, momenta_hbm, sines_hbm, out,
    u, edge_z, edge_t, sum_send, sums, line_t_send, line_t, line_z_send, line_z, table, momenta, sines, weights,
    plane_send, plane_recv, ring_send, ring_recv, smooth, smooth_za, smooth_zb, smooth_ta, smooth_tb, gauge,
    load_sems, edge_ss, edge_rs, first_ss, first_rs, plane_ss, plane_rs, ring_ss, ring_rs, halo_ss, halo_rs, out_sems,
):
    gz = lax.axis_index("gz")
    ta = lax.axis_index("ta")
    gz_x, gz_y = lax.div(gz, 4), lax.rem(gz, 4)
    chip, core = lax.div(ta, 2), lax.rem(ta, 2)
    other_core = 1 - core

    def device(z, t_chip, which):
        return z * TA + 2 * t_chip + which

    sibling = device(gz, chip, other_core)
    z_next, z_last = lax.rem(gz + 1, GZ), lax.rem(gz + GZ - 1, GZ)
    t_next, t_last = lax.rem(chip + 1, GZ), lax.rem(chip + GZ - 1, GZ)

    def around(place, step, size):
        return lax.rem(place + step, size)

    offsets = [(dx, dy) for dx in range(4) for dy in range(4) if dx or dy]
    offsets.sort(key=lambda o: -(min(o[0], 4 - o[0]) + min(o[1], 4 - o[1])))
    columns = [around(gz_x, dx, 4) for dx in range(4)]
    lines_y = [around(gz_y, dy, 4) for dy in range(4)]
    plane_partners = [(i, device(i, chip, core)) for i in [columns[dx] * 4 + lines_y[dy] for dx, dy in offsets]]
    steps = sorted(range(1, 16), key=lambda d: -min(d, 16 - d))
    ring_partners = [(i, device(gz, i, core)) for i in [around(chip, d, 16) for d in steps]]
    crossed = [
        device(gz, t_last, other_core),
        device(gz, t_next, other_core),
        device(z_last, chip, other_core),
        device(z_next, chip, other_core),
    ]

    barrier = pltpu.get_barrier_semaphore()

    def greet(target):
        pl.semaphore_signal(barrier, inc=1, device_id=target, device_id_type=LOGICAL)

    loads = [pltpu.make_async_copy(links.at[mu], u.at[core, mu], load_sems.at[mu]) for mu in range(4)]
    constants = [
        pltpu.make_async_copy(momenta_hbm, momenta, load_sems.at[4]),
        pltpu.make_async_copy(sines_hbm.at[chip], sines.at[0], load_sems.at[5]),
        pltpu.make_async_copy(sines_hbm.at[chip + 16], sines.at[1], load_sems.at[6]),
        pltpu.make_async_copy(sines_hbm.at[2 * gz], sines.at[2], load_sems.at[7]),
        pltpu.make_async_copy(sines_hbm.at[2 * gz + 1], sines.at[3], load_sems.at[8]),
        pltpu.make_async_copy(table_hbm, table, load_sems.at[9]),
    ]
    for copy in loads[::-1] + constants[-1:]:
        copy.start()
    for _, target in ring_partners + plane_partners:
        greet(target)
    for target in crossed + [sibling]:
        greet(target)
    for copy in constants[:-1]:
        copy.start()

    def transfer(src, dst, send_sem, recv_sem, target):
        return pltpu.make_async_remote_copy(
            src_ref=src, dst_ref=dst, send_sem=send_sem, recv_sem=recv_sem, device_id=target, device_id_type=LOGICAL
        )

    def exchange(sends, recvs, ss, rs, slot, partners, me, neighbour):
        send, recv = sends.at[slot], recvs.at[slot]
        own = pl.ds(pl.multiple_of(me * 8, 8), 8)

        for index, target in partners:
            theirs = pl.ds(pl.multiple_of(index * 8, 8), 8)
            transfer(send.at[theirs], recv.at[own], ss.at[slot], rs.at[slot], target).start()
        recv[own] = send[own]
        part = pl.ds(0, 120)
        return transfer(send.at[part], recv.at[part], ss.at[slot], rs.at[slot], neighbour)

    def plane_exchange(slot):
        neighbour = device(z_next, chip, core)
        return exchange(plane_send, plane_recv, plane_ss, plane_rs, slot, plane_partners, gz, neighbour)

    def ring_exchange(slot):
        neighbour = device(gz, t_next, core)
        return exchange(ring_send, ring_recv, ring_ss, ring_rs, slot, ring_partners, chip, neighbour)

    def halo_transfers(it):
        mine = smooth.at[it, core]
        ss, rs = halo_ss, halo_rs
        to_sibling = transfer(mine, mine, ss.at[it, 0], rs.at[it, 0], sibling)
        groups = []
        for which, (src, dst, z, t_chip) in enumerate(
            (
                (mine.at[0], smooth_ta.at[it, core], gz, t_last),
                (mine.at[:, :, 0], smooth_za.at[it, core], z_last, chip),
                (mine.at[1], smooth_tb.at[it, core], gz, t_next),
                (mine.at[:, :, 1], smooth_zb.at[it, core], z_next, chip),
            )
        ):
            groups.append(
                [
                    transfer(src, dst, ss.at[it, 1 + 2 * which + h], rs.at[it, 1 + which], device(z, t_chip, h))
                    for h in range(2)
                ]
            )
        return to_sibling, groups

    def arrived(it, which, ref):
        transfer(ref.at[it], ref.at[it], halo_ss.at[it, 0], halo_rs.at[it, 1 + which], sibling).wait_recv()

    lane_core = lax.broadcasted_iota(jnp.int32, (8, 128), 0) * 0 + core
    first_half = lane_core == 0

    def own_half(fields):
        return [jnp.where(jnp.broadcast_to(first_half, one.shape), one, two) for one, two in zip(fields[:4], fields[4:])]

    for copy in loads:
        copy.wait()
    lines = [projected(load_matrix(u.at[core, mu])) for mu in range(4)]
    planes = []
    for f in range(8):
        x, y, z, t = [lines[mu][f] for mu in range(4)]
        inner = jnp.concatenate([jnp.zeros((1, 8, 128), F32), z[:1]], axis=0)
        total_here = ((behind_x(x) - x) + (behind_y(y) - y)) + (inner - (z + t))
        planes += [total_here[0], total_here[1], t[0], t[1], z[1]]
    constants[-1].wait()
    planes = right(jnp.concatenate(planes, axis=0), table)
    for f in range(8):
        five = [planes[40 * f + 8 * i : 40 * f + 8 * i + 8] for i in range(5)]
        for z in range(2):
            sum_send[f // 4, f % 4, z] = five[z]
            line_t_send[f // 4, f % 4, z] = five[2 + z]
        line_z_send[f // 4, f % 4] = five[4]
    sums[core] = sum_send[core]

    @pl.when(core == 0)
    def _():
        line_t[1] = line_t_send[0]

    pl.semaphore_wait(barrier, 35)
    sum_out = transfer(sum_send.at[other_core], sums.at[core], first_ss.at[0], first_rs.at[0], sibling)
    sum_in = transfer(sums.at[other_core], sums.at[other_core], first_ss.at[0], first_rs.at[0], sibling)
    t_inner = transfer(line_t_send.at[1], line_t.at[1], first_ss.at[1], first_rs.at[1], sibling)
    t_outer = [
        transfer(line_t_send.at[h], line_t.at[0], first_ss.at[2 + h], first_rs.at[2], device(gz, t_next, h))
        for h in range(2)
    ]
    z_outer = [
        transfer(line_z_send.at[h], line_z.at[core], first_ss.at[4 + h], first_rs.at[3], device(z_next, chip, h))
        for h in range(2)
    ]

    @pl.when(core == 1)
    def _():
        for copy in t_outer:
            copy.start()

    for copy in z_outer:
        copy.start()
    sum_out.start()

    @pl.when(core == 0)
    def _():
        t_inner.start()

    for copy in constants[:-1]:
        copy.wait()
    weights[...] = inverse_momenta(momenta[...], [sines[i] for i in range(4)])
    sum_in.wait_recv()

    @pl.when(core == 1)
    def _():
        t_inner.wait_recv()

    transfer(line_z, line_z, first_ss.at[4], first_rs.at[3], sibling).wait_recv()
    t_outer[0].wait_recv()
    fields = []
    for tl in range(2):
        fields.append([])
        for f in range(4):
            value = sums[tl, f] + line_t[tl, f]
            edge = jnp.stack([line_z[tl, f], jnp.zeros((8, 128), F32)])
            value = value + edge
            factor = 0.5 if f < 2 else jnp.where(jnp.broadcast_to(first_half, value.shape), 0.5, 1.0)
            fields[tl].append(value * factor)
    store_tiles(plane_send.at[0], plane_forward(fields, None))

    to_sibling = [
        transfer(
            links.at[mu, pl.ds(0, 12)], u.at[core, mu, pl.ds(0, 12)], edge_ss.at[5 + mu], edge_rs.at[0], sibling
        )
        for mu in range(4)
    ]
    from_sibling = transfer(
        u.at[other_core, :, pl.ds(0, 12)], u.at[other_core, :, pl.ds(0, 12)], edge_ss.at[0], edge_rs.at[0], sibling
    )
    t_edges = [
        transfer(
            links.at[3, pl.ds(0, 12)], edge_t.at[pl.ds(0, 12)], edge_ss.at[1 + h], edge_rs.at[1], device(gz, t_next, h)
        )
        for h in range(2)
    ]
    z_edges = [
        transfer(
            links.at[2, pl.ds(0, 12), 1], edge_z.at[core, pl.ds(0, 12)], edge_ss.at[3 + h], edge_rs.at[2],
            device(z_next, chip, h),
        )
        for h in range(2)
    ]

    def everything_left():
        sum_out.wait_send()
        for copy in z_outer + z_edges + to_sibling:
            copy.wait_send()

        @pl.when(core == 0)
        def _():
            t_inner.wait_send()

        @pl.when(core == 1)
        def _():
            for copy in t_outer + t_edges:
                copy.wait_send()

        for slot in range(2 * ITERS):
            for send, ss, rs in ((plane_send, plane_ss, plane_rs), (ring_send, ring_ss, ring_rs)):
                part = send.at[slot, pl.ds(0, 120)]
                transfer(part, part, ss.at[slot], rs.at[slot], sibling).wait_send()
        for it in range(ITERS - 1):
            to_other, groups = halo_transfers(it)
            for copy in [to_other] + [copy for group in groups for copy in group]:
                copy.wait_send()

    def beside(it, which):
        if it == 0:
            to_sibling[which].start()
            if which in (1, 2):
                z_edges[which - 1].start()
            else:

                @pl.when(core == 1)
                def _():
                    t_edges[which // 3].start()

    for it in range(ITERS):
        last = it == ITERS - 1
        copy = plane_exchange(2 * it)
        beside(it, 0)
        copy.wait_recv()
        store_tiles(ring_send.at[2 * it], fine_to_coarse(load_tiles(plane_recv.at[2 * it]), 4))
        copy = ring_exchange(2 * it)
        beside(it, 1)
        copy.wait_recv()
        tiles = fine_to_coarse(load_tiles(ring_recv.at[2 * it]), 1)
        tiles = [v * w for v, w in zip(tiles, load_tiles(weights))]
        store_tiles(ring_send.at[2 * it + 1], coarse_to_fine(tiles, 1))
        copy = ring_exchange(2 * it + 1)
        beside(it, 2)
        copy.wait_recv()
        store_tiles(plane_send.at[2 * it + 1], coarse_to_fine(load_tiles(ring_recv.at[2 * it + 1]), 4))
        copy = plane_exchange(2 * it + 1)
        beside(it, 3)
        copy.wait_recv()
        fields = plane_inverse(plane_recv[2 * it + 1], table)
        for tl in range(2):
            for f in range(4):
                smooth[it, core, tl, f] = fields[tl][f]
        to_other, (ahead_t, ahead_z_, after_t, after_z) = halo_transfers(it)
        to_other.start()
        if last:
            ahead_t[1].start()
        else:
            for copy in ahead_t + after_t:
                copy.start()
        for copy in ahead_z_ + ([] if last else after_z):
            copy.start()
        theirs = smooth.at[it, other_core]
        transfer(theirs, theirs, halo_ss.at[it, 0], halo_rs.at[it, 0], sibling).wait_recv()

        def keep(slot, rows):
            for a in range(2):
                for b in range(3):
                    for r in range(2):
                        gauge[slot, 2 * (3 * a + b) + r] = rows[a][b][r]

        for tl in range(2):
            keep(tl, gauge_rows([smooth[it, f // 4, tl, f % 4] for f in range(8)]))

        def turned_inside(where):
            rows = load_rows(gauge.at[where])
            own = completed(rows)
            for mu, shift in ((0, ahead_x), (1, ahead_y)):
                turned = product_dagger(product(rows, load_matrix(u.at[where, mu])), each(shift, own))
                store_matrix(u.at[where, mu], completed(turned))
            for mu in (2, 3):
                store_matrix(u.at[where, mu], product(rows, load_matrix(u.at[where, mu])))

        def turned_z(where, plane, following):
            rows = product_dagger(load_rows(u.at[where, 2, :, plane]), completed(following))
            store_matrix(u.at[where, 2, :, plane], completed(rows))

        def turned_t(where, following):
            rows = product_dagger(load_rows(u.at[where, 3]), completed(load_rows(gauge.at[following])))
            store_matrix(u.at[where, 3], completed(rows))

        def edge_gauges(ref, tl):
            return [[tuple(v[tl] for v in e) for e in row] for row in ref]

        if last:
            outs = [pltpu.make_async_copy(u.at[core, mu], out.at[mu], out_sems.at[mu]) for mu in range(4)]
            turned_inside(core)
            outs[0].start()
            outs[1].start()
            turned_z(core, 0, load_rows(gauge.at[core, :, 1]))
            everything_left()
            arrived(it, 1, smooth_za)
            turned_z(core, 1, gauge_rows([smooth_za[it, f // 4, core, f % 4] for f in range(8)]))
            outs[2].start()

            @pl.when(core == 1)
            def _():
                arrived(it, 0, smooth_ta)
                keep(2, gauge_rows([smooth_ta[it, f // 4, f % 4] for f in range(8)]))

            turned_t(core, core + 1)
            outs[3].start()
        else:
            from_sibling.wait_recv()
            transfer(
                edge_z.at[:, pl.ds(0, 12)], edge_z.at[:, pl.ds(0, 12)], edge_ss.at[0], edge_rs.at[2], sibling
            ).wait_recv()
            t_edges[0].wait_recv()
            missing = [completed(load_rows(u.at[other_core, mu])) for mu in range(4)]
            for mu in range(4):
                store_matrix(u.at[other_core, mu], missing[mu])
            for tl in range(2):
                turned_inside(tl)
            here = [completed(load_rows(gauge.at[tl])) for tl in range(2)]
            store_matrix(edge_t, product_dagger(completed(load_rows(edge_t)), here[0]))
            for tl in range(2):
                edge = product_dagger(completed(load_rows(edge_z.at[tl])), each(lambda v: v[0], here[tl]))
                store_matrix(edge_z.at[tl], edge)
            turned_t(0, 1)
            for tl in range(2):
                turned_z(tl, 0, load_rows(gauge.at[tl, :, 1]))
            even_t = own_half(projected(load_matrix(u.at[0, 3])))
            for tl in range(2):
                x, y = [own_half(projected(load_matrix(u.at[tl, mu]))) for mu in range(2)]
                z = own_half(projected(load_matrix(u.at[tl, 2, :, 0])))
                for f in range(4):
                    value = ((behind_x(x[f]) - x[f]) + (behind_y(y[f]) - y[f])) + jnp.stack([-z[f], z[f]])
                    sums[tl, f] = value + even_t[f] if tl else value - even_t[f]
            arrived(it, 1, smooth_za)
            edges = gauge_rows([smooth_za[it, f // 4, :, f % 4] for f in range(8)])
            for tl in range(2):
                turned_z(tl, 1, edge_gauges(edges, tl))
            arrived(it, 3, smooth_zb)
            edges = gauge_rows([smooth_zb[it, f // 4, :, f % 4] for f in range(8)])
            z_edge = [
                own_half(projected(completed(product(edge_gauges(edges, tl), load_matrix(edge_z.at[tl])))))
                for tl in range(2)
            ]
            z_last_plane = [own_half(projected(load_matrix(u.at[tl, 2, :, 1]))) for tl in range(2)]
            arrived(it, 0, smooth_ta)
            keep(2, gauge_rows([smooth_ta[it, f // 4, f % 4] for f in range(8)]))
            turned_t(1, 2)
            odd_t = own_half(projected(load_matrix(u.at[1, 3])))
            arrived(it, 2, smooth_tb)
            edges = gauge_rows([smooth_tb[it, f // 4, f % 4] for f in range(8)])
            t_edge = own_half(projected(completed(product(edges, load_matrix(edge_t)))))
            fields = []
            for tl in range(2):
                fields.append([])
                for f in range(4):
                    value = sums[tl, f] + jnp.stack([z_edge[tl][f], -z_last_plane[tl][f]])
                    value = value - odd_t[f] if tl else value + t_edge[f]
                    factor = 0.5 if f < 2 else jnp.where(jnp.broadcast_to(first_half, value.shape), 0.5, 1.0)
                    fields[tl].append(value * factor)
            plane_send[2 * it + 2] = plane_forward(fields, table)

    to_other, (ahead_t, ahead_z_, after_t, after_z) = halo_transfers(ITERS - 1)
    for copy in [to_other] + ahead_z_ + ahead_t[1:]:
        copy.wait_send()
    for copy in outs:
        copy.wait()


def shards(links):
    constants = [jnp.asarray(t) for t in tables()]
    anywhere = pl.BlockSpec(memory_space=pl.ANY)
    vmem = pltpu.VMEM
    dma = pltpu.SemaphoreType.DMA
    slots = 2 * ITERS
    result = pl.pallas_call(
        kernel,
        out_shape=pltpu.VMEM((4, 18, 2, 8, 128), F32),
        in_specs=[anywhere] * 4,
        out_specs=anywhere,
        scratch_shapes=[
            vmem((2, 4, 18, 2, 8, 128), F32),
            vmem((2, 18, 8, 128), F32),
            vmem((18, 2, 8, 128), F32),
            vmem((2, 4, 2, 8, 128), F32),
            vmem((2, 4, 2, 8, 128), F32),
            vmem((2, 4, 2, 8, 128), F32),
            vmem((2, 4, 2, 8, 128), F32),
            vmem((2, 4, 8, 128), F32),
            vmem((2, 4, 8, 128), F32),
            vmem((256, 128), BF16),
            vmem((16, 8, 128), F32),
            vmem((4, 8, 128), F32),
            vmem((128, 128), F32),
            vmem((slots, 128, 128), F32),
            vmem((slots, 128, 128), F32),
            vmem((slots, 128, 128), F32),
            vmem((slots, 128, 128), F32),
            vmem((ITERS, 2, 2, 4, 2, 8, 128), F32),
            vmem((ITERS, 2, 2, 4, 8, 128), F32),
            vmem((ITERS, 2, 2, 4, 8, 128), F32),
            vmem((ITERS, 2, 4, 2, 8, 128), F32),
            vmem((ITERS, 2, 4, 2, 8, 128), F32),
            vmem((3, 12, 2, 8, 128), F32),
            dma((10,)),
            dma((9,)),
            dma((3,)),
            dma((6,)),
            dma((4,)),
            dma((slots,)),
            dma((slots,)),
            dma((slots,)),
            dma((slots,)),
            dma((ITERS, 9)),
            dma((ITERS, 5)),
            dma((4,)),
        ],
        compiler_params=pltpu.CompilerParams(
            collective_id=0, has_side_effects=True, vmem_limit_bytes=40 * 1024 * 1024
        ),
    )(*[pltpu.with_memory_space_constraint(a, pltpu.HBM) for a in [links.reshape(4, 18, 2, 8, 128)] + constants])
    return result.reshape(links.shape)


def solution(mesh):
    return jax.shard_map(
        shards,
        mesh=mesh,
        in_specs=(P(None, None, "gz", "ta", None),),
        out_specs=P(None, None, "gz", "ta", None),
        check_vma=False,
    )
```

```python
import functools
import math

import jax
import jax.numpy as jnp
import numpy as np
from jax import lax
from jax.experimental import pallas as pl
from jax.experimental.pallas import tpu as pltpu
from jax.sharding import PartitionSpec as P

ITERS = 2
STEP_SIZE = 0.08
LINE = 32
GZ = 16
TA = 32
PAIRS = ((0, 1), (0, 2), (1, 2))
LOGICAL = pl.DeviceIdType.LOGICAL
F32 = jnp.float32
BF16 = jnp.bfloat16


def halves(table):
    high = table.astype(jnp.bfloat16)
    return high, (table - high.astype(np.float64)).astype(jnp.bfloat16)


def tables():
    phase = 2.0 * np.pi * (np.outer(np.arange(LINE), np.arange(LINE)) % LINE) / LINE
    plane = np.kron(np.eye(4), (np.cos(phase) + np.sin(phase)) / np.sqrt(LINE))
    sines = 4.0 * np.sin(np.pi * np.arange(LINE) / LINE) ** 2
    row = np.arange(128)
    momenta = sines[row // 8 + 16 * (row % 2)][:, None] + np.tile(sines, 4)[None, :]
    tiles = np.broadcast_to(sines[:, None, None], (LINE, 8, 128))
    return (
        np.concatenate(halves(plane), axis=0),
        momenta.reshape(16, 8, 128).astype(np.float32),
        np.ascontiguousarray(tiles).astype(np.float32),
    )


def times(u, v):
    return (u[0] * v[0] - u[1] * v[1], u[0] * v[1] + u[1] * v[0])


def times_conj(u, v):
    return (u[0] * v[0] + u[1] * v[1], u[1] * v[0] - u[0] * v[1])


def plus(u, v):
    return (u[0] + v[0], u[1] + v[1])


def minus(u, v):
    return (u[0] - v[0], u[1] - v[1])


def conj(u):
    return (u[0], -u[1])


def scaled(u, factor):
    return (u[0] * factor, u[1] * factor)


def total(terms):
    return functools.reduce(plus, terms)


def product(left, right):
    return [[total([times(left[a][j], right[j][b]) for j in range(3)]) for b in range(3)] for a in range(len(left))]


def product_dagger(left, right):
    return [[total([times_conj(left[a][j], right[b][j]) for j in range(3)]) for b in range(3)] for a in range(len(left))]


def cross_conj(u, v):
    row = []
    for c in range(3):
        n, m = (c + 1) % 3, (c + 2) % 3
        row.append(conj(minus(times(u[n], v[m]), times(u[m], v[n]))))
    return row


def each(function, matrix):
    return [[(function(e[0]), function(e[1])) for e in row] for row in matrix]


def lanes(v):
    return lax.broadcasted_iota(jnp.int32, v.shape, v.ndim - 1)


def roll(v, shift, axis):
    return pltpu.roll(v, shift, axis)


def behind_x(v):
    moved = roll(v, 32, v.ndim - 1)
    return jnp.where(lanes(v) < 32, roll(moved, 1, v.ndim - 2), moved)


def ahead_x(v):
    moved = roll(v, 96, v.ndim - 1)
    return jnp.where(lanes(v) >= 96, roll(moved, 7, v.ndim - 2), moved)


def behind_y(v):
    return jnp.where(lanes(v) % 32 == 0, roll(v, 97, v.ndim - 1), roll(v, 1, v.ndim - 1))


def ahead_y(v):
    return jnp.where(lanes(v) % 32 == 31, roll(v, 31, v.ndim - 1), roll(v, 127, v.ndim - 1))


def behind_z(v, edge):
    return jnp.concatenate([edge[None], v[:1]], axis=0)


def ahead_z(v, edge):
    return jnp.concatenate([v[1:], edge[None]], axis=0)


def projected(u):
    third = (u[0][0][1] + u[1][1][1] + u[2][2][1]) * (1.0 / 3.0)
    return (
        [u[a][b][0] - u[b][a][0] for a, b in PAIRS]
        + [u[a][b][1] + u[b][a][1] for a, b in PAIRS]
        + [u[0][0][1] - third, u[1][1][1] - third]
    )


def block_transpose(planes):
    lane = lanes(planes[0])
    axis = planes[0].ndim - 1
    low = lane < 64
    even = (lane // 32) % 2 == 0
    first = [jnp.where(low, planes[p], roll(planes[p + 2], 64, axis)) for p in range(2)]
    second = [jnp.where(low, roll(planes[p], 64, axis), planes[p + 2]) for p in range(2)]
    out = []
    for one, two in (first, second):
        out.append(jnp.where(even, one, roll(two, 32, axis)))
        out.append(jnp.where(even, roll(one, 96, axis), two))
    return out


def rows_of(v):
    return lax.broadcasted_iota(jnp.int32, v.shape, v.ndim - 2)


def bit_exchange(one, two, stride):
    clear = lax.rem(lax.div(rows_of(one), stride), 2) == 0
    return (
        jnp.where(clear, one, roll(two, stride, one.ndim - 2)),
        jnp.where(clear, roll(one, 8 - stride, one.ndim - 2), two),
    )


def middle_exchange(v):
    pair = lax.div(rows_of(v), 2)
    return jnp.where(pair == 1, roll(v, 6, 0), jnp.where(pair == 2, roll(v, 2, 0), v))


def hartley(v):
    size = len(v)
    if size == 1:
        return v
    even, odd = hartley(v[0::2]), hartley(v[1::2])
    half = size // 2
    out = [None] * size
    for k in range(half):
        turned = odd[k]
        if k and 4 * k != size:
            angle = 2.0 * math.pi * k / size
            turned = odd[k] * math.cos(angle) + odd[half - k] * math.sin(angle)
        out[k], out[k + half] = even[k] + turned, even[k] - turned
    return out


def bit_clear(v, stride):
    return lax.rem(lax.div(rows_of(v), stride), 2) == 0


def rotated(v, stride):
    low = bit_clear(v[0], stride)
    out = list(v)
    for k in range(1, 16):
        if k != 8:
            angle = math.pi * k / 16
            out[k] = v[k] * jnp.where(low, 1.0, math.cos(angle)) + v[16 - k] * jnp.where(low, 0.0, math.sin(angle))
    return out


def butterflies(v, stride):
    low = bit_clear(v[0], stride)
    out = []
    for e in v:
        other = roll(e, stride, 0)
        if stride != 4:
            other = jnp.where(low, roll(e, 8 - stride, 0), other)
        out.append(other + jnp.where(low, e, -e))
    return out


def fine_to_coarse(v, stride):
    return butterflies(rotated(hartley(v), stride), stride)


def coarse_to_fine(v, stride):
    return hartley(rotated(butterflies(v, stride), stride))


def tiles_of(matrix):
    return [matrix[8 * i : 8 * i + 8] for i in range(16)]


def plane_forward(fields, table):
    parts = [block_transpose(fields[tl]) for tl in range(2)]
    tiles = [None] * 16
    for b in range(4):
        traded = [bit_exchange(parts[tl][b][0], parts[tl][b][1], 2) for tl in range(2)]
        for bit in range(2):
            tiles[8 * bit + b], tiles[8 * bit + 4 + b] = bit_exchange(traded[0][bit], traded[1][bit], 1)
    tiles = [middle_exchange(v) for v in coarse_to_fine(tiles, 4)]
    return tiles if table is None else right(jnp.concatenate(tiles, axis=0), table)


def plane_inverse(matrix, table):
    tiles = fine_to_coarse([middle_exchange(v) for v in tiles_of(right(matrix, table))], 4)
    blocks = [[None] * 4 for _ in range(2)]
    for b in range(4):
        pairs = [bit_exchange(tiles[8 * bit + b], tiles[8 * bit + 4 + b], 1) for bit in range(2)]
        for tl in range(2):
            blocks[tl][b] = jnp.stack(bit_exchange(pairs[0][tl], pairs[1][tl], 2))
    return [block_transpose(blocks[tl]) for tl in range(2)]


def split(v):
    high = v.astype(BF16)
    return high, (v - high.astype(F32)).astype(BF16)


def right(v, table):
    table_high, table_low = table[pl.ds(0, 128)], table[pl.ds(128, 128)]
    high, low = split(v)
    return jnp.dot(
        jnp.concatenate([high, low, high], axis=1),
        jnp.concatenate([table_high, table_high, table_low], axis=0),
        preferred_element_type=F32,
    )


def store_tiles(ref, tiles):
    for i, tile in enumerate(tiles):
        ref[pl.ds(8 * i, 8)] = tile


def load_tiles(ref):
    return [ref[pl.ds(8 * i, 8)] for i in range(16)]


def inverse_momenta(momenta, tiles):
    row = lax.broadcasted_iota(jnp.int32, (8, 128), 0)
    own = jnp.where(row < 4, tiles[0], tiles[1]) + jnp.where(lax.rem(lax.div(row, 2), 2) == 0, tiles[2], tiles[3])
    squares = momenta + own[None]
    positive = squares > 0.001
    return jnp.where(positive, (16.0 * STEP_SIZE / LINE**3) / jnp.where(positive, squares, 1.0), 0.0).reshape(128, 128)


def normalized(row):
    norm = functools.reduce(jnp.add, [e[0] * e[0] + e[1] * e[1] for e in row])
    scale = lax.rsqrt(norm)
    return [scaled(e, scale) for e in row]


def gauge_rows(fields):
    a, b, c = [(fields[i], fields[3 + i]) for i in range(3)]
    h0, h1 = fields[6], fields[7]
    h2 = -(h0 + h1)
    aa, bb, cc = [e[0] * e[0] + e[1] * e[1] for e in (a, b, c)]
    sixth = 1.0 / 6.0

    def turned(u, h):
        return (-(u[1] * h), u[0] * h)

    s01 = minus(turned(a, -h2), times_conj(b, c))
    s02 = plus(turned(b, -h1), times(a, c))
    s12 = minus(turned(c, -h0), times_conj(b, a))
    d0 = 1.0 - (h0 * h0 + aa + bb) * sixth
    d1 = 1.0 - (h1 * h1 + aa + cc) * sixth
    d2 = 1.0 - (h2 * h2 + bb + cc) * sixth

    def upper(u, s):
        return (0.5 * u[0] + s[0] * sixth, 0.5 * u[1] + s[1] * sixth)

    def lower(u, s):
        return (s[0] * sixth - 0.5 * u[0], 0.5 * u[1] - s[1] * sixth)

    inner = [
        [(d0, 0.5 * h0), upper(a, s01), upper(b, s02)],
        [lower(a, s01), (d1, 0.5 * h1), upper(c, s12)],
        [lower(b, s02), lower(c, s12), (d2, 0.5 * h2)],
    ]
    minus_a = (-a[0], a[1])
    p0 = [total([turned(inner[0][j], h0), times(a, inner[1][j]), times(b, inner[2][j])]) for j in range(3)]
    p1 = [total([times(minus_a, inner[0][j]), turned(inner[1][j], h1), times(c, inner[2][j])]) for j in range(3)]
    p0[0] = (p0[0][0] + 1.0, p0[0][1])
    p1[1] = (p1[1][0] + 1.0, p1[1][1])
    row0 = normalized(p0)
    overlap = total([times_conj(p1[j], row0[j]) for j in range(3)])
    row1 = normalized([minus(p1[j], times(overlap, row0[j])) for j in range(3)])
    return [row0, row1]


def completed(rows):
    return rows + [cross_conj(rows[0], rows[1])]


def load_matrix(ref):
    return [[(ref[2 * (3 * a + b)], ref[2 * (3 * a + b) + 1]) for b in range(3)] for a in range(3)]


def store_matrix(ref, matrix):
    for a, row in enumerate(matrix):
        for b, entry in enumerate(row):
            ref[2 * (3 * a + b)] = entry[0]
            ref[2 * (3 * a + b) + 1] = entry[1]


def load_rows(ref):
    return [[(ref[2 * (3 * a + b)], ref[2 * (3 * a + b) + 1]) for b in range(3)] for a in range(2)]


def kernel(
    links, table_hbm, momenta_hbm, sines_hbm, out,
    u, edge_z, edge_t, sum_send, sums, line_t_send, line_t, line_z_send, line_z, table, momenta, sines, weights,
    plane_send, plane_recv, ring_send, ring_recv, smooth, smooth_za, smooth_zb, smooth_ta, smooth_tb, gauge,
    load_sems, edge_ss, edge_rs, first_ss, first_rs, plane_ss, plane_rs, ring_ss, ring_rs, halo_ss, halo_rs, out_sems,
):
    gz = lax.axis_index("gz")
    ta = lax.axis_index("ta")
    gz_x, gz_y = lax.div(gz, 4), lax.rem(gz, 4)
    chip, core = lax.div(ta, 2), lax.rem(ta, 2)
    other_core = 1 - core

    def device(z, t_chip, which):
        return z * TA + 2 * t_chip + which

    sibling = device(gz, chip, other_core)
    z_next, z_last = lax.rem(gz + 1, GZ), lax.rem(gz + GZ - 1, GZ)
    t_next, t_last = lax.rem(chip + 1, GZ), lax.rem(chip + GZ - 1, GZ)

    def around(place, step, size):
        return lax.rem(place + step, size)

    offsets = [(dx, dy) for dx in range(4) for dy in range(4) if dx or dy]
    offsets.sort(key=lambda o: -(min(o[0], 4 - o[0]) + min(o[1], 4 - o[1])))
    columns = [around(gz_x, dx, 4) for dx in range(4)]
    lines_y = [around(gz_y, dy, 4) for dy in range(4)]
    plane_partners = [(i, device(i, chip, core)) for i in [columns[dx] * 4 + lines_y[dy] for dx, dy in offsets]]
    steps = sorted(range(1, 16), key=lambda d: -min(d, 16 - d))
    ring_partners = [(i, device(gz, i, core)) for i in [around(chip, d, 16) for d in steps]]
    crossed = [
        device(gz, t_last, other_core),
        device(gz, t_next, other_core),
        device(z_last, chip, other_core),
        device(z_next, chip, other_core),
    ]

    barrier = pltpu.get_barrier_semaphore()

    def greet(target):
        pl.semaphore_signal(barrier, inc=1, device_id=target, device_id_type=LOGICAL)

    loads = [pltpu.make_async_copy(links.at[mu], u.at[core, mu], load_sems.at[mu]) for mu in range(4)]
    constants = [
        pltpu.make_async_copy(momenta_hbm, momenta, load_sems.at[4]),
        pltpu.make_async_copy(sines_hbm.at[chip], sines.at[0], load_sems.at[5]),
        pltpu.make_async_copy(sines_hbm.at[chip + 16], sines.at[1], load_sems.at[6]),
        pltpu.make_async_copy(sines_hbm.at[2 * gz], sines.at[2], load_sems.at[7]),
        pltpu.make_async_copy(sines_hbm.at[2 * gz + 1], sines.at[3], load_sems.at[8]),
        pltpu.make_async_copy(table_hbm, table, load_sems.at[9]),
    ]
    for copy in loads[::-1] + constants[-1:]:
        copy.start()
    for _, target in ring_partners + plane_partners:
        greet(target)
    for target in crossed + [sibling]:
        greet(target)
    for copy in constants[:-1]:
        copy.start()

    def transfer(src, dst, send_sem, recv_sem, target):
        return pltpu.make_async_remote_copy(
            src_ref=src, dst_ref=dst, send_sem=send_sem, recv_sem=recv_sem, device_id=target, device_id_type=LOGICAL
        )

    def exchange(sends, recvs, ss, rs, slot, partners, me, neighbour):
        send, recv = sends.at[slot], recvs.at[slot]
        own = pl.ds(pl.multiple_of(me * 8, 8), 8)

        for index, target in partners:
            theirs = pl.ds(pl.multiple_of(index * 8, 8), 8)
            transfer(send.at[theirs], recv.at[own], ss.at[slot], rs.at[slot], target).start()
        recv[own] = send[own]
        part = pl.ds(0, 120)
        return transfer(send.at[part], recv.at[part], ss.at[slot], rs.at[slot], neighbour)

    def plane_exchange(slot):
        neighbour = device(z_next, chip, core)
        return exchange(plane_send, plane_recv, plane_ss, plane_rs, slot, plane_partners, gz, neighbour)

    def ring_exchange(slot):
        neighbour = device(gz, t_next, core)
        return exchange(ring_send, ring_recv, ring_ss, ring_rs, slot, ring_partners, chip, neighbour)

    def halo_transfers(it):
        mine = smooth.at[it, core]
        ss, rs = halo_ss, halo_rs
        to_sibling = transfer(mine, mine, ss.at[it, 0], rs.at[it, 0], sibling)
        groups = []
        for which, (src, dst, z, t_chip) in enumerate(
            (
                (mine.at[0], smooth_ta.at[it, core], gz, t_last),
                (mine.at[:, :, 0], smooth_za.at[it, core], z_last, chip),
                (mine.at[1], smooth_tb.at[it, core], gz, t_next),
                (mine.at[:, :, 1], smooth_zb.at[it, core], z_next, chip),
            )
        ):
            groups.append(
                [
                    transfer(src, dst, ss.at[it, 1 + 2 * which + h], rs.at[it, 1 + which], device(z, t_chip, h))
                    for h in range(2)
                ]
            )
        if it == ITERS - 1:
            groups[1] = [
                transfer(
                    mine.at[h, :, 0], smooth_za.at[it, core, h], ss.at[it, 3 + h], rs.at[it, 2],
                    device(z_last, chip, h),
                )
                for h in range(2)
            ]
        return to_sibling, groups

    def arrived(it, which, ref):
        transfer(ref.at[it], ref.at[it], halo_ss.at[it, 0], halo_rs.at[it, 1 + which], sibling).wait_recv()

    lane_core = lax.broadcasted_iota(jnp.int32, (8, 128), 0) * 0 + core
    first_half = lane_core == 0

    def own_half(fields):
        return [jnp.where(jnp.broadcast_to(first_half, one.shape), one, two) for one, two in zip(fields[:4], fields[4:])]

    for copy in loads:
        copy.wait()
    lines = [projected(load_matrix(u.at[core, mu])) for mu in range(4)]
    planes = []
    for f in range(8):
        x, y, z, t = [lines[mu][f] for mu in range(4)]
        inner = jnp.concatenate([jnp.zeros((1, 8, 128), F32), z[:1]], axis=0)
        total_here = ((behind_x(x) - x) + (behind_y(y) - y)) + (inner - (z + t))
        planes += [total_here[0], total_here[1], t[0], t[1], z[1]]
    constants[-1].wait()
    planes = right(jnp.concatenate(planes, axis=0), table)
    for f in range(8):
        five = [planes[40 * f + 8 * i : 40 * f + 8 * i + 8] for i in range(5)]
        for z in range(2):
            sum_send[f // 4, f % 4, z] = five[z]
            line_t_send[f // 4, f % 4, z] = five[2 + z]
        line_z_send[f // 4, f % 4] = five[4]
    sums[core] = sum_send[core]

    @pl.when(core == 0)
    def _():
        line_t[1] = line_t_send[0]

    pl.semaphore_wait(barrier, 35)
    sum_out = transfer(sum_send.at[other_core], sums.at[core], first_ss.at[0], first_rs.at[0], sibling)
    sum_in = transfer(sums.at[other_core], sums.at[other_core], first_ss.at[0], first_rs.at[0], sibling)
    t_inner = transfer(line_t_send.at[1], line_t.at[1], first_ss.at[1], first_rs.at[1], sibling)
    t_outer = [
        transfer(line_t_send.at[h], line_t.at[0], first_ss.at[2 + h], first_rs.at[2], device(gz, t_next, h))
        for h in range(2)
    ]
    z_outer = [
        transfer(line_z_send.at[h], line_z.at[core], first_ss.at[4 + h], first_rs.at[3], device(z_next, chip, h))
        for h in range(2)
    ]

    @pl.when(core == 1)
    def _():
        for copy in t_outer:
            copy.start()

    for copy in z_outer:
        copy.start()
    sum_out.start()

    @pl.when(core == 0)
    def _():
        t_inner.start()

    for copy in constants[:-1]:
        copy.wait()
    weights[...] = inverse_momenta(momenta[...], [sines[i] for i in range(4)])
    sum_in.wait_recv()

    @pl.when(core == 1)
    def _():
        t_inner.wait_recv()

    transfer(line_z, line_z, first_ss.at[4], first_rs.at[3], sibling).wait_recv()
    t_outer[0].wait_recv()
    fields = []
    for tl in range(2):
        fields.append([])
        for f in range(4):
            value = sums[tl, f] + line_t[tl, f]
            edge = jnp.stack([line_z[tl, f], jnp.zeros((8, 128), F32)])
            value = value + edge
            factor = 0.5 if f < 2 else jnp.where(jnp.broadcast_to(first_half, value.shape), 0.5, 1.0)
            fields[tl].append(value * factor)
    store_tiles(plane_send.at[0], plane_forward(fields, None))

    to_sibling = [
        transfer(
            links.at[mu, pl.ds(0, 12)], u.at[core, mu, pl.ds(0, 12)], edge_ss.at[5 + mu], edge_rs.at[0], sibling
        )
        for mu in range(4)
    ]
    from_sibling = transfer(
        u.at[other_core, :, pl.ds(0, 12)], u.at[other_core, :, pl.ds(0, 12)], edge_ss.at[0], edge_rs.at[0], sibling
    )
    t_edges = [
        transfer(
            links.at[3, pl.ds(0, 12)], edge_t.at[pl.ds(0, 12)], edge_ss.at[1 + h], edge_rs.at[1], device(gz, t_next, h)
        )
        for h in range(2)
    ]
    z_edges = [
        transfer(
            links.at[2, pl.ds(0, 12), 1], edge_z.at[core, pl.ds(0, 12)], edge_ss.at[3 + h], edge_rs.at[2],
            device(z_next, chip, h),
        )
        for h in range(2)
    ]

    def everything_left():
        sum_out.wait_send()
        for copy in z_outer + z_edges + to_sibling:
            copy.wait_send()

        @pl.when(core == 0)
        def _():
            t_inner.wait_send()

        @pl.when(core == 1)
        def _():
            for copy in t_outer + t_edges:
                copy.wait_send()

        for slot in range(2 * ITERS):
            for send, ss, rs in ((plane_send, plane_ss, plane_rs), (ring_send, ring_ss, ring_rs)):
                part = send.at[slot, pl.ds(0, 120)]
                transfer(part, part, ss.at[slot], rs.at[slot], sibling).wait_send()
        for it in range(ITERS - 1):
            to_other, groups = halo_transfers(it)
            for copy in [to_other] + [copy for group in groups for copy in group]:
                copy.wait_send()

    def beside(it, which):
        if it == 0:
            to_sibling[which].start()
            if which in (1, 2):
                z_edges[which - 1].start()
            else:

                @pl.when(core == 1)
                def _():
                    t_edges[which // 3].start()

    for it in range(ITERS):
        last = it == ITERS - 1
        copy = plane_exchange(2 * it)
        beside(it, 0)
        copy.wait_recv()
        store_tiles(ring_send.at[2 * it], fine_to_coarse(load_tiles(plane_recv.at[2 * it]), 4))
        copy = ring_exchange(2 * it)
        beside(it, 1)
        copy.wait_recv()
        tiles = fine_to_coarse(load_tiles(ring_recv.at[2 * it]), 1)
        tiles = [v * w for v, w in zip(tiles, load_tiles(weights))]
        store_tiles(ring_send.at[2 * it + 1], coarse_to_fine(tiles, 1))
        copy = ring_exchange(2 * it + 1)
        beside(it, 2)
        copy.wait_recv()
        store_tiles(plane_send.at[2 * it + 1], coarse_to_fine(load_tiles(ring_recv.at[2 * it + 1]), 4))
        copy = plane_exchange(2 * it + 1)
        beside(it, 3)
        copy.wait_recv()
        fields = plane_inverse(plane_recv[2 * it + 1], table)
        for tl in range(2):
            for f in range(4):
                smooth[it, core, tl, f] = fields[tl][f]
        to_other, (ahead_t, ahead_z_, after_t, after_z) = halo_transfers(it)
        if last:
            ahead_t[1].start()
        else:
            for copy in ahead_t + after_t:
                copy.start()
        for copy in ahead_z_ + ([] if last else after_z):
            copy.start()
        to_other.start()
        theirs = smooth.at[it, other_core]
        transfer(theirs, theirs, halo_ss.at[it, 0], halo_rs.at[it, 0], sibling).wait_recv()

        def keep(slot, rows):
            for a in range(2):
                for b in range(3):
                    for r in range(2):
                        gauge[slot, 2 * (3 * a + b) + r] = rows[a][b][r]

        for tl in range(2):
            keep(tl, gauge_rows([smooth[it, f // 4, tl, f % 4] for f in range(8)]))

        def turned_inside(where):
            rows = load_rows(gauge.at[where])
            own = completed(rows)
            for mu, shift in ((0, ahead_x), (1, ahead_y)):
                turned = product_dagger(product(rows, load_matrix(u.at[where, mu])), each(shift, own))
                store_matrix(u.at[where, mu], completed(turned))
            for mu in (2, 3):
                store_matrix(u.at[where, mu], product(rows, load_matrix(u.at[where, mu])))

        def turned_z(where, plane, following):
            rows = product_dagger(load_rows(u.at[where, 2, :, plane]), completed(following))
            store_matrix(u.at[where, 2, :, plane], completed(rows))

        def turned_t(where, following):
            rows = product_dagger(load_rows(u.at[where, 3]), completed(load_rows(gauge.at[following])))
            store_matrix(u.at[where, 3], completed(rows))

        def edge_gauges(ref, tl):
            return [[tuple(v[tl] for v in e) for e in row] for row in ref]

        if last:
            outs = [pltpu.make_async_copy(u.at[core, mu], out.at[mu], out_sems.at[mu]) for mu in range(4)]
            turned_inside(core)
            outs[0].start()
            outs[1].start()
            turned_z(core, 0, load_rows(gauge.at[core, :, 1]))
            everything_left()
            part = smooth_za.at[it, :, core]
            transfer(part, part, halo_ss.at[it, 0], halo_rs.at[it, 2], sibling).wait_recv()
            turned_z(core, 1, gauge_rows([smooth_za[it, f // 4, core, f % 4] for f in range(8)]))
            outs[2].start()

            @pl.when(core == 1)
            def _():
                arrived(it, 0, smooth_ta)
                keep(2, gauge_rows([smooth_ta[it, f // 4, f % 4] for f in range(8)]))

            turned_t(core, core + 1)
            outs[3].start()
        else:
            from_sibling.wait_recv()
            transfer(
                edge_z.at[:, pl.ds(0, 12)], edge_z.at[:, pl.ds(0, 12)], edge_ss.at[0], edge_rs.at[2], sibling
            ).wait_recv()
            t_edges[0].wait_recv()
            missing = [completed(load_rows(u.at[other_core, mu])) for mu in range(4)]
            for mu in range(4):
                store_matrix(u.at[other_core, mu], missing[mu])
            for tl in range(2):
                turned_inside(tl)
            here = [completed(load_rows(gauge.at[tl])) for tl in range(2)]
            store_matrix(edge_t, product_dagger(completed(load_rows(edge_t)), here[0]))
            for tl in range(2):
                edge = product_dagger(completed(load_rows(edge_z.at[tl])), each(lambda v: v[0], here[tl]))
                store_matrix(edge_z.at[tl], edge)
            turned_t(0, 1)
            for tl in range(2):
                turned_z(tl, 0, load_rows(gauge.at[tl, :, 1]))
            even_t = own_half(projected(load_matrix(u.at[0, 3])))
            for tl in range(2):
                x, y = [own_half(projected(load_matrix(u.at[tl, mu]))) for mu in range(2)]
                z = own_half(projected(load_matrix(u.at[tl, 2, :, 0])))
                for f in range(4):
                    value = ((behind_x(x[f]) - x[f]) + (behind_y(y[f]) - y[f])) + jnp.stack([-z[f], z[f]])
                    sums[tl, f] = value + even_t[f] if tl else value - even_t[f]
            arrived(it, 1, smooth_za)
            edges = gauge_rows([smooth_za[it, f // 4, :, f % 4] for f in range(8)])
            for tl in range(2):
                turned_z(tl, 1, edge_gauges(edges, tl))
            arrived(it, 3, smooth_zb)
            edges = gauge_rows([smooth_zb[it, f // 4, :, f % 4] for f in range(8)])
            z_edge = [
                own_half(projected(completed(product(edge_gauges(edges, tl), load_matrix(edge_z.at[tl])))))
                for tl in range(2)
            ]
            z_last_plane = [own_half(projected(load_matrix(u.at[tl, 2, :, 1]))) for tl in range(2)]
            arrived(it, 0, smooth_ta)
            keep(2, gauge_rows([smooth_ta[it, f // 4, f % 4] for f in range(8)]))
            turned_t(1, 2)
            odd_t = own_half(projected(load_matrix(u.at[1, 3])))
            arrived(it, 2, smooth_tb)
            edges = gauge_rows([smooth_tb[it, f // 4, f % 4] for f in range(8)])
            t_edge = own_half(projected(completed(product(edges, load_matrix(edge_t)))))
            fields = []
            for tl in range(2):
                fields.append([])
                for f in range(4):
                    value = sums[tl, f] + jnp.stack([z_edge[tl][f], -z_last_plane[tl][f]])
                    value = value - odd_t[f] if tl else value + t_edge[f]
                    factor = 0.5 if f < 2 else jnp.where(jnp.broadcast_to(first_half, value.shape), 0.5, 1.0)
                    fields[tl].append(value * factor)
            plane_send[2 * it + 2] = plane_forward(fields, table)

    to_other, (ahead_t, ahead_z_, after_t, after_z) = halo_transfers(ITERS - 1)
    for copy in [to_other] + ahead_z_ + ahead_t[1:]:
        copy.wait_send()
    for copy in outs:
        copy.wait()


def shards(links):
    constants = [jnp.asarray(t) for t in tables()]
    anywhere = pl.BlockSpec(memory_space=pl.ANY)
    vmem = pltpu.VMEM
    dma = pltpu.SemaphoreType.DMA
    slots = 2 * ITERS
    result = pl.pallas_call(
        kernel,
        out_shape=pltpu.VMEM((4, 18, 2, 8, 128), F32),
        in_specs=[anywhere] * 4,
        out_specs=anywhere,
        scratch_shapes=[
            vmem((2, 4, 18, 2, 8, 128), F32),
            vmem((2, 18, 8, 128), F32),
            vmem((18, 2, 8, 128), F32),
            vmem((2, 4, 2, 8, 128), F32),
            vmem((2, 4, 2, 8, 128), F32),
            vmem((2, 4, 2, 8, 128), F32),
            vmem((2, 4, 2, 8, 128), F32),
            vmem((2, 4, 8, 128), F32),
            vmem((2, 4, 8, 128), F32),
            vmem((256, 128), BF16),
            vmem((16, 8, 128), F32),
            vmem((4, 8, 128), F32),
            vmem((128, 128), F32),
            vmem((slots, 128, 128), F32),
            vmem((slots, 128, 128), F32),
            vmem((slots, 128, 128), F32),
            vmem((slots, 128, 128), F32),
            vmem((ITERS, 2, 2, 4, 2, 8, 128), F32),
            vmem((ITERS, 2, 2, 4, 8, 128), F32),
            vmem((ITERS, 2, 2, 4, 8, 128), F32),
            vmem((ITERS, 2, 4, 2, 8, 128), F32),
            vmem((ITERS, 2, 4, 2, 8, 128), F32),
            vmem((3, 12, 2, 8, 128), F32),
            dma((10,)),
            dma((9,)),
            dma((3,)),
            dma((6,)),
            dma((4,)),
            dma((slots,)),
            dma((slots,)),
            dma((slots,)),
            dma((slots,)),
            dma((ITERS, 9)),
            dma((ITERS, 5)),
            dma((4,)),
        ],
        compiler_params=pltpu.CompilerParams(
            collective_id=0, has_side_effects=True, vmem_limit_bytes=40 * 1024 * 1024
        ),
    )(*[pltpu.with_memory_space_constraint(a, pltpu.HBM) for a in [links.reshape(4, 18, 2, 8, 128)] + constants])
    return result.reshape(links.shape)


def solution(mesh):
    return jax.shard_map(
        shards,
        mesh=mesh,
        in_specs=(P(None, None, "gz", "ta", None),),
        out_specs=P(None, None, "gz", "ta", None),
        check_vma=False,
    )
```

```python
import functools
import math

import jax
import jax.numpy as jnp
import numpy as np
from jax import lax
from jax.experimental import pallas as pl
from jax.experimental.pallas import tpu as pltpu
from jax.sharding import PartitionSpec as P

ITERS = 2
STEP_SIZE = 0.08
LINE = 32
GZ = 16
TA = 32
PAIRS = ((0, 1), (0, 2), (1, 2))
LOGICAL = pl.DeviceIdType.LOGICAL
F32 = jnp.float32
BF16 = jnp.bfloat16


def halves(table):
    high = table.astype(jnp.bfloat16)
    return high, (table - high.astype(np.float64)).astype(jnp.bfloat16)


def tables():
    phase = 2.0 * np.pi * (np.outer(np.arange(LINE), np.arange(LINE)) % LINE) / LINE
    plane = np.kron(np.eye(4), (np.cos(phase) + np.sin(phase)) / np.sqrt(LINE))
    sines = 4.0 * np.sin(np.pi * np.arange(LINE) / LINE) ** 2
    row = np.arange(128)
    momenta = sines[row // 8 + 16 * (row % 2)][:, None] + np.tile(sines, 4)[None, :]
    tiles = np.broadcast_to(sines[:, None, None], (LINE, 8, 128))
    return (
        np.concatenate(halves(plane), axis=0),
        momenta.reshape(16, 8, 128).astype(np.float32),
        np.ascontiguousarray(tiles).astype(np.float32),
    )


def times(u, v):
    return (u[0] * v[0] - u[1] * v[1], u[0] * v[1] + u[1] * v[0])


def times_conj(u, v):
    return (u[0] * v[0] + u[1] * v[1], u[1] * v[0] - u[0] * v[1])


def plus(u, v):
    return (u[0] + v[0], u[1] + v[1])


def minus(u, v):
    return (u[0] - v[0], u[1] - v[1])


def conj(u):
    return (u[0], -u[1])


def scaled(u, factor):
    return (u[0] * factor, u[1] * factor)


def total(terms):
    return functools.reduce(plus, terms)


def product(left, right):
    return [[total([times(left[a][j], right[j][b]) for j in range(3)]) for b in range(3)] for a in range(len(left))]


def product_dagger(left, right):
    return [[total([times_conj(left[a][j], right[b][j]) for j in range(3)]) for b in range(3)] for a in range(len(left))]


def cross_conj(u, v):
    row = []
    for c in range(3):
        n, m = (c + 1) % 3, (c + 2) % 3
        row.append(conj(minus(times(u[n], v[m]), times(u[m], v[n]))))
    return row


def each(function, matrix):
    return [[(function(e[0]), function(e[1])) for e in row] for row in matrix]


def lanes(v):
    return lax.broadcasted_iota(jnp.int32, v.shape, v.ndim - 1)


def roll(v, shift, axis):
    return pltpu.roll(v, shift, axis)


def behind_x(v):
    moved = roll(v, 32, v.ndim - 1)
    return jnp.where(lanes(v) < 32, roll(moved, 1, v.ndim - 2), moved)


def ahead_x(v):
    moved = roll(v, 96, v.ndim - 1)
    return jnp.where(lanes(v) >= 96, roll(moved, 7, v.ndim - 2), moved)


def behind_y(v):
    return jnp.where(lanes(v) % 32 == 0, roll(v, 97, v.ndim - 1), roll(v, 1, v.ndim - 1))


def ahead_y(v):
    return jnp.where(lanes(v) % 32 == 31, roll(v, 31, v.ndim - 1), roll(v, 127, v.ndim - 1))


def behind_z(v, edge):
    return jnp.concatenate([edge[None], v[:1]], axis=0)


def ahead_z(v, edge):
    return jnp.concatenate([v[1:], edge[None]], axis=0)


def projected(u):
    third = (u[0][0][1] + u[1][1][1] + u[2][2][1]) * (1.0 / 3.0)
    return (
        [u[a][b][0] - u[b][a][0] for a, b in PAIRS]
        + [u[a][b][1] + u[b][a][1] for a, b in PAIRS]
        + [u[0][0][1] - third, u[1][1][1] - third]
    )


def block_transpose(planes):
    lane = lanes(planes[0])
    axis = planes[0].ndim - 1
    low = lane < 64
    even = (lane // 32) % 2 == 0
    first = [jnp.where(low, planes[p], roll(planes[p + 2], 64, axis)) for p in range(2)]
    second = [jnp.where(low, roll(planes[p], 64, axis), planes[p + 2]) for p in range(2)]
    out = []
    for one, two in (first, second):
        out.append(jnp.where(even, one, roll(two, 32, axis)))
        out.append(jnp.where(even, roll(one, 96, axis), two))
    return out


def rows_of(v):
    return lax.broadcasted_iota(jnp.int32, v.shape, v.ndim - 2)


def bit_exchange(one, two, stride):
    clear = lax.rem(lax.div(rows_of(one), stride), 2) == 0
    return (
        jnp.where(clear, one, roll(two, stride, one.ndim - 2)),
        jnp.where(clear, roll(one, 8 - stride, one.ndim - 2), two),
    )


def middle_exchange(v):
    pair = lax.div(rows_of(v), 2)
    return jnp.where(pair == 1, roll(v, 6, 0), jnp.where(pair == 2, roll(v, 2, 0), v))


def hartley(v):
    size = len(v)
    if size == 1:
        return v
    even, odd = hartley(v[0::2]), hartley(v[1::2])
    half = size // 2
    out = [None] * size
    for k in range(half):
        turned = odd[k]
        if k and 4 * k != size:
            angle = 2.0 * math.pi * k / size
            turned = odd[k] * math.cos(angle) + odd[half - k] * math.sin(angle)
        out[k], out[k + half] = even[k] + turned, even[k] - turned
    return out


def bit_clear(v, stride):
    return lax.rem(lax.div(rows_of(v), stride), 2) == 0


def rotated(v, stride):
    low = bit_clear(v[0], stride)
    out = list(v)
    for k in range(1, 16):
        if k != 8:
            angle = math.pi * k / 16
            out[k] = v[k] * jnp.where(low, 1.0, math.cos(angle)) + v[16 - k] * jnp.where(low, 0.0, math.sin(angle))
    return out


def butterflies(v, stride):
    low = bit_clear(v[0], stride)
    out = []
    for e in v:
        other = roll(e, stride, 0)
        if stride != 4:
            other = jnp.where(low, roll(e, 8 - stride, 0), other)
        out.append(other + jnp.where(low, e, -e))
    return out


def fine_to_coarse(v, stride):
    return butterflies(rotated(hartley(v), stride), stride)


def coarse_to_fine(v, stride):
    return hartley(rotated(butterflies(v, stride), stride))


def tiles_of(matrix):
    return [matrix[8 * i : 8 * i + 8] for i in range(16)]


def plane_forward(fields, table):
    parts = [block_transpose(fields[tl]) for tl in range(2)]
    tiles = [None] * 16
    for b in range(4):
        traded = [bit_exchange(parts[tl][b][0], parts[tl][b][1], 2) for tl in range(2)]
        for bit in range(2):
            tiles[8 * bit + b], tiles[8 * bit + 4 + b] = bit_exchange(traded[0][bit], traded[1][bit], 1)
    tiles = [middle_exchange(v) for v in coarse_to_fine(tiles, 4)]
    return tiles if table is None else right(jnp.concatenate(tiles, axis=0), table)


def plane_inverse(matrix, table):
    tiles = fine_to_coarse([middle_exchange(v) for v in tiles_of(right(matrix, table))], 4)
    blocks = [[None] * 4 for _ in range(2)]
    for b in range(4):
        pairs = [bit_exchange(tiles[8 * bit + b], tiles[8 * bit + 4 + b], 1) for bit in range(2)]
        for tl in range(2):
            blocks[tl][b] = jnp.stack(bit_exchange(pairs[0][tl], pairs[1][tl], 2))
    return [block_transpose(blocks[tl]) for tl in range(2)]


def split(v):
    high = v.astype(BF16)
    return high, (v - high.astype(F32)).astype(BF16)


def right(v, table):
    table_high, table_low = table[pl.ds(0, 128)], table[pl.ds(128, 128)]
    high, low = split(v)
    return jnp.dot(
        jnp.concatenate([high, low, high], axis=1),
        jnp.concatenate([table_high, table_high, table_low], axis=0),
        preferred_element_type=F32,
    )


def store_tiles(ref, tiles):
    for i, tile in enumerate(tiles):
        ref[pl.ds(8 * i, 8)] = tile


def load_tiles(ref):
    return [ref[pl.ds(8 * i, 8)] for i in range(16)]


def inverse_momenta(momenta, tiles):
    row = lax.broadcasted_iota(jnp.int32, (8, 128), 0)
    own = jnp.where(row < 4, tiles[0], tiles[1]) + jnp.where(lax.rem(lax.div(row, 2), 2) == 0, tiles[2], tiles[3])
    squares = momenta + own[None]
    positive = squares > 0.001
    return jnp.where(positive, (16.0 * STEP_SIZE / LINE**3) / jnp.where(positive, squares, 1.0), 0.0).reshape(128, 128)


def normalized(row):
    norm = functools.reduce(jnp.add, [e[0] * e[0] + e[1] * e[1] for e in row])
    scale = lax.rsqrt(norm)
    return [scaled(e, scale) for e in row]


def gauge_rows(fields):
    a, b, c = [(fields[i], fields[3 + i]) for i in range(3)]
    h0, h1 = fields[6], fields[7]
    h2 = -(h0 + h1)
    aa, bb, cc = [e[0] * e[0] + e[1] * e[1] for e in (a, b, c)]
    sixth = 1.0 / 6.0

    def turned(u, h):
        return (-(u[1] * h), u[0] * h)

    s01 = minus(turned(a, -h2), times_conj(b, c))
    s02 = plus(turned(b, -h1), times(a, c))
    s12 = minus(turned(c, -h0), times_conj(b, a))
    d0 = 1.0 - (h0 * h0 + aa + bb) * sixth
    d1 = 1.0 - (h1 * h1 + aa + cc) * sixth
    d2 = 1.0 - (h2 * h2 + bb + cc) * sixth

    def upper(u, s):
        return (0.5 * u[0] + s[0] * sixth, 0.5 * u[1] + s[1] * sixth)

    def lower(u, s):
        return (s[0] * sixth - 0.5 * u[0], 0.5 * u[1] - s[1] * sixth)

    inner = [
        [(d0, 0.5 * h0), upper(a, s01), upper(b, s02)],
        [lower(a, s01), (d1, 0.5 * h1), upper(c, s12)],
        [lower(b, s02), lower(c, s12), (d2, 0.5 * h2)],
    ]
    minus_a = (-a[0], a[1])
    p0 = [total([turned(inner[0][j], h0), times(a, inner[1][j]), times(b, inner[2][j])]) for j in range(3)]
    p1 = [total([times(minus_a, inner[0][j]), turned(inner[1][j], h1), times(c, inner[2][j])]) for j in range(3)]
    p0[0] = (p0[0][0] + 1.0, p0[0][1])
    p1[1] = (p1[1][0] + 1.0, p1[1][1])
    row0 = normalized(p0)
    overlap = total([times_conj(p1[j], row0[j]) for j in range(3)])
    row1 = normalized([minus(p1[j], times(overlap, row0[j])) for j in range(3)])
    return [row0, row1]


def completed(rows):
    return rows + [cross_conj(rows[0], rows[1])]


def load_matrix(ref):
    return [[(ref[2 * (3 * a + b)], ref[2 * (3 * a + b) + 1]) for b in range(3)] for a in range(3)]


def store_matrix(ref, matrix):
    for a, row in enumerate(matrix):
        for b, entry in enumerate(row):
            ref[2 * (3 * a + b)] = entry[0]
            ref[2 * (3 * a + b) + 1] = entry[1]


def load_rows(ref):
    return [[(ref[2 * (3 * a + b)], ref[2 * (3 * a + b) + 1]) for b in range(3)] for a in range(2)]


def kernel(
    links, table_hbm, momenta_hbm, sines_hbm, out,
    u, edge_z, edge_t, sum_send, sums, line_t_send, line_t, line_z_send, line_z, table, momenta, sines, weights,
    plane_send, plane_recv, ring_send, ring_recv, smooth, smooth_za, smooth_zb, smooth_ta, smooth_tb, gauge,
    load_sems, edge_ss, edge_rs, first_ss, first_rs, plane_ss, plane_rs, ring_ss, ring_rs, halo_ss, halo_rs,
):
    gz = lax.axis_index("gz")
    ta = lax.axis_index("ta")
    gz_x, gz_y = lax.div(gz, 4), lax.rem(gz, 4)
    chip, core = lax.div(ta, 2), lax.rem(ta, 2)
    other_core = 1 - core

    def device(z, t_chip, which):
        return z * TA + 2 * t_chip + which

    sibling = device(gz, chip, other_core)
    z_next, z_last = lax.rem(gz + 1, GZ), lax.rem(gz + GZ - 1, GZ)
    t_next, t_last = lax.rem(chip + 1, GZ), lax.rem(chip + GZ - 1, GZ)

    def around(place, step, size):
        return lax.rem(place + step, size)

    offsets = [(dx, dy) for dx in range(4) for dy in range(4) if dx or dy]
    offsets.sort(key=lambda o: -(min(o[0], 4 - o[0]) + min(o[1], 4 - o[1])))
    columns = [around(gz_x, dx, 4) for dx in range(4)]
    lines_y = [around(gz_y, dy, 4) for dy in range(4)]
    plane_partners = [(i, device(i, chip, core)) for i in [columns[dx] * 4 + lines_y[dy] for dx, dy in offsets]]
    steps = sorted(range(1, 16), key=lambda d: -min(d, 16 - d))
    ring_partners = [(i, device(gz, i, core)) for i in [around(chip, d, 16) for d in steps]]
    crossed = [
        device(gz, t_last, other_core),
        device(gz, t_next, other_core),
        device(z_last, chip, other_core),
        device(z_next, chip, other_core),
    ]

    barrier = pltpu.get_barrier_semaphore()

    def greet(target):
        pl.semaphore_signal(barrier, inc=1, device_id=target, device_id_type=LOGICAL)

    loads = [pltpu.make_async_copy(links.at[mu], u.at[core, mu], load_sems.at[mu]) for mu in range(4)]
    constants = [
        pltpu.make_async_copy(momenta_hbm, momenta, load_sems.at[4]),
        pltpu.make_async_copy(sines_hbm.at[chip], sines.at[0], load_sems.at[5]),
        pltpu.make_async_copy(sines_hbm.at[chip + 16], sines.at[1], load_sems.at[6]),
        pltpu.make_async_copy(sines_hbm.at[2 * gz], sines.at[2], load_sems.at[7]),
        pltpu.make_async_copy(sines_hbm.at[2 * gz + 1], sines.at[3], load_sems.at[8]),
        pltpu.make_async_copy(table_hbm, table, load_sems.at[9]),
    ]
    for copy in loads[::-1] + constants[-1:]:
        copy.start()
    for _, target in ring_partners + plane_partners:
        greet(target)
    for target in crossed + [sibling]:
        greet(target)
    for copy in constants[:-1]:
        copy.start()

    def transfer(src, dst, send_sem, recv_sem, target):
        return pltpu.make_async_remote_copy(
            src_ref=src, dst_ref=dst, send_sem=send_sem, recv_sem=recv_sem, device_id=target, device_id_type=LOGICAL
        )

    def exchange(sends, recvs, ss, rs, slot, partners, me, neighbour):
        send, recv = sends.at[slot], recvs.at[slot]
        own = pl.ds(pl.multiple_of(me * 8, 8), 8)

        for index, target in partners:
            theirs = pl.ds(pl.multiple_of(index * 8, 8), 8)
            transfer(send.at[theirs], recv.at[own], ss.at[slot], rs.at[slot], target).start()
        recv[own] = send[own]
        part = pl.ds(0, 120)
        return transfer(send.at[part], recv.at[part], ss.at[slot], rs.at[slot], neighbour)

    def plane_exchange(slot):
        neighbour = device(z_next, chip, core)
        return exchange(plane_send, plane_recv, plane_ss, plane_rs, slot, plane_partners, gz, neighbour)

    def ring_exchange(slot):
        neighbour = device(gz, t_next, core)
        return exchange(ring_send, ring_recv, ring_ss, ring_rs, slot, ring_partners, chip, neighbour)

    def halo_transfers(it):
        mine = smooth.at[it, core]
        ss, rs = halo_ss, halo_rs
        to_sibling = transfer(mine, mine, ss.at[it, 0], rs.at[it, 0], sibling)
        groups = []
        for which, (src, dst, z, t_chip) in enumerate(
            (
                (mine.at[0], smooth_ta.at[it, core], gz, t_last),
                (mine.at[:, :, 0], smooth_za.at[it, core], z_last, chip),
                (mine.at[1], smooth_tb.at[it, core], gz, t_next),
                (mine.at[:, :, 1], smooth_zb.at[it, core], z_next, chip),
            )
        ):
            groups.append(
                [
                    transfer(src, dst, ss.at[it, 1 + 2 * which + h], rs.at[it, 1 + which], device(z, t_chip, h))
                    for h in range(2)
                ]
            )
        if it == ITERS - 1:
            groups[1] = [
                transfer(
                    mine.at[h, :, 0], smooth_za.at[it, core, h], ss.at[it, 3 + h], rs.at[it, 2],
                    device(z_last, chip, h),
                )
                for h in range(2)
            ]
        return to_sibling, groups

    def arrived(it, which, ref):
        transfer(ref.at[it], ref.at[it], halo_ss.at[it, 0], halo_rs.at[it, 1 + which], sibling).wait_recv()

    lane_core = lax.broadcasted_iota(jnp.int32, (8, 128), 0) * 0 + core
    first_half = lane_core == 0

    def own_half(fields):
        return [jnp.where(jnp.broadcast_to(first_half, one.shape), one, two) for one, two in zip(fields[:4], fields[4:])]

    for copy in loads:
        copy.wait()
    lines = [projected(load_matrix(u.at[core, mu])) for mu in range(4)]
    planes = []
    for f in range(8):
        x, y, z, t = [lines[mu][f] for mu in range(4)]
        inner = jnp.concatenate([jnp.zeros((1, 8, 128), F32), z[:1]], axis=0)
        total_here = ((behind_x(x) - x) + (behind_y(y) - y)) + (inner - (z + t))
        planes += [total_here[0], total_here[1], t[0], t[1], z[1]]
    constants[-1].wait()
    planes = right(jnp.concatenate(planes, axis=0), table)
    for f in range(8):
        five = [planes[40 * f + 8 * i : 40 * f + 8 * i + 8] for i in range(5)]
        for z in range(2):
            sum_send[f // 4, f % 4, z] = five[z]
            line_t_send[f // 4, f % 4, z] = five[2 + z]
        line_z_send[f // 4, f % 4] = five[4]
    sums[core] = sum_send[core]

    @pl.when(core == 0)
    def _():
        line_t[1] = line_t_send[0]

    pl.semaphore_wait(barrier, 35)
    sum_out = transfer(sum_send.at[other_core], sums.at[core], first_ss.at[0], first_rs.at[0], sibling)
    sum_in = transfer(sums.at[other_core], sums.at[other_core], first_ss.at[0], first_rs.at[0], sibling)
    t_inner = transfer(line_t_send.at[1], line_t.at[1], first_ss.at[1], first_rs.at[1], sibling)
    t_outer = [
        transfer(line_t_send.at[h], line_t.at[0], first_ss.at[2 + h], first_rs.at[2], device(gz, t_next, h))
        for h in range(2)
    ]
    z_outer = [
        transfer(line_z_send.at[h], line_z.at[core], first_ss.at[4 + h], first_rs.at[3], device(z_next, chip, h))
        for h in range(2)
    ]

    @pl.when(core == 1)
    def _():
        for copy in t_outer:
            copy.start()

    for copy in z_outer:
        copy.start()
    sum_out.start()

    @pl.when(core == 0)
    def _():
        t_inner.start()

    for copy in constants[:-1]:
        copy.wait()
    weights[...] = inverse_momenta(momenta[...], [sines[i] for i in range(4)])
    sum_in.wait_recv()

    @pl.when(core == 1)
    def _():
        t_inner.wait_recv()

    transfer(line_z, line_z, first_ss.at[4], first_rs.at[3], sibling).wait_recv()
    t_outer[0].wait_recv()
    fields = []
    for tl in range(2):
        fields.append([])
        for f in range(4):
            value = sums[tl, f] + line_t[tl, f]
            edge = jnp.stack([line_z[tl, f], jnp.zeros((8, 128), F32)])
            value = value + edge
            factor = 0.5 if f < 2 else jnp.where(jnp.broadcast_to(first_half, value.shape), 0.5, 1.0)
            fields[tl].append(value * factor)
    store_tiles(plane_send.at[0], plane_forward(fields, None))

    to_sibling = [
        transfer(
            links.at[mu, pl.ds(0, 12)], u.at[core, mu, pl.ds(0, 12)], edge_ss.at[5 + mu], edge_rs.at[0], sibling
        )
        for mu in range(4)
    ]
    from_sibling = transfer(
        u.at[other_core, :, pl.ds(0, 12)], u.at[other_core, :, pl.ds(0, 12)], edge_ss.at[0], edge_rs.at[0], sibling
    )
    t_edges = [
        transfer(
            links.at[3, pl.ds(0, 12)], edge_t.at[pl.ds(0, 12)], edge_ss.at[1 + h], edge_rs.at[1], device(gz, t_next, h)
        )
        for h in range(2)
    ]
    z_edges = [
        transfer(
            links.at[2, pl.ds(0, 12), 1], edge_z.at[core, pl.ds(0, 12)], edge_ss.at[3 + h], edge_rs.at[2],
            device(z_next, chip, h),
        )
        for h in range(2)
    ]

    def everything_left():
        sum_out.wait_send()
        for copy in z_outer + z_edges + to_sibling:
            copy.wait_send()

        @pl.when(core == 0)
        def _():
            t_inner.wait_send()

        @pl.when(core == 1)
        def _():
            for copy in t_outer + t_edges:
                copy.wait_send()

        for slot in range(2 * ITERS):
            for send, ss, rs in ((plane_send, plane_ss, plane_rs), (ring_send, ring_ss, ring_rs)):
                part = send.at[slot, pl.ds(0, 120)]
                transfer(part, part, ss.at[slot], rs.at[slot], sibling).wait_send()
        for it in range(ITERS - 1):
            to_other, groups = halo_transfers(it)
            for copy in [to_other] + [copy for group in groups for copy in group]:
                copy.wait_send()

    def beside(it, which):
        if it == 0:
            to_sibling[which].start()
            if which in (1, 2):
                z_edges[which - 1].start()
            else:

                @pl.when(core == 1)
                def _():
                    t_edges[which // 3].start()

    for it in range(ITERS):
        last = it == ITERS - 1
        copy = plane_exchange(2 * it)
        beside(it, 0)
        copy.wait_recv()
        store_tiles(ring_send.at[2 * it], fine_to_coarse(load_tiles(plane_recv.at[2 * it]), 4))
        copy = ring_exchange(2 * it)
        beside(it, 1)
        copy.wait_recv()
        tiles = fine_to_coarse(load_tiles(ring_recv.at[2 * it]), 1)
        tiles = [v * w for v, w in zip(tiles, load_tiles(weights))]
        store_tiles(ring_send.at[2 * it + 1], coarse_to_fine(tiles, 1))
        copy = ring_exchange(2 * it + 1)
        beside(it, 2)
        copy.wait_recv()
        store_tiles(plane_send.at[2 * it + 1], coarse_to_fine(load_tiles(ring_recv.at[2 * it + 1]), 4))
        copy = plane_exchange(2 * it + 1)
        beside(it, 3)
        copy.wait_recv()
        fields = plane_inverse(plane_recv[2 * it + 1], table)
        for tl in range(2):
            for f in range(4):
                smooth[it, core, tl, f] = fields[tl][f]
        to_other, (ahead_t, ahead_z_, after_t, after_z) = halo_transfers(it)
        if last:
            ahead_t[1].start()
        else:
            for copy in ahead_t + after_t:
                copy.start()
        for copy in ahead_z_ + ([] if last else after_z):
            copy.start()
        to_other.start()
        theirs = smooth.at[it, other_core]
        transfer(theirs, theirs, halo_ss.at[it, 0], halo_rs.at[it, 0], sibling).wait_recv()

        def keep(slot, rows):
            for a in range(2):
                for b in range(3):
                    for r in range(2):
                        gauge[slot, 2 * (3 * a + b) + r] = rows[a][b][r]

        for tl in range(2):
            keep(tl, gauge_rows([smooth[it, f // 4, tl, f % 4] for f in range(8)]))

        def turned_inside(where, target):
            rows = load_rows(gauge.at[where])
            own = completed(rows)
            for mu, shift in ((0, ahead_x), (1, ahead_y)):
                turned = product_dagger(product(rows, load_matrix(u.at[where, mu])), each(shift, own))
                store_matrix(target.at[mu], completed(turned))
            for mu in (2, 3):
                store_matrix(u.at[where, mu], product(rows, load_matrix(u.at[where, mu])))

        def turned_z(where, target, plane, following):
            rows = product_dagger(load_rows(u.at[where, 2, :, plane]), completed(following))
            store_matrix(target.at[2, :, plane], completed(rows))

        def turned_t(where, target, following):
            rows = product_dagger(load_rows(u.at[where, 3]), completed(load_rows(gauge.at[following])))
            store_matrix(target.at[3], completed(rows))

        def edge_gauges(ref, tl):
            return [[tuple(v[tl] for v in e) for e in row] for row in ref]

        if last:
            turned_inside(core, out)
            turned_z(core, out, 0, load_rows(gauge.at[core, :, 1]))
            everything_left()
            part = smooth_za.at[it, :, core]
            transfer(part, part, halo_ss.at[it, 0], halo_rs.at[it, 2], sibling).wait_recv()
            turned_z(core, out, 1, gauge_rows([smooth_za[it, f // 4, core, f % 4] for f in range(8)]))

            @pl.when(core == 1)
            def _():
                arrived(it, 0, smooth_ta)
                keep(2, gauge_rows([smooth_ta[it, f // 4, f % 4] for f in range(8)]))

            turned_t(core, out, core + 1)
        else:
            from_sibling.wait_recv()
            transfer(
                edge_z.at[:, pl.ds(0, 12)], edge_z.at[:, pl.ds(0, 12)], edge_ss.at[0], edge_rs.at[2], sibling
            ).wait_recv()
            t_edges[0].wait_recv()
            missing = [completed(load_rows(u.at[other_core, mu])) for mu in range(4)]
            for mu in range(4):
                store_matrix(u.at[other_core, mu], missing[mu])
            for tl in range(2):
                turned_inside(tl, u.at[tl])
            here = [completed(load_rows(gauge.at[tl])) for tl in range(2)]
            store_matrix(edge_t, product_dagger(completed(load_rows(edge_t)), here[0]))
            for tl in range(2):
                edge = product_dagger(completed(load_rows(edge_z.at[tl])), each(lambda v: v[0], here[tl]))
                store_matrix(edge_z.at[tl], edge)
            turned_t(0, u.at[0], 1)
            for tl in range(2):
                turned_z(tl, u.at[tl], 0, load_rows(gauge.at[tl, :, 1]))
            even_t = own_half(projected(load_matrix(u.at[0, 3])))
            for tl in range(2):
                x, y = [own_half(projected(load_matrix(u.at[tl, mu]))) for mu in range(2)]
                z = own_half(projected(load_matrix(u.at[tl, 2, :, 0])))
                for f in range(4):
                    value = ((behind_x(x[f]) - x[f]) + (behind_y(y[f]) - y[f])) + jnp.stack([-z[f], z[f]])
                    sums[tl, f] = value + even_t[f] if tl else value - even_t[f]
            arrived(it, 1, smooth_za)
            edges = gauge_rows([smooth_za[it, f // 4, :, f % 4] for f in range(8)])
            for tl in range(2):
                turned_z(tl, u.at[tl], 1, edge_gauges(edges, tl))
            arrived(it, 3, smooth_zb)
            edges = gauge_rows([smooth_zb[it, f // 4, :, f % 4] for f in range(8)])
            z_edge = [
                own_half(projected(completed(product(edge_gauges(edges, tl), load_matrix(edge_z.at[tl])))))
                for tl in range(2)
            ]
            z_last_plane = [own_half(projected(load_matrix(u.at[tl, 2, :, 1]))) for tl in range(2)]
            arrived(it, 0, smooth_ta)
            keep(2, gauge_rows([smooth_ta[it, f // 4, f % 4] for f in range(8)]))
            turned_t(1, u.at[1], 2)
            odd_t = own_half(projected(load_matrix(u.at[1, 3])))
            arrived(it, 2, smooth_tb)
            edges = gauge_rows([smooth_tb[it, f // 4, f % 4] for f in range(8)])
            t_edge = own_half(projected(completed(product(edges, load_matrix(edge_t)))))
            fields = []
            for tl in range(2):
                fields.append([])
                for f in range(4):
                    value = sums[tl, f] + jnp.stack([z_edge[tl][f], -z_last_plane[tl][f]])
                    value = value - odd_t[f] if tl else value + t_edge[f]
                    factor = 0.5 if f < 2 else jnp.where(jnp.broadcast_to(first_half, value.shape), 0.5, 1.0)
                    fields[tl].append(value * factor)
            plane_send[2 * it + 2] = plane_forward(fields, table)

    to_other, (ahead_t, ahead_z_, after_t, after_z) = halo_transfers(ITERS - 1)
    for copy in [to_other] + ahead_z_ + ahead_t[1:]:
        copy.wait_send()


def shards(links):
    constants = [jnp.asarray(t) for t in tables()]
    anywhere = pl.BlockSpec(memory_space=pl.ANY)
    vmem = pltpu.VMEM
    dma = pltpu.SemaphoreType.DMA
    slots = 2 * ITERS
    result = pl.pallas_call(
        kernel,
        out_shape=pltpu.VMEM((4, 18, 2, 8, 128), F32),
        in_specs=[anywhere] * 4,
        out_specs=pl.BlockSpec(memory_space=vmem),
        scratch_shapes=[
            vmem((2, 4, 18, 2, 8, 128), F32),
            vmem((2, 18, 8, 128), F32),
            vmem((18, 2, 8, 128), F32),
            vmem((2, 4, 2, 8, 128), F32),
            vmem((2, 4, 2, 8, 128), F32),
            vmem((2, 4, 2, 8, 128), F32),
            vmem((2, 4, 2, 8, 128), F32),
            vmem((2, 4, 8, 128), F32),
            vmem((2, 4, 8, 128), F32),
            vmem((256, 128), BF16),
            vmem((16, 8, 128), F32),
            vmem((4, 8, 128), F32),
            vmem((128, 128), F32),
            vmem((slots, 128, 128), F32),
            vmem((slots, 128, 128), F32),
            vmem((slots, 128, 128), F32),
            vmem((slots, 128, 128), F32),
            vmem((ITERS, 2, 2, 4, 2, 8, 128), F32),
            vmem((ITERS, 2, 2, 4, 8, 128), F32),
            vmem((ITERS, 2, 2, 4, 8, 128), F32),
            vmem((ITERS, 2, 4, 2, 8, 128), F32),
            vmem((ITERS, 2, 4, 2, 8, 128), F32),
            vmem((3, 12, 2, 8, 128), F32),
            dma((10,)),
            dma((9,)),
            dma((3,)),
            dma((6,)),
            dma((4,)),
            dma((slots,)),
            dma((slots,)),
            dma((slots,)),
            dma((slots,)),
            dma((ITERS, 9)),
            dma((ITERS, 5)),
        ],
        compiler_params=pltpu.CompilerParams(
            collective_id=0, has_side_effects=True, vmem_limit_bytes=40 * 1024 * 1024
        ),
    )(*[pltpu.with_memory_space_constraint(a, pltpu.HBM) for a in [links.reshape(4, 18, 2, 8, 128)] + constants])
    return result.reshape(links.shape)


def solution(mesh):
    return jax.shard_map(
        shards,
        mesh=mesh,
        in_specs=(P(None, None, "gz", "ta", None),),
        out_specs=P(None, None, "gz", "ta", None),
        check_vma=False,
    )
```

```python
import functools
import math

import jax
import jax.numpy as jnp
import numpy as np
from jax import lax
from jax.experimental import pallas as pl
from jax.experimental.pallas import tpu as pltpu
from jax.sharding import PartitionSpec as P

ITERS = 2
STEP_SIZE = 0.08
LINE = 32
GZ = 16
TA = 32
PAIRS = ((0, 1), (0, 2), (1, 2))
LOGICAL = pl.DeviceIdType.LOGICAL
F32 = jnp.float32
BF16 = jnp.bfloat16


def halves(table):
    high = table.astype(jnp.bfloat16)
    return high, (table - high.astype(np.float64)).astype(jnp.bfloat16)


def tables():
    phase = 2.0 * np.pi * (np.outer(np.arange(LINE), np.arange(LINE)) % LINE) / LINE
    plane = np.kron(np.eye(4), (np.cos(phase) + np.sin(phase)) / np.sqrt(LINE))
    sines = 4.0 * np.sin(np.pi * np.arange(LINE) / LINE) ** 2
    row = np.arange(128)
    momenta = sines[row // 8 + 16 * (row % 2)][:, None] + np.tile(sines, 4)[None, :]
    tiles = np.broadcast_to(sines[:, None, None], (LINE, 8, 128))
    return (
        np.concatenate(halves(plane), axis=0),
        momenta.reshape(16, 8, 128).astype(np.float32),
        np.ascontiguousarray(tiles).astype(np.float32),
    )


def times(u, v):
    return (u[0] * v[0] - u[1] * v[1], u[0] * v[1] + u[1] * v[0])


def times_conj(u, v):
    return (u[0] * v[0] + u[1] * v[1], u[1] * v[0] - u[0] * v[1])


def plus(u, v):
    return (u[0] + v[0], u[1] + v[1])


def minus(u, v):
    return (u[0] - v[0], u[1] - v[1])


def conj(u):
    return (u[0], -u[1])


def scaled(u, factor):
    return (u[0] * factor, u[1] * factor)


def total(terms):
    return functools.reduce(plus, terms)


def product(left, right):
    return [[total([times(left[a][j], right[j][b]) for j in range(3)]) for b in range(3)] for a in range(len(left))]


def product_dagger(left, right):
    return [[total([times_conj(left[a][j], right[b][j]) for j in range(3)]) for b in range(3)] for a in range(len(left))]


def cross_conj(u, v):
    row = []
    for c in range(3):
        n, m = (c + 1) % 3, (c + 2) % 3
        row.append(conj(minus(times(u[n], v[m]), times(u[m], v[n]))))
    return row


def each(function, matrix):
    return [[(function(e[0]), function(e[1])) for e in row] for row in matrix]


def lanes(v):
    return lax.broadcasted_iota(jnp.int32, v.shape, v.ndim - 1)


def roll(v, shift, axis):
    return pltpu.roll(v, shift, axis)


def behind_x(v):
    moved = roll(v, 32, v.ndim - 1)
    return jnp.where(lanes(v) < 32, roll(moved, 1, v.ndim - 2), moved)


def ahead_x(v):
    moved = roll(v, 96, v.ndim - 1)
    return jnp.where(lanes(v) >= 96, roll(moved, 7, v.ndim - 2), moved)


def behind_y(v):
    return jnp.where(lanes(v) % 32 == 0, roll(v, 97, v.ndim - 1), roll(v, 1, v.ndim - 1))


def ahead_y(v):
    return jnp.where(lanes(v) % 32 == 31, roll(v, 31, v.ndim - 1), roll(v, 127, v.ndim - 1))


def behind_z(v, edge):
    return jnp.concatenate([edge[None], v[:1]], axis=0)


def ahead_z(v, edge):
    return jnp.concatenate([v[1:], edge[None]], axis=0)


def projected(u):
    third = (u[0][0][1] + u[1][1][1] + u[2][2][1]) * (1.0 / 3.0)
    return (
        [u[a][b][0] - u[b][a][0] for a, b in PAIRS]
        + [u[a][b][1] + u[b][a][1] for a, b in PAIRS]
        + [u[0][0][1] - third, u[1][1][1] - third]
    )


def block_transpose(planes):
    lane = lanes(planes[0])
    axis = planes[0].ndim - 1
    low = lane < 64
    even = (lane // 32) % 2 == 0
    first = [jnp.where(low, planes[p], roll(planes[p + 2], 64, axis)) for p in range(2)]
    second = [jnp.where(low, roll(planes[p], 64, axis), planes[p + 2]) for p in range(2)]
    out = []
    for one, two in (first, second):
        out.append(jnp.where(even, one, roll(two, 32, axis)))
        out.append(jnp.where(even, roll(one, 96, axis), two))
    return out


def rows_of(v):
    return lax.broadcasted_iota(jnp.int32, v.shape, v.ndim - 2)


def bit_exchange(one, two, stride):
    clear = lax.rem(lax.div(rows_of(one), stride), 2) == 0
    return (
        jnp.where(clear, one, roll(two, stride, one.ndim - 2)),
        jnp.where(clear, roll(one, 8 - stride, one.ndim - 2), two),
    )


def middle_exchange(v):
    pair = lax.div(rows_of(v), 2)
    return jnp.where(pair == 1, roll(v, 6, 0), jnp.where(pair == 2, roll(v, 2, 0), v))


def hartley(v):
    size = len(v)
    if size == 1:
        return v
    even, odd = hartley(v[0::2]), hartley(v[1::2])
    half = size // 2
    out = [None] * size
    for k in range(half):
        turned = odd[k]
        if k and 4 * k != size:
            angle = 2.0 * math.pi * k / size
            turned = odd[k] * math.cos(angle) + odd[half - k] * math.sin(angle)
        out[k], out[k + half] = even[k] + turned, even[k] - turned
    return out


def bit_clear(v, stride):
    return lax.rem(lax.div(rows_of(v), stride), 2) == 0


def rotated(v, stride):
    low = bit_clear(v[0], stride)
    out = list(v)
    for k in range(1, 16):
        if k != 8:
            angle = math.pi * k / 16
            out[k] = v[k] * jnp.where(low, 1.0, math.cos(angle)) + v[16 - k] * jnp.where(low, 0.0, math.sin(angle))
    return out


def butterflies(v, stride):
    low = bit_clear(v[0], stride)
    out = []
    for e in v:
        other = roll(e, stride, 0)
        if stride != 4:
            other = jnp.where(low, roll(e, 8 - stride, 0), other)
        out.append(other + jnp.where(low, e, -e))
    return out


def fine_to_coarse(v, stride):
    return butterflies(rotated(hartley(v), stride), stride)


def coarse_to_fine(v, stride):
    return hartley(rotated(butterflies(v, stride), stride))


def tiles_of(matrix):
    return [matrix[8 * i : 8 * i + 8] for i in range(16)]


def plane_forward(fields, table):
    parts = [block_transpose(fields[tl]) for tl in range(2)]
    tiles = [None] * 16
    for b in range(4):
        traded = [bit_exchange(parts[tl][b][0], parts[tl][b][1], 2) for tl in range(2)]
        for bit in range(2):
            tiles[8 * bit + b], tiles[8 * bit + 4 + b] = bit_exchange(traded[0][bit], traded[1][bit], 1)
    tiles = [middle_exchange(v) for v in coarse_to_fine(tiles, 4)]
    return tiles if table is None else right(jnp.concatenate(tiles, axis=0), table)


def plane_inverse(matrix, table):
    tiles = fine_to_coarse([middle_exchange(v) for v in tiles_of(right(matrix, table))], 4)
    blocks = [[None] * 4 for _ in range(2)]
    for b in range(4):
        pairs = [bit_exchange(tiles[8 * bit + b], tiles[8 * bit + 4 + b], 1) for bit in range(2)]
        for tl in range(2):
            blocks[tl][b] = jnp.stack(bit_exchange(pairs[0][tl], pairs[1][tl], 2))
    return [block_transpose(blocks[tl]) for tl in range(2)]


def split(v):
    high = v.astype(BF16)
    return high, (v - high.astype(F32)).astype(BF16)


def right(v, table):
    table_high, table_low = table[pl.ds(0, 128)], table[pl.ds(128, 128)]
    high, low = split(v)
    return jnp.dot(
        jnp.concatenate([high, low, high], axis=1),
        jnp.concatenate([table_high, table_high, table_low], axis=0),
        preferred_element_type=F32,
    )


def store_tiles(ref, tiles):
    for i, tile in enumerate(tiles):
        ref[pl.ds(8 * i, 8)] = tile


def load_tiles(ref):
    return [ref[pl.ds(8 * i, 8)] for i in range(16)]


def inverse_momenta(momenta, tiles):
    row = lax.broadcasted_iota(jnp.int32, (8, 128), 0)
    own = jnp.where(row < 4, tiles[0], tiles[1]) + jnp.where(lax.rem(lax.div(row, 2), 2) == 0, tiles[2], tiles[3])
    squares = momenta + own[None]
    positive = squares > 0.001
    return jnp.where(positive, (16.0 * STEP_SIZE / LINE**3) / jnp.where(positive, squares, 1.0), 0.0).reshape(128, 128)


def normalized(row):
    norm = functools.reduce(jnp.add, [e[0] * e[0] + e[1] * e[1] for e in row])
    scale = lax.rsqrt(norm)
    return [scaled(e, scale) for e in row]


def gauge_rows(fields):
    a, b, c = [(fields[i], fields[3 + i]) for i in range(3)]
    h0, h1 = fields[6], fields[7]
    h2 = -(h0 + h1)
    aa, bb, cc = [e[0] * e[0] + e[1] * e[1] for e in (a, b, c)]
    sixth = 1.0 / 6.0

    def turned(u, h):
        return (-(u[1] * h), u[0] * h)

    s01 = minus(turned(a, -h2), times_conj(b, c))
    s02 = plus(turned(b, -h1), times(a, c))
    s12 = minus(turned(c, -h0), times_conj(b, a))
    d0 = 1.0 - (h0 * h0 + aa + bb) * sixth
    d1 = 1.0 - (h1 * h1 + aa + cc) * sixth
    d2 = 1.0 - (h2 * h2 + bb + cc) * sixth

    def upper(u, s):
        return (0.5 * u[0] + s[0] * sixth, 0.5 * u[1] + s[1] * sixth)

    def lower(u, s):
        return (s[0] * sixth - 0.5 * u[0], 0.5 * u[1] - s[1] * sixth)

    inner = [
        [(d0, 0.5 * h0), upper(a, s01), upper(b, s02)],
        [lower(a, s01), (d1, 0.5 * h1), upper(c, s12)],
        [lower(b, s02), lower(c, s12), (d2, 0.5 * h2)],
    ]
    minus_a = (-a[0], a[1])
    p0 = [total([turned(inner[0][j], h0), times(a, inner[1][j]), times(b, inner[2][j])]) for j in range(3)]
    p1 = [total([times(minus_a, inner[0][j]), turned(inner[1][j], h1), times(c, inner[2][j])]) for j in range(3)]
    p0[0] = (p0[0][0] + 1.0, p0[0][1])
    p1[1] = (p1[1][0] + 1.0, p1[1][1])
    row0 = normalized(p0)
    overlap = total([times_conj(p1[j], row0[j]) for j in range(3)])
    row1 = normalized([minus(p1[j], times(overlap, row0[j])) for j in range(3)])
    return [row0, row1]


def completed(rows):
    return rows + [cross_conj(rows[0], rows[1])]


def load_matrix(ref):
    return [[(ref[2 * (3 * a + b)], ref[2 * (3 * a + b) + 1]) for b in range(3)] for a in range(3)]


def store_matrix(ref, matrix):
    for a, row in enumerate(matrix):
        for b, entry in enumerate(row):
            ref[2 * (3 * a + b)] = entry[0]
            ref[2 * (3 * a + b) + 1] = entry[1]


def load_rows(ref):
    return [[(ref[2 * (3 * a + b)], ref[2 * (3 * a + b) + 1]) for b in range(3)] for a in range(2)]


def kernel(
    links, table_hbm, momenta_hbm, sines_hbm, out, factor_t, follow_t,
    u, edge_z, edge_t, sum_send, sums, line_t_send, line_t, line_z_send, line_z, table, momenta, sines, weights,
    plane_send, plane_recv, ring_send, ring_recv, smooth, smooth_za, smooth_zb, smooth_ta, smooth_tb, gauge,
    load_sems, edge_ss, edge_rs, first_ss, first_rs, plane_ss, plane_rs, ring_ss, ring_rs, halo_ss, halo_rs,
):
    gz = lax.axis_index("gz")
    ta = lax.axis_index("ta")
    gz_x, gz_y = lax.div(gz, 4), lax.rem(gz, 4)
    chip, core = lax.div(ta, 2), lax.rem(ta, 2)
    other_core = 1 - core

    def device(z, t_chip, which):
        return z * TA + 2 * t_chip + which

    sibling = device(gz, chip, other_core)
    z_next, z_last = lax.rem(gz + 1, GZ), lax.rem(gz + GZ - 1, GZ)
    t_next, t_last = lax.rem(chip + 1, GZ), lax.rem(chip + GZ - 1, GZ)

    def around(place, step, size):
        return lax.rem(place + step, size)

    offsets = [(dx, dy) for dx in range(4) for dy in range(4) if dx or dy]
    offsets.sort(key=lambda o: -(min(o[0], 4 - o[0]) + min(o[1], 4 - o[1])))
    columns = [around(gz_x, dx, 4) for dx in range(4)]
    lines_y = [around(gz_y, dy, 4) for dy in range(4)]
    plane_partners = [(i, device(i, chip, core)) for i in [columns[dx] * 4 + lines_y[dy] for dx, dy in offsets]]
    steps = sorted(range(1, 16), key=lambda d: -min(d, 16 - d))
    ring_partners = [(i, device(gz, i, core)) for i in [around(chip, d, 16) for d in steps]]
    crossed = [
        device(gz, t_last, other_core),
        device(gz, t_next, other_core),
        device(z_last, chip, other_core),
        device(z_next, chip, other_core),
    ]

    barrier = pltpu.get_barrier_semaphore()

    def greet(target):
        pl.semaphore_signal(barrier, inc=1, device_id=target, device_id_type=LOGICAL)

    loads = [pltpu.make_async_copy(links.at[mu], u.at[core, mu], load_sems.at[mu]) for mu in range(4)]
    constants = [
        pltpu.make_async_copy(momenta_hbm, momenta, load_sems.at[4]),
        pltpu.make_async_copy(sines_hbm.at[chip], sines.at[0], load_sems.at[5]),
        pltpu.make_async_copy(sines_hbm.at[chip + 16], sines.at[1], load_sems.at[6]),
        pltpu.make_async_copy(sines_hbm.at[2 * gz], sines.at[2], load_sems.at[7]),
        pltpu.make_async_copy(sines_hbm.at[2 * gz + 1], sines.at[3], load_sems.at[8]),
        pltpu.make_async_copy(table_hbm, table, load_sems.at[9]),
    ]
    for copy in loads[::-1] + constants[-1:]:
        copy.start()
    for _, target in ring_partners + plane_partners:
        greet(target)
    for target in crossed + [sibling]:
        greet(target)
    for copy in constants[:-1]:
        copy.start()

    def transfer(src, dst, send_sem, recv_sem, target):
        return pltpu.make_async_remote_copy(
            src_ref=src, dst_ref=dst, send_sem=send_sem, recv_sem=recv_sem, device_id=target, device_id_type=LOGICAL
        )

    def exchange(sends, recvs, ss, rs, slot, partners, me, neighbour):
        send, recv = sends.at[slot], recvs.at[slot]
        own = pl.ds(pl.multiple_of(me * 8, 8), 8)

        for index, target in partners:
            theirs = pl.ds(pl.multiple_of(index * 8, 8), 8)
            transfer(send.at[theirs], recv.at[own], ss.at[slot], rs.at[slot], target).start()
        recv[own] = send[own]
        part = pl.ds(0, 120)
        return transfer(send.at[part], recv.at[part], ss.at[slot], rs.at[slot], neighbour)

    def plane_exchange(slot):
        neighbour = device(z_next, chip, core)
        return exchange(plane_send, plane_recv, plane_ss, plane_rs, slot, plane_partners, gz, neighbour)

    def ring_exchange(slot):
        neighbour = device(gz, t_next, core)
        return exchange(ring_send, ring_recv, ring_ss, ring_rs, slot, ring_partners, chip, neighbour)

    def halo_transfers(it):
        mine = smooth.at[it, core]
        ss, rs = halo_ss, halo_rs
        to_sibling = transfer(mine, mine, ss.at[it, 0], rs.at[it, 0], sibling)
        groups = []
        for which, (src, dst, z, t_chip) in enumerate(
            (
                (mine.at[0], smooth_ta.at[it, core], gz, t_last),
                (mine.at[:, :, 0], smooth_za.at[it, core], z_last, chip),
                (mine.at[1], smooth_tb.at[it, core], gz, t_next),
                (mine.at[:, :, 1], smooth_zb.at[it, core], z_next, chip),
            )
        ):
            groups.append(
                [
                    transfer(src, dst, ss.at[it, 1 + 2 * which + h], rs.at[it, 1 + which], device(z, t_chip, h))
                    for h in range(2)
                ]
            )
        if it == ITERS - 1:
            groups[1] = [
                transfer(
                    mine.at[h, :, 0], smooth_za.at[it, core, h], ss.at[it, 3 + h], rs.at[it, 2],
                    device(z_last, chip, h),
                )
                for h in range(2)
            ]
        return to_sibling, groups

    def arrived(it, which, ref):
        transfer(ref.at[it], ref.at[it], halo_ss.at[it, 0], halo_rs.at[it, 1 + which], sibling).wait_recv()

    lane_core = lax.broadcasted_iota(jnp.int32, (8, 128), 0) * 0 + core
    first_half = lane_core == 0

    def own_half(fields):
        return [jnp.where(jnp.broadcast_to(first_half, one.shape), one, two) for one, two in zip(fields[:4], fields[4:])]

    for copy in loads:
        copy.wait()
    lines = [projected(load_matrix(u.at[core, mu])) for mu in range(4)]
    planes = []
    for f in range(8):
        x, y, z, t = [lines[mu][f] for mu in range(4)]
        inner = jnp.concatenate([jnp.zeros((1, 8, 128), F32), z[:1]], axis=0)
        total_here = ((behind_x(x) - x) + (behind_y(y) - y)) + (inner - (z + t))
        planes += [total_here[0], total_here[1], t[0], t[1], z[1]]
    constants[-1].wait()
    planes = right(jnp.concatenate(planes, axis=0), table)
    for f in range(8):
        five = [planes[40 * f + 8 * i : 40 * f + 8 * i + 8] for i in range(5)]
        for z in range(2):
            sum_send[f // 4, f % 4, z] = five[z]
            line_t_send[f // 4, f % 4, z] = five[2 + z]
        line_z_send[f // 4, f % 4] = five[4]
    sums[core] = sum_send[core]

    @pl.when(core == 0)
    def _():
        line_t[1] = line_t_send[0]

    pl.semaphore_wait(barrier, 35)
    sum_out = transfer(sum_send.at[other_core], sums.at[core], first_ss.at[0], first_rs.at[0], sibling)
    sum_in = transfer(sums.at[other_core], sums.at[other_core], first_ss.at[0], first_rs.at[0], sibling)
    t_inner = transfer(line_t_send.at[1], line_t.at[1], first_ss.at[1], first_rs.at[1], sibling)
    t_outer = [
        transfer(line_t_send.at[h], line_t.at[0], first_ss.at[2 + h], first_rs.at[2], device(gz, t_next, h))
        for h in range(2)
    ]
    z_outer = [
        transfer(line_z_send.at[h], line_z.at[core], first_ss.at[4 + h], first_rs.at[3], device(z_next, chip, h))
        for h in range(2)
    ]

    @pl.when(core == 1)
    def _():
        for copy in t_outer:
            copy.start()

    for copy in z_outer:
        copy.start()
    sum_out.start()

    @pl.when(core == 0)
    def _():
        t_inner.start()

    for copy in constants[:-1]:
        copy.wait()
    weights[...] = inverse_momenta(momenta[...], [sines[i] for i in range(4)])
    sum_in.wait_recv()

    @pl.when(core == 1)
    def _():
        t_inner.wait_recv()

    transfer(line_z, line_z, first_ss.at[4], first_rs.at[3], sibling).wait_recv()
    t_outer[0].wait_recv()
    fields = []
    for tl in range(2):
        fields.append([])
        for f in range(4):
            value = sums[tl, f] + line_t[tl, f]
            edge = jnp.stack([line_z[tl, f], jnp.zeros((8, 128), F32)])
            value = value + edge
            factor = 0.5 if f < 2 else jnp.where(jnp.broadcast_to(first_half, value.shape), 0.5, 1.0)
            fields[tl].append(value * factor)
    store_tiles(plane_send.at[0], plane_forward(fields, None))

    to_sibling = [
        transfer(
            links.at[mu, pl.ds(0, 12)], u.at[core, mu, pl.ds(0, 12)], edge_ss.at[5 + mu], edge_rs.at[0], sibling
        )
        for mu in range(4)
    ]
    from_sibling = transfer(
        u.at[other_core, :, pl.ds(0, 12)], u.at[other_core, :, pl.ds(0, 12)], edge_ss.at[0], edge_rs.at[0], sibling
    )
    t_edges = [
        transfer(
            links.at[3, pl.ds(0, 12)], edge_t.at[pl.ds(0, 12)], edge_ss.at[1 + h], edge_rs.at[1], device(gz, t_next, h)
        )
        for h in range(2)
    ]
    z_edges = [
        transfer(
            links.at[2, pl.ds(0, 12), 1], edge_z.at[core, pl.ds(0, 12)], edge_ss.at[3 + h], edge_rs.at[2],
            device(z_next, chip, h),
        )
        for h in range(2)
    ]

    def everything_left():
        sum_out.wait_send()
        for copy in z_outer + z_edges + to_sibling:
            copy.wait_send()

        @pl.when(core == 0)
        def _():
            t_inner.wait_send()

        @pl.when(core == 1)
        def _():
            for copy in t_outer + t_edges:
                copy.wait_send()

        for slot in range(2 * ITERS):
            for send, ss, rs in ((plane_send, plane_ss, plane_rs), (ring_send, ring_ss, ring_rs)):
                part = send.at[slot, pl.ds(0, 120)]
                transfer(part, part, ss.at[slot], rs.at[slot], sibling).wait_send()
        for it in range(ITERS - 1):
            to_other, groups = halo_transfers(it)
            for copy in [to_other] + [copy for group in groups for copy in group]:
                copy.wait_send()

    def beside(it, which):
        if it == 0:
            to_sibling[which].start()
            if which in (1, 2):
                z_edges[which - 1].start()
            else:

                @pl.when(core == 1)
                def _():
                    t_edges[which // 3].start()

    for it in range(ITERS):
        last = it == ITERS - 1
        copy = plane_exchange(2 * it)
        beside(it, 0)
        copy.wait_recv()
        store_tiles(ring_send.at[2 * it], fine_to_coarse(load_tiles(plane_recv.at[2 * it]), 4))
        copy = ring_exchange(2 * it)
        beside(it, 1)
        copy.wait_recv()
        tiles = fine_to_coarse(load_tiles(ring_recv.at[2 * it]), 1)
        tiles = [v * w for v, w in zip(tiles, load_tiles(weights))]
        store_tiles(ring_send.at[2 * it + 1], coarse_to_fine(tiles, 1))
        copy = ring_exchange(2 * it + 1)
        beside(it, 2)
        copy.wait_recv()
        store_tiles(plane_send.at[2 * it + 1], coarse_to_fine(load_tiles(ring_recv.at[2 * it + 1]), 4))
        copy = plane_exchange(2 * it + 1)
        beside(it, 3)
        copy.wait_recv()
        fields = plane_inverse(plane_recv[2 * it + 1], table)
        for tl in range(2):
            for f in range(4):
                smooth[it, core, tl, f] = fields[tl][f]
        to_other, (ahead_t, ahead_z_, after_t, after_z) = halo_transfers(it)
        if last:
            ahead_t[1].start()
        else:
            for copy in ahead_t + after_t:
                copy.start()
        for copy in ahead_z_ + ([] if last else after_z):
            copy.start()
        to_other.start()
        theirs = smooth.at[it, other_core]
        transfer(theirs, theirs, halo_ss.at[it, 0], halo_rs.at[it, 0], sibling).wait_recv()

        def keep(slot, rows):
            store_matrix(gauge.at[slot], rows)

        for tl in range(2):
            keep(tl, gauge_rows([smooth[it, f // 4, tl, f % 4] for f in range(8)]))

        def turned_inside(where, target):
            rows = load_rows(gauge.at[where])
            own = completed(rows)
            for mu, shift in ((0, ahead_x), (1, ahead_y)):
                turned = product_dagger(product(rows, load_matrix(u.at[where, mu])), each(shift, own))
                store_matrix(target.at[mu], completed(turned))
            for mu in (2, 3):
                left = factor_t if last and mu == 3 else u.at[where, mu]
                store_matrix(left, product(rows, load_matrix(u.at[where, mu])))

        def turned_z(where, target, plane, following):
            rows = product_dagger(load_rows(u.at[where, 2, :, plane]), completed(following))
            store_matrix(target.at[2, :, plane], completed(rows))

        def turned_t(where, target, following):
            rows = product_dagger(load_rows(u.at[where, 3]), completed(load_rows(gauge.at[following])))
            store_matrix(target.at[3], completed(rows))

        def edge_gauges(ref, tl):
            return [[tuple(v[tl] for v in e) for e in row] for row in ref]

        if last:
            turned_inside(core, out)
            turned_z(core, out, 0, load_rows(gauge.at[core, :, 1]))
            everything_left()
            part = smooth_za.at[it, :, core]
            transfer(part, part, halo_ss.at[it, 0], halo_rs.at[it, 2], sibling).wait_recv()
            turned_z(core, out, 1, gauge_rows([smooth_za[it, f // 4, core, f % 4] for f in range(8)]))

            @pl.when(core == 0)
            def _():
                follow_t[...] = gauge[1]

            @pl.when(core == 1)
            def _():
                arrived(it, 0, smooth_ta)
                store_matrix(follow_t, gauge_rows([smooth_ta[it, f // 4, f % 4] for f in range(8)]))
        else:
            from_sibling.wait_recv()
            transfer(
                edge_z.at[:, pl.ds(0, 12)], edge_z.at[:, pl.ds(0, 12)], edge_ss.at[0], edge_rs.at[2], sibling
            ).wait_recv()
            t_edges[0].wait_recv()
            missing = [completed(load_rows(u.at[other_core, mu])) for mu in range(4)]
            for mu in range(4):
                store_matrix(u.at[other_core, mu], missing[mu])
            for tl in range(2):
                turned_inside(tl, u.at[tl])
            here = [completed(load_rows(gauge.at[tl])) for tl in range(2)]
            store_matrix(edge_t, product_dagger(completed(load_rows(edge_t)), here[0]))
            for tl in range(2):
                edge = product_dagger(completed(load_rows(edge_z.at[tl])), each(lambda v: v[0], here[tl]))
                store_matrix(edge_z.at[tl], edge)
            turned_t(0, u.at[0], 1)
            for tl in range(2):
                turned_z(tl, u.at[tl], 0, load_rows(gauge.at[tl, :, 1]))
            even_t = own_half(projected(load_matrix(u.at[0, 3])))
            for tl in range(2):
                x, y = [own_half(projected(load_matrix(u.at[tl, mu]))) for mu in range(2)]
                z = own_half(projected(load_matrix(u.at[tl, 2, :, 0])))
                for f in range(4):
                    value = ((behind_x(x[f]) - x[f]) + (behind_y(y[f]) - y[f])) + jnp.stack([-z[f], z[f]])
                    sums[tl, f] = value + even_t[f] if tl else value - even_t[f]
            arrived(it, 1, smooth_za)
            edges = gauge_rows([smooth_za[it, f // 4, :, f % 4] for f in range(8)])
            for tl in range(2):
                turned_z(tl, u.at[tl], 1, edge_gauges(edges, tl))
            arrived(it, 3, smooth_zb)
            edges = gauge_rows([smooth_zb[it, f // 4, :, f % 4] for f in range(8)])
            z_edge = [
                own_half(projected(completed(product(edge_gauges(edges, tl), load_matrix(edge_z.at[tl])))))
                for tl in range(2)
            ]
            z_last_plane = [own_half(projected(load_matrix(u.at[tl, 2, :, 1]))) for tl in range(2)]
            arrived(it, 0, smooth_ta)
            keep(2, gauge_rows([smooth_ta[it, f // 4, f % 4] for f in range(8)]))
            turned_t(1, u.at[1], 2)
            odd_t = own_half(projected(load_matrix(u.at[1, 3])))
            arrived(it, 2, smooth_tb)
            edges = gauge_rows([smooth_tb[it, f // 4, f % 4] for f in range(8)])
            t_edge = own_half(projected(completed(product(edges, load_matrix(edge_t)))))
            fields = []
            for tl in range(2):
                fields.append([])
                for f in range(4):
                    value = sums[tl, f] + jnp.stack([z_edge[tl][f], -z_last_plane[tl][f]])
                    value = value - odd_t[f] if tl else value + t_edge[f]
                    factor = 0.5 if f < 2 else jnp.where(jnp.broadcast_to(first_half, value.shape), 0.5, 1.0)
                    fields[tl].append(value * factor)
            plane_send[2 * it + 2] = plane_forward(fields, table)

    to_other, (ahead_t, ahead_z_, after_t, after_z) = halo_transfers(ITERS - 1)
    for copy in [to_other] + ahead_z_ + ahead_t[1:]:
        copy.wait_send()


def closing_kernel(done, factor_t, follow_t, out, last_links, sems):
    copies = [pltpu.make_async_copy(done.at[mu], out.at[mu], sems.at[mu]) for mu in range(3)]
    copies.append(pltpu.make_async_copy(last_links, out.at[3], sems.at[3]))
    for copy in copies[:3]:
        copy.start()
    store_matrix(last_links, completed(product_dagger(load_rows(factor_t), completed(load_rows(follow_t)))))
    copies[3].start()
    for copy in copies:
        copy.wait()


def shards(links):
    constants = [jnp.asarray(t) for t in tables()]
    anywhere = pl.BlockSpec(memory_space=pl.ANY)
    vmem = pltpu.VMEM
    dma = pltpu.SemaphoreType.DMA
    slots = 2 * ITERS
    parts = pl.pallas_call(
        kernel,
        out_shape=[vmem((3, 18, 2, 8, 128), F32), vmem((12, 2, 8, 128), F32), vmem((12, 2, 8, 128), F32)],
        in_specs=[anywhere] * 4,
        out_specs=[pl.BlockSpec(memory_space=vmem)] * 3,
        scratch_shapes=[
            vmem((2, 4, 18, 2, 8, 128), F32),
            vmem((2, 18, 8, 128), F32),
            vmem((18, 2, 8, 128), F32),
            vmem((2, 4, 2, 8, 128), F32),
            vmem((2, 4, 2, 8, 128), F32),
            vmem((2, 4, 2, 8, 128), F32),
            vmem((2, 4, 2, 8, 128), F32),
            vmem((2, 4, 8, 128), F32),
            vmem((2, 4, 8, 128), F32),
            vmem((256, 128), BF16),
            vmem((16, 8, 128), F32),
            vmem((4, 8, 128), F32),
            vmem((128, 128), F32),
            vmem((slots, 128, 128), F32),
            vmem((slots, 128, 128), F32),
            vmem((slots, 128, 128), F32),
            vmem((slots, 128, 128), F32),
            vmem((ITERS, 2, 2, 4, 2, 8, 128), F32),
            vmem((ITERS, 2, 2, 4, 8, 128), F32),
            vmem((ITERS, 2, 2, 4, 8, 128), F32),
            vmem((ITERS, 2, 4, 2, 8, 128), F32),
            vmem((ITERS, 2, 4, 2, 8, 128), F32),
            vmem((3, 12, 2, 8, 128), F32),
            dma((10,)),
            dma((9,)),
            dma((3,)),
            dma((6,)),
            dma((4,)),
            dma((slots,)),
            dma((slots,)),
            dma((slots,)),
            dma((slots,)),
            dma((ITERS, 9)),
            dma((ITERS, 5)),
        ],
        compiler_params=pltpu.CompilerParams(
            collective_id=0, has_side_effects=True, vmem_limit_bytes=40 * 1024 * 1024
        ),
    )(*[pltpu.with_memory_space_constraint(a, pltpu.HBM) for a in [links.reshape(4, 18, 2, 8, 128)] + constants])
    result = pl.pallas_call(
        closing_kernel,
        out_shape=jax.ShapeDtypeStruct((4, 18, 2, 8, 128), F32),
        in_specs=[pl.BlockSpec(memory_space=vmem)] * 3,
        out_specs=anywhere,
        scratch_shapes=[vmem((18, 2, 8, 128), F32), dma((4,))],
        compiler_params=pltpu.CompilerParams(vmem_limit_bytes=40 * 1024 * 1024),
    )(*parts)
    return result.reshape(links.shape)


def solution(mesh):
    return jax.shard_map(
        shards,
        mesh=mesh,
        in_specs=(P(None, None, "gz", "ta", None),),
        out_specs=P(None, None, "gz", "ta", None),
        check_vma=False,
    )
```

```python
import functools
import math

import jax
import jax.numpy as jnp
import numpy as np
from jax import lax
from jax.experimental import pallas as pl
from jax.experimental.pallas import tpu as pltpu
from jax.sharding import PartitionSpec as P

ITERS = 2
STEP_SIZE = 0.08
LINE = 32
GZ = 16
TA = 32
PAIRS = ((0, 1), (0, 2), (1, 2))
LOGICAL = pl.DeviceIdType.LOGICAL
F32 = jnp.float32
BF16 = jnp.bfloat16


def halves(table):
    high = table.astype(jnp.bfloat16)
    return high, (table - high.astype(np.float64)).astype(jnp.bfloat16)


def tables():
    phase = 2.0 * np.pi * (np.outer(np.arange(LINE), np.arange(LINE)) % LINE) / LINE
    plane = np.kron(np.eye(4), (np.cos(phase) + np.sin(phase)) / np.sqrt(LINE))
    sines = 4.0 * np.sin(np.pi * np.arange(LINE) / LINE) ** 2
    row = np.arange(128)
    momenta = sines[row // 8 + 16 * (row % 2)][:, None] + np.tile(sines, 4)[None, :]
    tiles = np.broadcast_to(sines[:, None, None], (LINE, 8, 128))
    return (
        np.concatenate(halves(plane), axis=0),
        momenta.reshape(16, 8, 128).astype(np.float32),
        np.ascontiguousarray(tiles).astype(np.float32),
    )


def times(u, v):
    return (u[0] * v[0] - u[1] * v[1], u[0] * v[1] + u[1] * v[0])


def times_conj(u, v):
    return (u[0] * v[0] + u[1] * v[1], u[1] * v[0] - u[0] * v[1])


def plus(u, v):
    return (u[0] + v[0], u[1] + v[1])


def minus(u, v):
    return (u[0] - v[0], u[1] - v[1])


def conj(u):
    return (u[0], -u[1])


def scaled(u, factor):
    return (u[0] * factor, u[1] * factor)


def total(terms):
    return functools.reduce(plus, terms)


def product(left, right):
    return [[total([times(left[a][j], right[j][b]) for j in range(3)]) for b in range(3)] for a in range(len(left))]


def product_dagger(left, right):
    return [[total([times_conj(left[a][j], right[b][j]) for j in range(3)]) for b in range(3)] for a in range(len(left))]


def cross_conj(u, v):
    row = []
    for c in range(3):
        n, m = (c + 1) % 3, (c + 2) % 3
        row.append(conj(minus(times(u[n], v[m]), times(u[m], v[n]))))
    return row


def each(function, matrix):
    return [[(function(e[0]), function(e[1])) for e in row] for row in matrix]


def lanes(v):
    return lax.broadcasted_iota(jnp.int32, v.shape, v.ndim - 1)


def roll(v, shift, axis):
    return pltpu.roll(v, shift, axis)


def behind_x(v):
    moved = roll(v, 32, v.ndim - 1)
    return jnp.where(lanes(v) < 32, roll(moved, 1, v.ndim - 2), moved)


def ahead_x(v):
    moved = roll(v, 96, v.ndim - 1)
    return jnp.where(lanes(v) >= 96, roll(moved, 7, v.ndim - 2), moved)


def behind_y(v):
    return jnp.where(lanes(v) % 32 == 0, roll(v, 97, v.ndim - 1), roll(v, 1, v.ndim - 1))


def ahead_y(v):
    return jnp.where(lanes(v) % 32 == 31, roll(v, 31, v.ndim - 1), roll(v, 127, v.ndim - 1))


def behind_z(v, edge):
    return jnp.concatenate([edge[None], v[:1]], axis=0)


def ahead_z(v, edge):
    return jnp.concatenate([v[1:], edge[None]], axis=0)


def projected(u):
    third = (u[0][0][1] + u[1][1][1] + u[2][2][1]) * (1.0 / 3.0)
    return (
        [u[a][b][0] - u[b][a][0] for a, b in PAIRS]
        + [u[a][b][1] + u[b][a][1] for a, b in PAIRS]
        + [u[0][0][1] - third, u[1][1][1] - third]
    )


def block_transpose(planes):
    lane = lanes(planes[0])
    axis = planes[0].ndim - 1
    low = lane < 64
    even = (lane // 32) % 2 == 0
    first = [jnp.where(low, planes[p], roll(planes[p + 2], 64, axis)) for p in range(2)]
    second = [jnp.where(low, roll(planes[p], 64, axis), planes[p + 2]) for p in range(2)]
    out = []
    for one, two in (first, second):
        out.append(jnp.where(even, one, roll(two, 32, axis)))
        out.append(jnp.where(even, roll(one, 96, axis), two))
    return out


def rows_of(v):
    return lax.broadcasted_iota(jnp.int32, v.shape, v.ndim - 2)


def bit_exchange(one, two, stride):
    clear = lax.rem(lax.div(rows_of(one), stride), 2) == 0
    return (
        jnp.where(clear, one, roll(two, stride, one.ndim - 2)),
        jnp.where(clear, roll(one, 8 - stride, one.ndim - 2), two),
    )


def middle_exchange(v):
    pair = lax.div(rows_of(v), 2)
    return jnp.where(pair == 1, roll(v, 6, 0), jnp.where(pair == 2, roll(v, 2, 0), v))


def hartley(v):
    size = len(v)
    if size == 1:
        return v
    even, odd = hartley(v[0::2]), hartley(v[1::2])
    half = size // 2
    out = [None] * size
    for k in range(half):
        turned = odd[k]
        if k and 4 * k != size:
            angle = 2.0 * math.pi * k / size
            turned = odd[k] * math.cos(angle) + odd[half - k] * math.sin(angle)
        out[k], out[k + half] = even[k] + turned, even[k] - turned
    return out


def bit_clear(v, stride):
    return lax.rem(lax.div(rows_of(v), stride), 2) == 0


def rotated(v, stride):
    low = bit_clear(v[0], stride)
    out = list(v)
    for k in range(1, 16):
        if k != 8:
            angle = math.pi * k / 16
            out[k] = v[k] * jnp.where(low, 1.0, math.cos(angle)) + v[16 - k] * jnp.where(low, 0.0, math.sin(angle))
    return out


def butterflies(v, stride):
    low = bit_clear(v[0], stride)
    out = []
    for e in v:
        other = roll(e, stride, 0)
        if stride != 4:
            other = jnp.where(low, roll(e, 8 - stride, 0), other)
        out.append(other + jnp.where(low, e, -e))
    return out


def fine_to_coarse(v, stride):
    return butterflies(rotated(hartley(v), stride), stride)


def coarse_to_fine(v, stride):
    return hartley(rotated(butterflies(v, stride), stride))


def tiles_of(matrix):
    return [matrix[8 * i : 8 * i + 8] for i in range(16)]


def plane_forward(fields, table):
    parts = [block_transpose(fields[tl]) for tl in range(2)]
    tiles = [None] * 16
    for b in range(4):
        traded = [bit_exchange(parts[tl][b][0], parts[tl][b][1], 2) for tl in range(2)]
        for bit in range(2):
            tiles[8 * bit + b], tiles[8 * bit + 4 + b] = bit_exchange(traded[0][bit], traded[1][bit], 1)
    tiles = [middle_exchange(v) for v in coarse_to_fine(tiles, 4)]
    return tiles if table is None else right(jnp.concatenate(tiles, axis=0), table)


def plane_inverse(matrix, table):
    tiles = fine_to_coarse([middle_exchange(v) for v in tiles_of(right(matrix, table))], 4)
    blocks = [[None] * 4 for _ in range(2)]
    for b in range(4):
        pairs = [bit_exchange(tiles[8 * bit + b], tiles[8 * bit + 4 + b], 1) for bit in range(2)]
        for tl in range(2):
            blocks[tl][b] = jnp.stack(bit_exchange(pairs[0][tl], pairs[1][tl], 2))
    return [block_transpose(blocks[tl]) for tl in range(2)]


def split(v):
    high = v.astype(BF16)
    return high, (v - high.astype(F32)).astype(BF16)


def right(v, table):
    table_high, table_low = table[pl.ds(0, 128)], table[pl.ds(128, 128)]
    high, low = split(v)
    return jnp.dot(
        jnp.concatenate([high, low, high], axis=1),
        jnp.concatenate([table_high, table_high, table_low], axis=0),
        preferred_element_type=F32,
    )


def store_tiles(ref, tiles):
    for i, tile in enumerate(tiles):
        ref[pl.ds(8 * i, 8)] = tile


def load_tiles(ref):
    return [ref[pl.ds(8 * i, 8)] for i in range(16)]


def inverse_momenta(momenta, tiles):
    row = lax.broadcasted_iota(jnp.int32, (8, 128), 0)
    own = jnp.where(row < 4, tiles[0], tiles[1]) + jnp.where(lax.rem(lax.div(row, 2), 2) == 0, tiles[2], tiles[3])
    squares = momenta + own[None]
    positive = squares > 0.001
    return jnp.where(positive, (16.0 * STEP_SIZE / LINE**3) / jnp.where(positive, squares, 1.0), 0.0).reshape(128, 128)


def normalized(row):
    norm = functools.reduce(jnp.add, [e[0] * e[0] + e[1] * e[1] for e in row])
    scale = lax.rsqrt(norm)
    return [scaled(e, scale) for e in row]


def gauge_rows(fields):
    a, b, c = [(fields[i], fields[3 + i]) for i in range(3)]
    h0, h1 = fields[6], fields[7]
    h2 = -(h0 + h1)
    aa, bb, cc = [e[0] * e[0] + e[1] * e[1] for e in (a, b, c)]
    sixth = 1.0 / 6.0

    def turned(u, h):
        return (-(u[1] * h), u[0] * h)

    s01 = minus(turned(a, -h2), times_conj(b, c))
    s02 = plus(turned(b, -h1), times(a, c))
    s12 = minus(turned(c, -h0), times_conj(b, a))
    d0 = 1.0 - (h0 * h0 + aa + bb) * sixth
    d1 = 1.0 - (h1 * h1 + aa + cc) * sixth
    d2 = 1.0 - (h2 * h2 + bb + cc) * sixth

    def upper(u, s):
        return (0.5 * u[0] + s[0] * sixth, 0.5 * u[1] + s[1] * sixth)

    def lower(u, s):
        return (s[0] * sixth - 0.5 * u[0], 0.5 * u[1] - s[1] * sixth)

    inner = [
        [(d0, 0.5 * h0), upper(a, s01), upper(b, s02)],
        [lower(a, s01), (d1, 0.5 * h1), upper(c, s12)],
        [lower(b, s02), lower(c, s12), (d2, 0.5 * h2)],
    ]
    minus_a = (-a[0], a[1])
    p0 = [total([turned(inner[0][j], h0), times(a, inner[1][j]), times(b, inner[2][j])]) for j in range(3)]
    p1 = [total([times(minus_a, inner[0][j]), turned(inner[1][j], h1), times(c, inner[2][j])]) for j in range(3)]
    p0[0] = (p0[0][0] + 1.0, p0[0][1])
    p1[1] = (p1[1][0] + 1.0, p1[1][1])
    row0 = normalized(p0)
    overlap = total([times_conj(p1[j], row0[j]) for j in range(3)])
    row1 = normalized([minus(p1[j], times(overlap, row0[j])) for j in range(3)])
    return [row0, row1]


def completed(rows):
    return rows + [cross_conj(rows[0], rows[1])]


def load_matrix(ref):
    return [[(ref[2 * (3 * a + b)], ref[2 * (3 * a + b) + 1]) for b in range(3)] for a in range(3)]


def store_matrix(ref, matrix):
    for a, row in enumerate(matrix):
        for b, entry in enumerate(row):
            ref[2 * (3 * a + b)] = entry[0]
            ref[2 * (3 * a + b) + 1] = entry[1]


def load_rows(ref):
    return [[(ref[2 * (3 * a + b)], ref[2 * (3 * a + b) + 1]) for b in range(3)] for a in range(2)]


def kernel(
    links, table_hbm, momenta_hbm, sines_hbm, out, factor_t, follow_t,
    u, edge_z, edge_t, sum_send, sums, line_t_send, line_t, line_z_send, line_z, table, momenta, sines, weights,
    plane_send, plane_recv, ring_send, ring_recv, smooth, smooth_za, smooth_zb, smooth_ta, smooth_tb, gauge,
    load_sems, edge_ss, edge_rs, first_ss, first_rs, plane_ss, plane_rs, ring_ss, ring_rs, halo_ss, halo_rs,
):
    gz = lax.axis_index("gz")
    ta = lax.axis_index("ta")
    gz_x, gz_y = lax.div(gz, 4), lax.rem(gz, 4)
    chip, core = lax.div(ta, 2), lax.rem(ta, 2)
    other_core = 1 - core

    def device(z, t_chip, which):
        return z * TA + 2 * t_chip + which

    sibling = device(gz, chip, other_core)
    z_next, z_last = lax.rem(gz + 1, GZ), lax.rem(gz + GZ - 1, GZ)
    t_next, t_last = lax.rem(chip + 1, GZ), lax.rem(chip + GZ - 1, GZ)

    def around(place, step, size):
        return lax.rem(place + step, size)

    offsets = [(dx, dy) for dx in range(4) for dy in range(4) if dx or dy]
    offsets.sort(key=lambda o: -(min(o[0], 4 - o[0]) + min(o[1], 4 - o[1])))
    columns = [around(gz_x, dx, 4) for dx in range(4)]
    lines_y = [around(gz_y, dy, 4) for dy in range(4)]
    plane_partners = [(i, device(i, chip, core)) for i in [columns[dx] * 4 + lines_y[dy] for dx, dy in offsets]]
    steps = sorted(range(1, 16), key=lambda d: -min(d, 16 - d))
    ring_partners = [(i, device(gz, i, core)) for i in [around(chip, d, 16) for d in steps]]
    crossed = [
        device(gz, t_last, other_core),
        device(gz, t_next, other_core),
        device(z_last, chip, other_core),
        device(z_next, chip, other_core),
    ]

    barrier = pltpu.get_barrier_semaphore()

    def greet(target):
        pl.semaphore_signal(barrier, inc=1, device_id=target, device_id_type=LOGICAL)

    loads = [pltpu.make_async_copy(links.at[mu], u.at[core, mu], load_sems.at[mu]) for mu in range(4)]
    constants = [
        pltpu.make_async_copy(momenta_hbm, momenta, load_sems.at[4]),
        pltpu.make_async_copy(sines_hbm.at[chip], sines.at[0], load_sems.at[5]),
        pltpu.make_async_copy(sines_hbm.at[chip + 16], sines.at[1], load_sems.at[6]),
        pltpu.make_async_copy(sines_hbm.at[2 * gz], sines.at[2], load_sems.at[7]),
        pltpu.make_async_copy(sines_hbm.at[2 * gz + 1], sines.at[3], load_sems.at[8]),
        pltpu.make_async_copy(table_hbm, table, load_sems.at[9]),
    ]
    for copy in loads[::-1] + constants[-1:]:
        copy.start()
    for _, target in ring_partners + plane_partners:
        greet(target)
    for target in crossed + [sibling]:
        greet(target)
    for copy in constants[:-1]:
        copy.start()

    def transfer(src, dst, send_sem, recv_sem, target):
        return pltpu.make_async_remote_copy(
            src_ref=src, dst_ref=dst, send_sem=send_sem, recv_sem=recv_sem, device_id=target, device_id_type=LOGICAL
        )

    def exchange(sends, recvs, ss, rs, slot, partners, me, neighbour):
        send, recv = sends.at[slot], recvs.at[slot]
        own = pl.ds(pl.multiple_of(me * 8, 8), 8)

        for index, target in partners:
            theirs = pl.ds(pl.multiple_of(index * 8, 8), 8)
            transfer(send.at[theirs], recv.at[own], ss.at[slot], rs.at[slot], target).start()
        recv[own] = send[own]
        part = pl.ds(0, 120)
        return transfer(send.at[part], recv.at[part], ss.at[slot], rs.at[slot], neighbour)

    def plane_exchange(slot):
        neighbour = device(z_next, chip, core)
        return exchange(plane_send, plane_recv, plane_ss, plane_rs, slot, plane_partners, gz, neighbour)

    def ring_exchange(slot):
        neighbour = device(gz, t_next, core)
        return exchange(ring_send, ring_recv, ring_ss, ring_rs, slot, ring_partners, chip, neighbour)

    def halo_transfers(it):
        mine = smooth.at[it, core]
        ss, rs = halo_ss, halo_rs
        to_sibling = transfer(mine, mine, ss.at[it, 0], rs.at[it, 0], sibling)
        groups = []
        for which, (src, dst, z, t_chip) in enumerate(
            (
                (mine.at[0], smooth_ta.at[it, core], gz, t_last),
                (mine.at[:, :, 0], smooth_za.at[it, core], z_last, chip),
                (mine.at[1], smooth_tb.at[it, core], gz, t_next),
                (mine.at[:, :, 1], smooth_zb.at[it, core], z_next, chip),
            )
        ):
            groups.append(
                [
                    transfer(src, dst, ss.at[it, 1 + 2 * which + h], rs.at[it, 1 + which], device(z, t_chip, h))
                    for h in range(2)
                ]
            )
        if it == ITERS - 1:
            groups[1] = [
                transfer(
                    mine.at[h, :, 0], smooth_za.at[it, core, h], ss.at[it, 3 + h], rs.at[it, 2],
                    device(z_last, chip, h),
                )
                for h in range(2)
            ]
        return to_sibling, groups

    def arrived(it, which, ref):
        transfer(ref.at[it], ref.at[it], halo_ss.at[it, 0], halo_rs.at[it, 1 + which], sibling).wait_recv()

    lane_core = lax.broadcasted_iota(jnp.int32, (8, 128), 0) * 0 + core
    first_half = lane_core == 0

    def own_half(fields):
        return [jnp.where(jnp.broadcast_to(first_half, one.shape), one, two) for one, two in zip(fields[:4], fields[4:])]

    for copy in loads:
        copy.wait()
    lines = [projected(load_matrix(u.at[core, mu])) for mu in range(4)]
    planes = []
    for f in range(8):
        x, y, z, t = [lines[mu][f] for mu in range(4)]
        inner = jnp.concatenate([jnp.zeros((1, 8, 128), F32), z[:1]], axis=0)
        total_here = ((behind_x(x) - x) + (behind_y(y) - y)) + (inner - (z + t))
        planes += [total_here[0], total_here[1], t[0], t[1], z[1]]
    constants[-1].wait()
    planes = right(jnp.concatenate(planes, axis=0), table)
    for f in range(8):
        five = [planes[40 * f + 8 * i : 40 * f + 8 * i + 8] for i in range(5)]
        for z in range(2):
            sum_send[f // 4, f % 4, z] = five[z]
            line_t_send[f // 4, f % 4, z] = five[2 + z]
        line_z_send[f // 4, f % 4] = five[4]
    sums[core] = sum_send[core]

    @pl.when(core == 0)
    def _():
        line_t[1] = line_t_send[0]

    pl.semaphore_wait(barrier, 35)
    sum_out = transfer(sum_send.at[other_core], sums.at[core], first_ss.at[0], first_rs.at[0], sibling)
    sum_in = transfer(sums.at[other_core], sums.at[other_core], first_ss.at[0], first_rs.at[0], sibling)
    t_inner = transfer(line_t_send.at[1], line_t.at[1], first_ss.at[1], first_rs.at[1], sibling)
    t_outer = [
        transfer(line_t_send.at[h], line_t.at[0], first_ss.at[2 + h], first_rs.at[2], device(gz, t_next, h))
        for h in range(2)
    ]
    z_outer = [
        transfer(line_z_send.at[h], line_z.at[core], first_ss.at[4 + h], first_rs.at[3], device(z_next, chip, h))
        for h in range(2)
    ]

    @pl.when(core == 1)
    def _():
        for copy in t_outer:
            copy.start()

    for copy in z_outer:
        copy.start()
    sum_out.start()

    @pl.when(core == 0)
    def _():
        t_inner.start()

    for copy in constants[:-1]:
        copy.wait()
    weights[...] = inverse_momenta(momenta[...], [sines[i] for i in range(4)])
    sum_in.wait_recv()

    @pl.when(core == 1)
    def _():
        t_inner.wait_recv()

    transfer(line_z, line_z, first_ss.at[4], first_rs.at[3], sibling).wait_recv()
    t_outer[0].wait_recv()
    fields = []
    for tl in range(2):
        fields.append([])
        for f in range(4):
            value = sums[tl, f] + line_t[tl, f]
            edge = jnp.stack([line_z[tl, f], jnp.zeros((8, 128), F32)])
            value = value + edge
            factor = 0.5 if f < 2 else jnp.where(jnp.broadcast_to(first_half, value.shape), 0.5, 1.0)
            fields[tl].append(value * factor)
    store_tiles(plane_send.at[0], plane_forward(fields, None))

    to_sibling = [
        transfer(
            links.at[mu, pl.ds(0, 12)], u.at[core, mu, pl.ds(0, 12)], edge_ss.at[5 + mu], edge_rs.at[0], sibling
        )
        for mu in range(4)
    ]
    from_sibling = transfer(
        u.at[other_core, :, pl.ds(0, 12)], u.at[other_core, :, pl.ds(0, 12)], edge_ss.at[0], edge_rs.at[0], sibling
    )
    t_edges = [
        transfer(
            links.at[3, pl.ds(0, 12)], edge_t.at[pl.ds(0, 12)], edge_ss.at[1 + h], edge_rs.at[1], device(gz, t_next, h)
        )
        for h in range(2)
    ]
    z_edges = [
        transfer(
            links.at[2, pl.ds(0, 12), 1], edge_z.at[core, pl.ds(0, 12)], edge_ss.at[3 + h], edge_rs.at[2],
            device(z_next, chip, h),
        )
        for h in range(2)
    ]

    def everything_left():
        sum_out.wait_send()
        for copy in z_outer + z_edges + to_sibling:
            copy.wait_send()

        @pl.when(core == 0)
        def _():
            t_inner.wait_send()

        @pl.when(core == 1)
        def _():
            for copy in t_outer + t_edges:
                copy.wait_send()

        for slot in range(2 * ITERS):
            for send, ss, rs in ((plane_send, plane_ss, plane_rs), (ring_send, ring_ss, ring_rs)):
                part = send.at[slot, pl.ds(0, 120)]
                transfer(part, part, ss.at[slot], rs.at[slot], sibling).wait_send()
        for it in range(ITERS - 1):
            to_other, groups = halo_transfers(it)
            for copy in [to_other] + [copy for group in groups for copy in group]:
                copy.wait_send()

    def beside(it, which):
        if it == 0:
            to_sibling[which].start()
            if which in (1, 2):
                z_edges[which - 1].start()
            else:

                @pl.when(core == 1)
                def _():
                    t_edges[which // 3].start()

    for it in range(ITERS):
        last = it == ITERS - 1
        copy = plane_exchange(2 * it)
        beside(it, 0)
        copy.wait_recv()
        store_tiles(ring_send.at[2 * it], fine_to_coarse(load_tiles(plane_recv.at[2 * it]), 4))
        copy = ring_exchange(2 * it)
        beside(it, 1)
        copy.wait_recv()
        tiles = fine_to_coarse(load_tiles(ring_recv.at[2 * it]), 1)
        tiles = [v * w for v, w in zip(tiles, load_tiles(weights))]
        store_tiles(ring_send.at[2 * it + 1], coarse_to_fine(tiles, 1))
        copy = ring_exchange(2 * it + 1)
        beside(it, 2)
        copy.wait_recv()
        store_tiles(plane_send.at[2 * it + 1], coarse_to_fine(load_tiles(ring_recv.at[2 * it + 1]), 4))
        copy = plane_exchange(2 * it + 1)
        beside(it, 3)
        copy.wait_recv()
        fields = plane_inverse(plane_recv[2 * it + 1], table)
        for tl in range(2):
            for f in range(4):
                smooth[it, core, tl, f] = fields[tl][f]
        to_other, (ahead_t, ahead_z_, after_t, after_z) = halo_transfers(it)
        if last:
            order = ahead_z_ + ahead_t[1:] + [to_other]
        else:
            order = ahead_z_ + after_z + [to_other] + ahead_t + after_t
        for copy in order:
            copy.start()
        theirs = smooth.at[it, other_core]
        transfer(theirs, theirs, halo_ss.at[it, 0], halo_rs.at[it, 0], sibling).wait_recv()

        def keep(slot, rows):
            store_matrix(gauge.at[slot], rows)

        for tl in range(2):
            keep(tl, gauge_rows([smooth[it, f // 4, tl, f % 4] for f in range(8)]))

        def turned_inside(where, target):
            rows = load_rows(gauge.at[where])
            own = completed(rows)
            for mu, shift in ((0, ahead_x), (1, ahead_y)):
                turned = product_dagger(product(rows, load_matrix(u.at[where, mu])), each(shift, own))
                store_matrix(target.at[mu], completed(turned))
            for mu in (2, 3):
                left = factor_t if last and mu == 3 else u.at[where, mu]
                store_matrix(left, product(rows, load_matrix(u.at[where, mu])))

        def turned_z(where, target, plane, following):
            rows = product_dagger(load_rows(u.at[where, 2, :, plane]), completed(following))
            store_matrix(target.at[2, :, plane], completed(rows))

        def turned_t(where, target, following):
            rows = product_dagger(load_rows(u.at[where, 3]), completed(load_rows(gauge.at[following])))
            store_matrix(target.at[3], completed(rows))

        def edge_gauges(ref, tl):
            return [[tuple(v[tl] for v in e) for e in row] for row in ref]

        if last:
            turned_inside(core, out)
            turned_z(core, out, 0, load_rows(gauge.at[core, :, 1]))
            everything_left()
            part = smooth_za.at[it, :, core]
            transfer(part, part, halo_ss.at[it, 0], halo_rs.at[it, 2], sibling).wait_recv()
            turned_z(core, out, 1, gauge_rows([smooth_za[it, f // 4, core, f % 4] for f in range(8)]))

            @pl.when(core == 0)
            def _():
                follow_t[...] = gauge[1]

            @pl.when(core == 1)
            def _():
                arrived(it, 0, smooth_ta)
                store_matrix(follow_t, gauge_rows([smooth_ta[it, f // 4, f % 4] for f in range(8)]))
        else:
            from_sibling.wait_recv()
            transfer(
                edge_z.at[:, pl.ds(0, 12)], edge_z.at[:, pl.ds(0, 12)], edge_ss.at[0], edge_rs.at[2], sibling
            ).wait_recv()
            t_edges[0].wait_recv()
            missing = [completed(load_rows(u.at[other_core, mu])) for mu in range(4)]
            for mu in range(4):
                store_matrix(u.at[other_core, mu], missing[mu])
            for tl in range(2):
                turned_inside(tl, u.at[tl])
            here = [completed(load_rows(gauge.at[tl])) for tl in range(2)]
            store_matrix(edge_t, product_dagger(completed(load_rows(edge_t)), here[0]))
            for tl in range(2):
                edge = product_dagger(completed(load_rows(edge_z.at[tl])), each(lambda v: v[0], here[tl]))
                store_matrix(edge_z.at[tl], edge)
            turned_t(0, u.at[0], 1)
            for tl in range(2):
                turned_z(tl, u.at[tl], 0, load_rows(gauge.at[tl, :, 1]))
            even_t = own_half(projected(load_matrix(u.at[0, 3])))
            for tl in range(2):
                x, y = [own_half(projected(load_matrix(u.at[tl, mu]))) for mu in range(2)]
                z = own_half(projected(load_matrix(u.at[tl, 2, :, 0])))
                for f in range(4):
                    value = ((behind_x(x[f]) - x[f]) + (behind_y(y[f]) - y[f])) + jnp.stack([-z[f], z[f]])
                    sums[tl, f] = value + even_t[f] if tl else value - even_t[f]
            arrived(it, 1, smooth_za)
            edges = gauge_rows([smooth_za[it, f // 4, :, f % 4] for f in range(8)])
            for tl in range(2):
                turned_z(tl, u.at[tl], 1, edge_gauges(edges, tl))
            arrived(it, 3, smooth_zb)
            edges = gauge_rows([smooth_zb[it, f // 4, :, f % 4] for f in range(8)])
            z_edge = [
                own_half(projected(completed(product(edge_gauges(edges, tl), load_matrix(edge_z.at[tl])))))
                for tl in range(2)
            ]
            z_last_plane = [own_half(projected(load_matrix(u.at[tl, 2, :, 1]))) for tl in range(2)]
            arrived(it, 0, smooth_ta)
            keep(2, gauge_rows([smooth_ta[it, f // 4, f % 4] for f in range(8)]))
            turned_t(1, u.at[1], 2)
            odd_t = own_half(projected(load_matrix(u.at[1, 3])))
            arrived(it, 2, smooth_tb)
            edges = gauge_rows([smooth_tb[it, f // 4, f % 4] for f in range(8)])
            t_edge = own_half(projected(completed(product(edges, load_matrix(edge_t)))))
            fields = []
            for tl in range(2):
                fields.append([])
                for f in range(4):
                    value = sums[tl, f] + jnp.stack([z_edge[tl][f], -z_last_plane[tl][f]])
                    value = value - odd_t[f] if tl else value + t_edge[f]
                    factor = 0.5 if f < 2 else jnp.where(jnp.broadcast_to(first_half, value.shape), 0.5, 1.0)
                    fields[tl].append(value * factor)
            plane_send[2 * it + 2] = plane_forward(fields, table)

    to_other, (ahead_t, ahead_z_, after_t, after_z) = halo_transfers(ITERS - 1)
    for copy in [to_other] + ahead_z_ + ahead_t[1:]:
        copy.wait_send()


def closing_kernel(done, factor_t, follow_t, out, last_links, sems):
    pieces = [(mu, pl.ds(9 * half, 9)) for mu in range(4) for half in range(2)]
    copies = [
        pltpu.make_async_copy((last_links if mu == 3 else done.at[mu]).at[part], out.at[mu, part], sems.at[i])
        for i, (mu, part) in enumerate(pieces)
    ]
    for copy in copies[:6]:
        copy.start()
    store_matrix(last_links, completed(product_dagger(load_rows(factor_t), completed(load_rows(follow_t)))))
    for copy in copies[6:]:
        copy.start()
    for copy in copies:
        copy.wait()


def shards(links):
    constants = [jnp.asarray(t) for t in tables()]
    anywhere = pl.BlockSpec(memory_space=pl.ANY)
    vmem = pltpu.VMEM
    dma = pltpu.SemaphoreType.DMA
    slots = 2 * ITERS
    parts = pl.pallas_call(
        kernel,
        out_shape=[vmem((3, 18, 2, 8, 128), F32), vmem((12, 2, 8, 128), F32), vmem((12, 2, 8, 128), F32)],
        in_specs=[anywhere] * 4,
        out_specs=[pl.BlockSpec(memory_space=vmem)] * 3,
        scratch_shapes=[
            vmem((2, 4, 18, 2, 8, 128), F32),
            vmem((2, 18, 8, 128), F32),
            vmem((18, 2, 8, 128), F32),
            vmem((2, 4, 2, 8, 128), F32),
            vmem((2, 4, 2, 8, 128), F32),
            vmem((2, 4, 2, 8, 128), F32),
            vmem((2, 4, 2, 8, 128), F32),
            vmem((2, 4, 8, 128), F32),
            vmem((2, 4, 8, 128), F32),
            vmem((256, 128), BF16),
            vmem((16, 8, 128), F32),
            vmem((4, 8, 128), F32),
            vmem((128, 128), F32),
            vmem((slots, 128, 128), F32),
            vmem((slots, 128, 128), F32),
            vmem((slots, 128, 128), F32),
            vmem((slots, 128, 128), F32),
            vmem((ITERS, 2, 2, 4, 2, 8, 128), F32),
            vmem((ITERS, 2, 2, 4, 8, 128), F32),
            vmem((ITERS, 2, 2, 4, 8, 128), F32),
            vmem((ITERS, 2, 4, 2, 8, 128), F32),
            vmem((ITERS, 2, 4, 2, 8, 128), F32),
            vmem((3, 12, 2, 8, 128), F32),
            dma((10,)),
            dma((9,)),
            dma((3,)),
            dma((6,)),
            dma((4,)),
            dma((slots,)),
            dma((slots,)),
            dma((slots,)),
            dma((slots,)),
            dma((ITERS, 9)),
            dma((ITERS, 5)),
        ],
        compiler_params=pltpu.CompilerParams(
            collective_id=0, has_side_effects=True, vmem_limit_bytes=40 * 1024 * 1024
        ),
    )(*[pltpu.with_memory_space_constraint(a, pltpu.HBM) for a in [links.reshape(4, 18, 2, 8, 128)] + constants])
    result = pl.pallas_call(
        closing_kernel,
        out_shape=jax.ShapeDtypeStruct((4, 18, 2, 8, 128), F32),
        in_specs=[pl.BlockSpec(memory_space=vmem)] * 3,
        out_specs=anywhere,
        scratch_shapes=[vmem((18, 2, 8, 128), F32), dma((8,))],
        compiler_params=pltpu.CompilerParams(vmem_limit_bytes=40 * 1024 * 1024),
    )(*parts)
    return result.reshape(links.shape)


def solution(mesh):
    return jax.shard_map(
        shards,
        mesh=mesh,
        in_specs=(P(None, None, "gz", "ta", None),),
        out_specs=P(None, None, "gz", "ta", None),
        check_vma=False,
    )
```

```python
import functools
import math

import jax
import jax.numpy as jnp
import numpy as np
from jax import lax
from jax.experimental import pallas as pl
from jax.experimental.pallas import tpu as pltpu
from jax.sharding import PartitionSpec as P

ITERS = 2
STEP_SIZE = 0.08
LINE = 32
GZ = 16
TA = 32
PAIRS = ((0, 1), (0, 2), (1, 2))
LOGICAL = pl.DeviceIdType.LOGICAL
F32 = jnp.float32
BF16 = jnp.bfloat16


def halves(table):
    high = table.astype(jnp.bfloat16)
    return high, (table - high.astype(np.float64)).astype(jnp.bfloat16)


def tables():
    phase = 2.0 * np.pi * (np.outer(np.arange(LINE), np.arange(LINE)) % LINE) / LINE
    plane = np.kron(np.eye(4), (np.cos(phase) + np.sin(phase)) / np.sqrt(LINE))
    sines = 4.0 * np.sin(np.pi * np.arange(LINE) / LINE) ** 2
    row = np.arange(128)
    momenta = sines[row // 8 + 16 * (row % 2)][:, None] + np.tile(sines, 4)[None, :]
    tiles = np.broadcast_to(sines[:, None, None], (LINE, 8, 128))
    return (
        np.concatenate(halves(plane), axis=0),
        momenta.reshape(16, 8, 128).astype(np.float32),
        np.ascontiguousarray(tiles).astype(np.float32),
    )


def times(u, v):
    return (u[0] * v[0] - u[1] * v[1], u[0] * v[1] + u[1] * v[0])


def times_conj(u, v):
    return (u[0] * v[0] + u[1] * v[1], u[1] * v[0] - u[0] * v[1])


def plus(u, v):
    return (u[0] + v[0], u[1] + v[1])


def minus(u, v):
    return (u[0] - v[0], u[1] - v[1])


def conj(u):
    return (u[0], -u[1])


def scaled(u, factor):
    return (u[0] * factor, u[1] * factor)


def total(terms):
    return functools.reduce(plus, terms)


def product(left, right):
    return [[total([times(left[a][j], right[j][b]) for j in range(3)]) for b in range(3)] for a in range(len(left))]


def product_dagger(left, right):
    return [[total([times_conj(left[a][j], right[b][j]) for j in range(3)]) for b in range(3)] for a in range(len(left))]


def cross_conj(u, v):
    row = []
    for c in range(3):
        n, m = (c + 1) % 3, (c + 2) % 3
        row.append(conj(minus(times(u[n], v[m]), times(u[m], v[n]))))
    return row


def each(function, matrix):
    return [[(function(e[0]), function(e[1])) for e in row] for row in matrix]


def lanes(v):
    return lax.broadcasted_iota(jnp.int32, v.shape, v.ndim - 1)


def roll(v, shift, axis):
    return pltpu.roll(v, shift, axis)


def behind_x(v):
    moved = roll(v, 32, v.ndim - 1)
    return jnp.where(lanes(v) < 32, roll(moved, 1, v.ndim - 2), moved)


def ahead_x(v):
    moved = roll(v, 96, v.ndim - 1)
    return jnp.where(lanes(v) >= 96, roll(moved, 7, v.ndim - 2), moved)


def behind_y(v):
    return jnp.where(lanes(v) % 32 == 0, roll(v, 97, v.ndim - 1), roll(v, 1, v.ndim - 1))


def ahead_y(v):
    return jnp.where(lanes(v) % 32 == 31, roll(v, 31, v.ndim - 1), roll(v, 127, v.ndim - 1))


def behind_z(v, edge):
    return jnp.concatenate([edge[None], v[:1]], axis=0)


def ahead_z(v, edge):
    return jnp.concatenate([v[1:], edge[None]], axis=0)


def projected(u):
    third = (u[0][0][1] + u[1][1][1] + u[2][2][1]) * (1.0 / 3.0)
    return (
        [u[a][b][0] - u[b][a][0] for a, b in PAIRS]
        + [u[a][b][1] + u[b][a][1] for a, b in PAIRS]
        + [u[0][0][1] - third, u[1][1][1] - third]
    )


def block_transpose(planes):
    lane = lanes(planes[0])
    axis = planes[0].ndim - 1
    low = lane < 64
    even = (lane // 32) % 2 == 0
    first = [jnp.where(low, planes[p], roll(planes[p + 2], 64, axis)) for p in range(2)]
    second = [jnp.where(low, roll(planes[p], 64, axis), planes[p + 2]) for p in range(2)]
    out = []
    for one, two in (first, second):
        out.append(jnp.where(even, one, roll(two, 32, axis)))
        out.append(jnp.where(even, roll(one, 96, axis), two))
    return out


def rows_of(v):
    return lax.broadcasted_iota(jnp.int32, v.shape, v.ndim - 2)


def bit_exchange(one, two, stride):
    clear = lax.rem(lax.div(rows_of(one), stride), 2) == 0
    return (
        jnp.where(clear, one, roll(two, stride, one.ndim - 2)),
        jnp.where(clear, roll(one, 8 - stride, one.ndim - 2), two),
    )


def middle_exchange(v):
    pair = lax.div(rows_of(v), 2)
    return jnp.where(pair == 1, roll(v, 6, 0), jnp.where(pair == 2, roll(v, 2, 0), v))


def hartley(v):
    size = len(v)
    if size == 1:
        return v
    even, odd = hartley(v[0::2]), hartley(v[1::2])
    half = size // 2
    out = [None] * size
    for k in range(half):
        turned = odd[k]
        if k and 4 * k != size:
            angle = 2.0 * math.pi * k / size
            turned = odd[k] * math.cos(angle) + odd[half - k] * math.sin(angle)
        out[k], out[k + half] = even[k] + turned, even[k] - turned
    return out


def bit_clear(v, stride):
    return lax.rem(lax.div(rows_of(v), stride), 2) == 0


def rotated(v, stride):
    low = bit_clear(v[0], stride)
    out = list(v)
    for k in range(1, 16):
        if k != 8:
            angle = math.pi * k / 16
            out[k] = v[k] * jnp.where(low, 1.0, math.cos(angle)) + v[16 - k] * jnp.where(low, 0.0, math.sin(angle))
    return out


def butterflies(v, stride):
    low = bit_clear(v[0], stride)
    out = []
    for e in v:
        other = roll(e, stride, 0)
        if stride != 4:
            other = jnp.where(low, roll(e, 8 - stride, 0), other)
        out.append(other + jnp.where(low, e, -e))
    return out


def fine_to_coarse(v, stride):
    return butterflies(rotated(hartley(v), stride), stride)


def coarse_to_fine(v, stride):
    return hartley(rotated(butterflies(v, stride), stride))


def tiles_of(matrix):
    return [matrix[8 * i : 8 * i + 8] for i in range(16)]


def plane_forward(fields, table):
    parts = [block_transpose(fields[tl]) for tl in range(2)]
    tiles = [None] * 16
    for b in range(4):
        traded = [bit_exchange(parts[tl][b][0], parts[tl][b][1], 2) for tl in range(2)]
        for bit in range(2):
            tiles[8 * bit + b], tiles[8 * bit + 4 + b] = bit_exchange(traded[0][bit], traded[1][bit], 1)
    tiles = [middle_exchange(v) for v in coarse_to_fine(tiles, 4)]
    return tiles if table is None else right(jnp.concatenate(tiles, axis=0), table)


def plane_inverse(matrix, table):
    tiles = fine_to_coarse([middle_exchange(v) for v in tiles_of(right(matrix, table))], 4)
    blocks = [[None] * 4 for _ in range(2)]
    for b in range(4):
        pairs = [bit_exchange(tiles[8 * bit + b], tiles[8 * bit + 4 + b], 1) for bit in range(2)]
        for tl in range(2):
            blocks[tl][b] = jnp.stack(bit_exchange(pairs[0][tl], pairs[1][tl], 2))
    return [block_transpose(blocks[tl]) for tl in range(2)]


def split(v):
    high = v.astype(BF16)
    return high, (v - high.astype(F32)).astype(BF16)


def right(v, table):
    table_high, table_low = table[pl.ds(0, 128)], table[pl.ds(128, 128)]
    high, low = split(v)
    return jnp.dot(
        jnp.concatenate([high, low, high], axis=1),
        jnp.concatenate([table_high, table_high, table_low], axis=0),
        preferred_element_type=F32,
    )


def store_tiles(ref, tiles):
    for i, tile in enumerate(tiles):
        ref[pl.ds(8 * i, 8)] = tile


def load_tiles(ref):
    return [ref[pl.ds(8 * i, 8)] for i in range(16)]


def inverse_momenta(momenta, tiles):
    row = lax.broadcasted_iota(jnp.int32, (8, 128), 0)
    own = jnp.where(row < 4, tiles[0], tiles[1]) + jnp.where(lax.rem(lax.div(row, 2), 2) == 0, tiles[2], tiles[3])
    squares = momenta + own[None]
    positive = squares > 0.001
    return jnp.where(positive, (16.0 * STEP_SIZE / LINE**3) / jnp.where(positive, squares, 1.0), 0.0).reshape(128, 128)


def normalized(row):
    norm = functools.reduce(jnp.add, [e[0] * e[0] + e[1] * e[1] for e in row])
    scale = lax.rsqrt(norm)
    return [scaled(e, scale) for e in row]


def gauge_rows(fields):
    a, b, c = [(fields[i], fields[3 + i]) for i in range(3)]
    h0, h1 = fields[6], fields[7]
    h2 = -(h0 + h1)
    aa, bb, cc = [e[0] * e[0] + e[1] * e[1] for e in (a, b, c)]
    sixth = 1.0 / 6.0

    def turned(u, h):
        return (-(u[1] * h), u[0] * h)

    s01 = minus(turned(a, -h2), times_conj(b, c))
    s02 = plus(turned(b, -h1), times(a, c))
    s12 = minus(turned(c, -h0), times_conj(b, a))
    d0 = 1.0 - (h0 * h0 + aa + bb) * sixth
    d1 = 1.0 - (h1 * h1 + aa + cc) * sixth
    d2 = 1.0 - (h2 * h2 + bb + cc) * sixth

    def upper(u, s):
        return (0.5 * u[0] + s[0] * sixth, 0.5 * u[1] + s[1] * sixth)

    def lower(u, s):
        return (s[0] * sixth - 0.5 * u[0], 0.5 * u[1] - s[1] * sixth)

    inner = [
        [(d0, 0.5 * h0), upper(a, s01), upper(b, s02)],
        [lower(a, s01), (d1, 0.5 * h1), upper(c, s12)],
        [lower(b, s02), lower(c, s12), (d2, 0.5 * h2)],
    ]
    minus_a = (-a[0], a[1])
    p0 = [total([turned(inner[0][j], h0), times(a, inner[1][j]), times(b, inner[2][j])]) for j in range(3)]
    p1 = [total([times(minus_a, inner[0][j]), turned(inner[1][j], h1), times(c, inner[2][j])]) for j in range(3)]
    p0[0] = (p0[0][0] + 1.0, p0[0][1])
    p1[1] = (p1[1][0] + 1.0, p1[1][1])
    row0 = normalized(p0)
    overlap = total([times_conj(p1[j], row0[j]) for j in range(3)])
    row1 = normalized([minus(p1[j], times(overlap, row0[j])) for j in range(3)])
    return [row0, row1]


def completed(rows):
    return rows + [cross_conj(rows[0], rows[1])]


def load_matrix(ref):
    return [[(ref[2 * (3 * a + b)], ref[2 * (3 * a + b) + 1]) for b in range(3)] for a in range(3)]


def store_matrix(ref, matrix):
    for a, row in enumerate(matrix):
        for b, entry in enumerate(row):
            ref[2 * (3 * a + b)] = entry[0]
            ref[2 * (3 * a + b) + 1] = entry[1]


def load_rows(ref):
    return [[(ref[2 * (3 * a + b)], ref[2 * (3 * a + b) + 1]) for b in range(3)] for a in range(2)]


def kernel(
    links, table_hbm, momenta_hbm, sines_hbm, out, factor_t, follow_t,
    u, edge_z, edge_t, sum_send, sums, line_t_send, line_t, line_z_send, line_z, table, momenta, sines, weights,
    plane_send, plane_recv, ring_send, ring_recv, smooth, smooth_za, smooth_zb, smooth_ta, smooth_tb, gauge,
    load_sems, edge_ss, edge_rs, first_ss, first_rs, plane_ss, plane_rs, ring_ss, ring_rs, halo_ss, halo_rs,
):
    gz = lax.axis_index("gz")
    ta = lax.axis_index("ta")
    gz_x, gz_y = lax.div(gz, 4), lax.rem(gz, 4)
    chip, core = lax.div(ta, 2), lax.rem(ta, 2)
    other_core = 1 - core

    def device(z, t_chip, which):
        return z * TA + 2 * t_chip + which

    sibling = device(gz, chip, other_core)
    z_next, z_last = lax.rem(gz + 1, GZ), lax.rem(gz + GZ - 1, GZ)
    t_next, t_last = lax.rem(chip + 1, GZ), lax.rem(chip + GZ - 1, GZ)

    def around(place, step, size):
        return lax.rem(place + step, size)

    offsets = [(dx, dy) for dx in range(4) for dy in range(4) if dx or dy]
    offsets.sort(key=lambda o: -(min(o[0], 4 - o[0]) + min(o[1], 4 - o[1])))
    sign = 1 - 2 * core
    columns = [around(gz_x + 4, dx * sign, 4) for dx in range(4)]
    lines_y = [around(gz_y + 4, dy * sign, 4) for dy in range(4)]
    plane_partners = [(i, device(i, chip, core)) for i in [columns[dx] * 4 + lines_y[dy] for dx, dy in offsets]]
    steps = sorted(range(1, 16), key=lambda d: -min(d, 16 - d))
    ring_partners = [(i, device(gz, i, core)) for i in [around(chip + 16, d * sign, 16) for d in steps]]
    crossed = [
        device(gz, t_last, other_core),
        device(gz, t_next, other_core),
        device(z_last, chip, other_core),
        device(z_next, chip, other_core),
    ]

    barrier = pltpu.get_barrier_semaphore()

    def greet(target):
        pl.semaphore_signal(barrier, inc=1, device_id=target, device_id_type=LOGICAL)

    loads = [pltpu.make_async_copy(links.at[mu], u.at[core, mu], load_sems.at[mu]) for mu in range(4)]
    constants = [
        pltpu.make_async_copy(momenta_hbm, momenta, load_sems.at[4]),
        pltpu.make_async_copy(sines_hbm.at[chip], sines.at[0], load_sems.at[5]),
        pltpu.make_async_copy(sines_hbm.at[chip + 16], sines.at[1], load_sems.at[6]),
        pltpu.make_async_copy(sines_hbm.at[2 * gz], sines.at[2], load_sems.at[7]),
        pltpu.make_async_copy(sines_hbm.at[2 * gz + 1], sines.at[3], load_sems.at[8]),
        pltpu.make_async_copy(table_hbm, table, load_sems.at[9]),
    ]
    for copy in loads[::-1] + constants[-1:]:
        copy.start()
    for _, target in ring_partners + plane_partners:
        greet(target)
    for target in crossed + [sibling]:
        greet(target)
    for copy in constants[:-1]:
        copy.start()

    def transfer(src, dst, send_sem, recv_sem, target):
        return pltpu.make_async_remote_copy(
            src_ref=src, dst_ref=dst, send_sem=send_sem, recv_sem=recv_sem, device_id=target, device_id_type=LOGICAL
        )

    def exchange(sends, recvs, ss, rs, slot, partners, me, neighbour):
        send, recv = sends.at[slot], recvs.at[slot]
        own = pl.ds(pl.multiple_of(me * 8, 8), 8)

        for index, target in partners:
            theirs = pl.ds(pl.multiple_of(index * 8, 8), 8)
            transfer(send.at[theirs], recv.at[own], ss.at[slot], rs.at[slot], target).start()
        recv[own] = send[own]
        part = pl.ds(0, 120)
        return transfer(send.at[part], recv.at[part], ss.at[slot], rs.at[slot], neighbour)

    def plane_exchange(slot):
        neighbour = device(z_next, chip, core)
        return exchange(plane_send, plane_recv, plane_ss, plane_rs, slot, plane_partners, gz, neighbour)

    def ring_exchange(slot):
        neighbour = device(gz, t_next, core)
        return exchange(ring_send, ring_recv, ring_ss, ring_rs, slot, ring_partners, chip, neighbour)

    def halo_transfers(it):
        mine = smooth.at[it, core]
        ss, rs = halo_ss, halo_rs
        to_sibling = transfer(mine, mine, ss.at[it, 0], rs.at[it, 0], sibling)
        groups = []
        for which, (src, dst, z, t_chip) in enumerate(
            (
                (mine.at[0], smooth_ta.at[it, core], gz, t_last),
                (mine.at[:, :, 0], smooth_za.at[it, core], z_last, chip),
                (mine.at[1], smooth_tb.at[it, core], gz, t_next),
                (mine.at[:, :, 1], smooth_zb.at[it, core], z_next, chip),
            )
        ):
            groups.append(
                [
                    transfer(src, dst, ss.at[it, 1 + 2 * which + h], rs.at[it, 1 + which], device(z, t_chip, h))
                    for h in range(2)
                ]
            )
        if it == ITERS - 1:
            groups[1] = [
                transfer(
                    mine.at[h, :, 0], smooth_za.at[it, core, h], ss.at[it, 3 + h], rs.at[it, 2],
                    device(z_last, chip, h),
                )
                for h in range(2)
            ]
        return to_sibling, groups

    def arrived(it, which, ref):
        transfer(ref.at[it], ref.at[it], halo_ss.at[it, 0], halo_rs.at[it, 1 + which], sibling).wait_recv()

    lane_core = lax.broadcasted_iota(jnp.int32, (8, 128), 0) * 0 + core
    first_half = lane_core == 0

    def own_half(fields):
        return [jnp.where(jnp.broadcast_to(first_half, one.shape), one, two) for one, two in zip(fields[:4], fields[4:])]

    for copy in loads:
        copy.wait()
    lines = [projected(load_matrix(u.at[core, mu])) for mu in range(4)]
    planes = []
    for f in range(8):
        x, y, z, t = [lines[mu][f] for mu in range(4)]
        inner = jnp.concatenate([jnp.zeros((1, 8, 128), F32), z[:1]], axis=0)
        total_here = ((behind_x(x) - x) + (behind_y(y) - y)) + (inner - (z + t))
        planes += [total_here[0], total_here[1], t[0], t[1], z[1]]
    constants[-1].wait()
    planes = right(jnp.concatenate(planes, axis=0), table)
    for f in range(8):
        five = [planes[40 * f + 8 * i : 40 * f + 8 * i + 8] for i in range(5)]
        for z in range(2):
            sum_send[f // 4, f % 4, z] = five[z]
            line_t_send[f // 4, f % 4, z] = five[2 + z]
        line_z_send[f // 4, f % 4] = five[4]
    sums[core] = sum_send[core]

    @pl.when(core == 0)
    def _():
        line_t[1] = line_t_send[0]

    pl.semaphore_wait(barrier, 35)
    sum_out = transfer(sum_send.at[other_core], sums.at[core], first_ss.at[0], first_rs.at[0], sibling)
    sum_in = transfer(sums.at[other_core], sums.at[other_core], first_ss.at[0], first_rs.at[0], sibling)
    t_inner = transfer(line_t_send.at[1], line_t.at[1], first_ss.at[1], first_rs.at[1], sibling)
    t_outer = [
        transfer(line_t_send.at[h], line_t.at[0], first_ss.at[2 + h], first_rs.at[2], device(gz, t_next, h))
        for h in range(2)
    ]
    z_outer = [
        transfer(line_z_send.at[h], line_z.at[core], first_ss.at[4 + h], first_rs.at[3], device(z_next, chip, h))
        for h in range(2)
    ]

    z_outer[0].start()

    @pl.when(core == 1)
    def _():
        for copy in t_outer:
            copy.start()

    z_outer[1].start()
    sum_out.start()

    @pl.when(core == 0)
    def _():
        t_inner.start()

    for copy in constants[:-1]:
        copy.wait()
    weights[...] = inverse_momenta(momenta[...], [sines[i] for i in range(4)])
    sum_in.wait_recv()

    @pl.when(core == 1)
    def _():
        t_inner.wait_recv()

    transfer(line_z, line_z, first_ss.at[4], first_rs.at[3], sibling).wait_recv()
    t_outer[0].wait_recv()
    fields = []
    for tl in range(2):
        fields.append([])
        for f in range(4):
            value = sums[tl, f] + line_t[tl, f]
            edge = jnp.stack([line_z[tl, f], jnp.zeros((8, 128), F32)])
            value = value + edge
            factor = 0.5 if f < 2 else jnp.where(jnp.broadcast_to(first_half, value.shape), 0.5, 1.0)
            fields[tl].append(value * factor)
    store_tiles(plane_send.at[0], plane_forward(fields, None))

    to_sibling = [
        transfer(
            links.at[mu, pl.ds(0, 12)], u.at[core, mu, pl.ds(0, 12)], edge_ss.at[5 + mu], edge_rs.at[0], sibling
        )
        for mu in range(4)
    ]
    from_sibling = transfer(
        u.at[other_core, :, pl.ds(0, 12)], u.at[other_core, :, pl.ds(0, 12)], edge_ss.at[0], edge_rs.at[0], sibling
    )
    t_edges = [
        transfer(
            links.at[3, pl.ds(0, 12)], edge_t.at[pl.ds(0, 12)], edge_ss.at[1 + h], edge_rs.at[1], device(gz, t_next, h)
        )
        for h in range(2)
    ]
    z_edges = [
        transfer(
            links.at[2, pl.ds(0, 12), 1], edge_z.at[core, pl.ds(0, 12)], edge_ss.at[3 + h], edge_rs.at[2],
            device(z_next, chip, h),
        )
        for h in range(2)
    ]

    def everything_left():
        sum_out.wait_send()
        for copy in z_outer + z_edges + to_sibling:
            copy.wait_send()

        @pl.when(core == 0)
        def _():
            t_inner.wait_send()

        @pl.when(core == 1)
        def _():
            for copy in t_outer + t_edges:
                copy.wait_send()

        for slot in range(2 * ITERS):
            for send, ss, rs in ((plane_send, plane_ss, plane_rs), (ring_send, ring_ss, ring_rs)):
                part = send.at[slot, pl.ds(0, 120)]
                transfer(part, part, ss.at[slot], rs.at[slot], sibling).wait_send()
        for it in range(ITERS - 1):
            to_other, groups = halo_transfers(it)
            for copy in [to_other] + [copy for group in groups for copy in group]:
                copy.wait_send()

    def beside(it, which):
        if it == 0:
            to_sibling[which].start()
            if which in (1, 2):
                z_edges[which - 1].start()
            else:

                @pl.when(core == 1)
                def _():
                    t_edges[which // 3].start()

    for it in range(ITERS):
        last = it == ITERS - 1
        copy = plane_exchange(2 * it)
        beside(it, 0)
        copy.wait_recv()
        store_tiles(ring_send.at[2 * it], fine_to_coarse(load_tiles(plane_recv.at[2 * it]), 4))
        copy = ring_exchange(2 * it)
        beside(it, 1)
        copy.wait_recv()
        tiles = fine_to_coarse(load_tiles(ring_recv.at[2 * it]), 1)
        tiles = [v * w for v, w in zip(tiles, load_tiles(weights))]
        store_tiles(ring_send.at[2 * it + 1], coarse_to_fine(tiles, 1))
        copy = ring_exchange(2 * it + 1)
        beside(it, 2)
        copy.wait_recv()
        store_tiles(plane_send.at[2 * it + 1], coarse_to_fine(load_tiles(ring_recv.at[2 * it + 1]), 4))
        copy = plane_exchange(2 * it + 1)
        beside(it, 3)
        copy.wait_recv()
        fields = plane_inverse(plane_recv[2 * it + 1], table)
        for tl in range(2):
            for f in range(4):
                smooth[it, core, tl, f] = fields[tl][f]
        to_other, (ahead_t, ahead_z_, after_t, after_z) = halo_transfers(it)
        for which in range(2):
            if last:
                order = [ahead_z_[which], ahead_t[1], ahead_z_[1 - which], to_other]
            else:
                links_round = [ahead_z_, ahead_t, after_z, after_t]
                links_round = links_round[2 * which :] + links_round[: 2 * which]
                order = [group[0] for group in links_round] + [to_other] + [group[1] for group in links_round]

            @pl.when(core == which)
            def _():
                for copy in order:
                    copy.start()

        theirs = smooth.at[it, other_core]
        transfer(theirs, theirs, halo_ss.at[it, 0], halo_rs.at[it, 0], sibling).wait_recv()

        def keep(slot, rows):
            store_matrix(gauge.at[slot], rows)

        for tl in range(2):
            keep(tl, gauge_rows([smooth[it, f // 4, tl, f % 4] for f in range(8)]))

        def turned_inside(where, target):
            rows = load_rows(gauge.at[where])
            own = completed(rows)
            for mu, shift in ((0, ahead_x), (1, ahead_y)):
                turned = product_dagger(product(rows, load_matrix(u.at[where, mu])), each(shift, own))
                store_matrix(target.at[mu], completed(turned))
            for mu in (2, 3):
                left = factor_t if last and mu == 3 else u.at[where, mu]
                store_matrix(left, product(rows, load_matrix(u.at[where, mu])))

        def turned_z(where, target, plane, following):
            rows = product_dagger(load_rows(u.at[where, 2, :, plane]), completed(following))
            store_matrix(target.at[2, :, plane], completed(rows))

        def turned_t(where, target, following):
            rows = product_dagger(load_rows(u.at[where, 3]), completed(load_rows(gauge.at[following])))
            store_matrix(target.at[3], completed(rows))

        def edge_gauges(ref, tl):
            return [[tuple(v[tl] for v in e) for e in row] for row in ref]

        if last:
            turned_inside(core, out)
            turned_z(core, out, 0, load_rows(gauge.at[core, :, 1]))
            everything_left()
            part = smooth_za.at[it, :, core]
            transfer(part, part, halo_ss.at[it, 0], halo_rs.at[it, 2], sibling).wait_recv()
            turned_z(core, out, 1, gauge_rows([smooth_za[it, f // 4, core, f % 4] for f in range(8)]))

            @pl.when(core == 0)
            def _():
                follow_t[...] = gauge[1]

            @pl.when(core == 1)
            def _():
                arrived(it, 0, smooth_ta)
                store_matrix(follow_t, gauge_rows([smooth_ta[it, f // 4, f % 4] for f in range(8)]))
        else:
            from_sibling.wait_recv()
            transfer(
                edge_z.at[:, pl.ds(0, 12)], edge_z.at[:, pl.ds(0, 12)], edge_ss.at[0], edge_rs.at[2], sibling
            ).wait_recv()
            t_edges[0].wait_recv()
            missing = [completed(load_rows(u.at[other_core, mu])) for mu in range(4)]
            for mu in range(4):
                store_matrix(u.at[other_core, mu], missing[mu])
            for tl in range(2):
                turned_inside(tl, u.at[tl])
            here = [completed(load_rows(gauge.at[tl])) for tl in range(2)]
            store_matrix(edge_t, product_dagger(completed(load_rows(edge_t)), here[0]))
            for tl in range(2):
                edge = product_dagger(completed(load_rows(edge_z.at[tl])), each(lambda v: v[0], here[tl]))
                store_matrix(edge_z.at[tl], edge)
            turned_t(0, u.at[0], 1)
            for tl in range(2):
                turned_z(tl, u.at[tl], 0, load_rows(gauge.at[tl, :, 1]))
            even_t = own_half(projected(load_matrix(u.at[0, 3])))
            for tl in range(2):
                x, y = [own_half(projected(load_matrix(u.at[tl, mu]))) for mu in range(2)]
                z = own_half(projected(load_matrix(u.at[tl, 2, :, 0])))
                for f in range(4):
                    value = ((behind_x(x[f]) - x[f]) + (behind_y(y[f]) - y[f])) + jnp.stack([-z[f], z[f]])
                    sums[tl, f] = value + even_t[f] if tl else value - even_t[f]
            arrived(it, 1, smooth_za)
            edges = gauge_rows([smooth_za[it, f // 4, :, f % 4] for f in range(8)])
            for tl in range(2):
                turned_z(tl, u.at[tl], 1, edge_gauges(edges, tl))
            arrived(it, 3, smooth_zb)
            edges = gauge_rows([smooth_zb[it, f // 4, :, f % 4] for f in range(8)])
            z_edge = [
                own_half(projected(completed(product(edge_gauges(edges, tl), load_matrix(edge_z.at[tl])))))
                for tl in range(2)
            ]
            z_last_plane = [own_half(projected(load_matrix(u.at[tl, 2, :, 1]))) for tl in range(2)]
            arrived(it, 0, smooth_ta)
            keep(2, gauge_rows([smooth_ta[it, f // 4, f % 4] for f in range(8)]))
            turned_t(1, u.at[1], 2)
            odd_t = own_half(projected(load_matrix(u.at[1, 3])))
            arrived(it, 2, smooth_tb)
            edges = gauge_rows([smooth_tb[it, f // 4, f % 4] for f in range(8)])
            t_edge = own_half(projected(completed(product(edges, load_matrix(edge_t)))))
            fields = []
            for tl in range(2):
                fields.append([])
                for f in range(4):
                    value = sums[tl, f] + jnp.stack([z_edge[tl][f], -z_last_plane[tl][f]])
                    value = value - odd_t[f] if tl else value + t_edge[f]
                    factor = 0.5 if f < 2 else jnp.where(jnp.broadcast_to(first_half, value.shape), 0.5, 1.0)
                    fields[tl].append(value * factor)
            plane_send[2 * it + 2] = plane_forward(fields, table)

    to_other, (ahead_t, ahead_z_, after_t, after_z) = halo_transfers(ITERS - 1)
    for copy in [to_other] + ahead_z_ + ahead_t[1:]:
        copy.wait_send()


def closing_kernel(done, factor_t, follow_t, out, last_links, sems):
    pieces = [(mu, pl.ds(9 * half, 9)) for mu in range(4) for half in range(2)]
    copies = [
        pltpu.make_async_copy((last_links if mu == 3 else done.at[mu]).at[part], out.at[mu, part], sems.at[i])
        for i, (mu, part) in enumerate(pieces)
    ]
    for copy in copies[:6]:
        copy.start()
    store_matrix(last_links, completed(product_dagger(load_rows(factor_t), completed(load_rows(follow_t)))))
    for copy in copies[6:]:
        copy.start()
    for copy in copies:
        copy.wait()


def shards(links):
    constants = [jnp.asarray(t) for t in tables()]
    anywhere = pl.BlockSpec(memory_space=pl.ANY)
    vmem = pltpu.VMEM
    dma = pltpu.SemaphoreType.DMA
    slots = 2 * ITERS
    parts = pl.pallas_call(
        kernel,
        out_shape=[vmem((3, 18, 2, 8, 128), F32), vmem((12, 2, 8, 128), F32), vmem((12, 2, 8, 128), F32)],
        in_specs=[anywhere] * 4,
        out_specs=[pl.BlockSpec(memory_space=vmem)] * 3,
        scratch_shapes=[
            vmem((2, 4, 18, 2, 8, 128), F32),
            vmem((2, 18, 8, 128), F32),
            vmem((18, 2, 8, 128), F32),
            vmem((2, 4, 2, 8, 128), F32),
            vmem((2, 4, 2, 8, 128), F32),
            vmem((2, 4, 2, 8, 128), F32),
            vmem((2, 4, 2, 8, 128), F32),
            vmem((2, 4, 8, 128), F32),
            vmem((2, 4, 8, 128), F32),
            vmem((256, 128), BF16),
            vmem((16, 8, 128), F32),
            vmem((4, 8, 128), F32),
            vmem((128, 128), F32),
            vmem((slots, 128, 128), F32),
            vmem((slots, 128, 128), F32),
            vmem((slots, 128, 128), F32),
            vmem((slots, 128, 128), F32),
            vmem((ITERS, 2, 2, 4, 2, 8, 128), F32),
            vmem((ITERS, 2, 2, 4, 8, 128), F32),
            vmem((ITERS, 2, 2, 4, 8, 128), F32),
            vmem((ITERS, 2, 4, 2, 8, 128), F32),
            vmem((ITERS, 2, 4, 2, 8, 128), F32),
            vmem((3, 12, 2, 8, 128), F32),
            dma((10,)),
            dma((9,)),
            dma((3,)),
            dma((6,)),
            dma((4,)),
            dma((slots,)),
            dma((slots,)),
            dma((slots,)),
            dma((slots,)),
            dma((ITERS, 9)),
            dma((ITERS, 5)),
        ],
        compiler_params=pltpu.CompilerParams(
            collective_id=0, has_side_effects=True, vmem_limit_bytes=40 * 1024 * 1024
        ),
    )(*[pltpu.with_memory_space_constraint(a, pltpu.HBM) for a in [links.reshape(4, 18, 2, 8, 128)] + constants])
    result = pl.pallas_call(
        closing_kernel,
        out_shape=jax.ShapeDtypeStruct((4, 18, 2, 8, 128), F32),
        in_specs=[pl.BlockSpec(memory_space=vmem)] * 3,
        out_specs=anywhere,
        scratch_shapes=[vmem((18, 2, 8, 128), F32), dma((8,))],
        compiler_params=pltpu.CompilerParams(vmem_limit_bytes=40 * 1024 * 1024),
    )(*parts)
    return result.reshape(links.shape)


def solution(mesh):
    return jax.shard_map(
        shards,
        mesh=mesh,
        in_specs=(P(None, None, "gz", "ta", None),),
        out_specs=P(None, None, "gz", "ta", None),
        check_vma=False,
    )
```

```python
import functools
import math

import jax
import jax.numpy as jnp
import numpy as np
from jax import lax
from jax.experimental import pallas as pl
from jax.experimental.pallas import tpu as pltpu
from jax.sharding import PartitionSpec as P

ITERS = 2
STEP_SIZE = 0.08
LINE = 32
GZ = 16
TA = 32
PAIRS = ((0, 1), (0, 2), (1, 2))
LOGICAL = pl.DeviceIdType.LOGICAL
F32 = jnp.float32
BF16 = jnp.bfloat16


def halves(table):
    high = table.astype(jnp.bfloat16)
    return high, (table - high.astype(np.float64)).astype(jnp.bfloat16)


def tables():
    phase = 2.0 * np.pi * (np.outer(np.arange(LINE), np.arange(LINE)) % LINE) / LINE
    plane = np.kron(np.eye(4), (np.cos(phase) + np.sin(phase)) / np.sqrt(LINE))
    sines = 4.0 * np.sin(np.pi * np.arange(LINE) / LINE) ** 2
    row = np.arange(128)
    momenta = sines[row // 8 + 16 * (row % 2)][:, None] + np.tile(sines, 4)[None, :]
    tiles = np.broadcast_to(sines[:, None, None], (LINE, 8, 128))
    return (
        np.concatenate(halves(plane), axis=0),
        momenta.reshape(16, 8, 128).astype(np.float32),
        np.ascontiguousarray(tiles).astype(np.float32),
    )


def times(u, v):
    return (u[0] * v[0] - u[1] * v[1], u[0] * v[1] + u[1] * v[0])


def times_conj(u, v):
    return (u[0] * v[0] + u[1] * v[1], u[1] * v[0] - u[0] * v[1])


def plus(u, v):
    return (u[0] + v[0], u[1] + v[1])


def minus(u, v):
    return (u[0] - v[0], u[1] - v[1])


def conj(u):
    return (u[0], -u[1])


def scaled(u, factor):
    return (u[0] * factor, u[1] * factor)


def total(terms):
    return functools.reduce(plus, terms)


def product(left, right):
    return [[total([times(left[a][j], right[j][b]) for j in range(3)]) for b in range(3)] for a in range(len(left))]


def product_dagger(left, right):
    return [[total([times_conj(left[a][j], right[b][j]) for j in range(3)]) for b in range(3)] for a in range(len(left))]


def cross_conj(u, v):
    row = []
    for c in range(3):
        n, m = (c + 1) % 3, (c + 2) % 3
        row.append(conj(minus(times(u[n], v[m]), times(u[m], v[n]))))
    return row


def each(function, matrix):
    return [[(function(e[0]), function(e[1])) for e in row] for row in matrix]


def lanes(v):
    return lax.broadcasted_iota(jnp.int32, v.shape, v.ndim - 1)


def roll(v, shift, axis):
    return pltpu.roll(v, shift, axis)


def behind_x(v):
    moved = roll(v, 32, v.ndim - 1)
    return jnp.where(lanes(v) < 32, roll(moved, 1, v.ndim - 2), moved)


def ahead_x(v):
    moved = roll(v, 96, v.ndim - 1)
    return jnp.where(lanes(v) >= 96, roll(moved, 7, v.ndim - 2), moved)


def behind_y(v):
    return jnp.where(lanes(v) % 32 == 0, roll(v, 97, v.ndim - 1), roll(v, 1, v.ndim - 1))


def ahead_y(v):
    return jnp.where(lanes(v) % 32 == 31, roll(v, 31, v.ndim - 1), roll(v, 127, v.ndim - 1))


def behind_z(v, edge):
    return jnp.concatenate([edge[None], v[:1]], axis=0)


def ahead_z(v, edge):
    return jnp.concatenate([v[1:], edge[None]], axis=0)


def projected(u):
    third = (u[0][0][1] + u[1][1][1] + u[2][2][1]) * (1.0 / 3.0)
    return (
        [u[a][b][0] - u[b][a][0] for a, b in PAIRS]
        + [u[a][b][1] + u[b][a][1] for a, b in PAIRS]
        + [u[0][0][1] - third, u[1][1][1] - third]
    )


def block_transpose(planes):
    lane = lanes(planes[0])
    axis = planes[0].ndim - 1
    low = lane < 64
    even = (lane // 32) % 2 == 0
    first = [jnp.where(low, planes[p], roll(planes[p + 2], 64, axis)) for p in range(2)]
    second = [jnp.where(low, roll(planes[p], 64, axis), planes[p + 2]) for p in range(2)]
    out = []
    for one, two in (first, second):
        out.append(jnp.where(even, one, roll(two, 32, axis)))
        out.append(jnp.where(even, roll(one, 96, axis), two))
    return out


def rows_of(v):
    return lax.broadcasted_iota(jnp.int32, v.shape, v.ndim - 2)


def bit_exchange(one, two, stride):
    clear = lax.rem(lax.div(rows_of(one), stride), 2) == 0
    return (
        jnp.where(clear, one, roll(two, stride, one.ndim - 2)),
        jnp.where(clear, roll(one, 8 - stride, one.ndim - 2), two),
    )


def middle_exchange(v):
    pair = lax.div(rows_of(v), 2)
    return jnp.where(pair == 1, roll(v, 6, 0), jnp.where(pair == 2, roll(v, 2, 0), v))


def hartley(v):
    size = len(v)
    if size == 1:
        return v
    even, odd = hartley(v[0::2]), hartley(v[1::2])
    half = size // 2
    out = [None] * size
    for k in range(half):
        turned = odd[k]
        if k and 4 * k != size:
            angle = 2.0 * math.pi * k / size
            turned = odd[k] * math.cos(angle) + odd[half - k] * math.sin(angle)
        out[k], out[k + half] = even[k] + turned, even[k] - turned
    return out


def bit_clear(v, stride):
    return lax.rem(lax.div(rows_of(v), stride), 2) == 0


def rotated(v, stride):
    low = bit_clear(v[0], stride)
    out = list(v)
    for k in range(1, 16):
        if k != 8:
            angle = math.pi * k / 16
            out[k] = v[k] * jnp.where(low, 1.0, math.cos(angle)) + v[16 - k] * jnp.where(low, 0.0, math.sin(angle))
    return out


def butterflies(v, stride):
    low = bit_clear(v[0], stride)
    out = []
    for e in v:
        other = roll(e, stride, 0)
        if stride != 4:
            other = jnp.where(low, roll(e, 8 - stride, 0), other)
        out.append(other + jnp.where(low, e, -e))
    return out


def fine_to_coarse(v, stride):
    return butterflies(rotated(hartley(v), stride), stride)


def coarse_to_fine(v, stride):
    return hartley(rotated(butterflies(v, stride), stride))


def tiles_of(matrix):
    return [matrix[8 * i : 8 * i + 8] for i in range(16)]


def plane_forward(fields, table):
    parts = [block_transpose(fields[tl]) for tl in range(2)]
    tiles = [None] * 16
    for b in range(4):
        traded = [bit_exchange(parts[tl][b][0], parts[tl][b][1], 2) for tl in range(2)]
        for bit in range(2):
            tiles[8 * bit + b], tiles[8 * bit + 4 + b] = bit_exchange(traded[0][bit], traded[1][bit], 1)
    tiles = [middle_exchange(v) for v in coarse_to_fine(tiles, 4)]
    return tiles if table is None else right(jnp.concatenate(tiles, axis=0), table)


def plane_inverse(matrix, table):
    tiles = fine_to_coarse([middle_exchange(v) for v in tiles_of(right(matrix, table))], 4)
    blocks = [[None] * 4 for _ in range(2)]
    for b in range(4):
        pairs = [bit_exchange(tiles[8 * bit + b], tiles[8 * bit + 4 + b], 1) for bit in range(2)]
        for tl in range(2):
            blocks[tl][b] = jnp.stack(bit_exchange(pairs[0][tl], pairs[1][tl], 2))
    return [block_transpose(blocks[tl]) for tl in range(2)]


def split(v):
    high = v.astype(BF16)
    return high, (v - high.astype(F32)).astype(BF16)


def right(v, table):
    table_high, table_low = table[pl.ds(0, 128)], table[pl.ds(128, 128)]
    high, low = split(v)
    return jnp.dot(
        jnp.concatenate([high, low, high], axis=1),
        jnp.concatenate([table_high, table_high, table_low], axis=0),
        preferred_element_type=F32,
    )


def store_tiles(ref, tiles):
    for i, tile in enumerate(tiles):
        ref[pl.ds(8 * i, 8)] = tile


def load_tiles(ref):
    return [ref[pl.ds(8 * i, 8)] for i in range(16)]


def inverse_momenta(momenta, tiles):
    row = lax.broadcasted_iota(jnp.int32, (8, 128), 0)
    own = jnp.where(row < 4, tiles[0], tiles[1]) + jnp.where(lax.rem(lax.div(row, 2), 2) == 0, tiles[2], tiles[3])
    squares = momenta + own[None]
    positive = squares > 0.001
    return jnp.where(positive, (16.0 * STEP_SIZE / LINE**3) / jnp.where(positive, squares, 1.0), 0.0).reshape(128, 128)


def normalized(row):
    norm = functools.reduce(jnp.add, [e[0] * e[0] + e[1] * e[1] for e in row])
    scale = lax.rsqrt(norm)
    return [scaled(e, scale) for e in row]


def gauge_rows(fields):
    a, b, c = [(fields[i], fields[3 + i]) for i in range(3)]
    h0, h1 = fields[6], fields[7]
    h2 = -(h0 + h1)
    aa, bb, cc = [e[0] * e[0] + e[1] * e[1] for e in (a, b, c)]
    sixth = 1.0 / 6.0

    def turned(u, h):
        return (-(u[1] * h), u[0] * h)

    s01 = minus(turned(a, -h2), times_conj(b, c))
    s02 = plus(turned(b, -h1), times(a, c))
    s12 = minus(turned(c, -h0), times_conj(b, a))
    d0 = 1.0 - (h0 * h0 + aa + bb) * sixth
    d1 = 1.0 - (h1 * h1 + aa + cc) * sixth
    d2 = 1.0 - (h2 * h2 + bb + cc) * sixth

    def upper(u, s):
        return (0.5 * u[0] + s[0] * sixth, 0.5 * u[1] + s[1] * sixth)

    def lower(u, s):
        return (s[0] * sixth - 0.5 * u[0], 0.5 * u[1] - s[1] * sixth)

    inner = [
        [(d0, 0.5 * h0), upper(a, s01), upper(b, s02)],
        [lower(a, s01), (d1, 0.5 * h1), upper(c, s12)],
        [lower(b, s02), lower(c, s12), (d2, 0.5 * h2)],
    ]
    minus_a = (-a[0], a[1])
    p0 = [total([turned(inner[0][j], h0), times(a, inner[1][j]), times(b, inner[2][j])]) for j in range(3)]
    p1 = [total([times(minus_a, inner[0][j]), turned(inner[1][j], h1), times(c, inner[2][j])]) for j in range(3)]
    p0[0] = (p0[0][0] + 1.0, p0[0][1])
    p1[1] = (p1[1][0] + 1.0, p1[1][1])
    row0 = normalized(p0)
    overlap = total([times_conj(p1[j], row0[j]) for j in range(3)])
    row1 = normalized([minus(p1[j], times(overlap, row0[j])) for j in range(3)])
    return [row0, row1]


def completed(rows):
    return rows + [cross_conj(rows[0], rows[1])]


def load_matrix(ref):
    return [[(ref[2 * (3 * a + b)], ref[2 * (3 * a + b) + 1]) for b in range(3)] for a in range(3)]


def store_matrix(ref, matrix):
    for a, row in enumerate(matrix):
        for b, entry in enumerate(row):
            ref[2 * (3 * a + b)] = entry[0]
            ref[2 * (3 * a + b) + 1] = entry[1]


def load_rows(ref):
    return [[(ref[2 * (3 * a + b)], ref[2 * (3 * a + b) + 1]) for b in range(3)] for a in range(2)]


def kernel(
    links, table_hbm, momenta_hbm, sines_hbm, out, factor_t, follow_t,
    u, edge_z, edge_t, sum_send, sums, line_t_send, line_t, line_z_send, line_z, table, momenta, sines, weights,
    plane_send, plane_recv, ring_send, ring_recv, smooth, smooth_za, smooth_zb, smooth_ta, smooth_tb, gauge,
    load_sems, edge_ss, edge_rs, first_ss, first_rs, plane_ss, plane_rs, ring_ss, ring_rs, halo_ss, halo_rs,
):
    gz = lax.axis_index("gz")
    ta = lax.axis_index("ta")
    gz_x, gz_y = lax.div(gz, 4), lax.rem(gz, 4)
    chip, core = lax.div(ta, 2), lax.rem(ta, 2)
    other_core = 1 - core

    def device(z, t_chip, which):
        return z * TA + 2 * t_chip + which

    sibling = device(gz, chip, other_core)
    z_next, z_last = lax.rem(gz + 1, GZ), lax.rem(gz + GZ - 1, GZ)
    t_next, t_last = lax.rem(chip + 1, GZ), lax.rem(chip + GZ - 1, GZ)

    def around(place, step, size):
        return lax.rem(place + step, size)

    offsets = [(dx, dy) for dx in range(4) for dy in range(4) if dx or dy]
    offsets.sort(key=lambda o: -(min(o[0], 4 - o[0]) + min(o[1], 4 - o[1])))
    columns = [around(gz_x, dx, 4) for dx in range(4)]
    lines_y = [around(gz_y, dy, 4) for dy in range(4)]
    plane_partners = [(i, device(i, chip, core)) for i in [columns[dx] * 4 + lines_y[dy] for dx, dy in offsets]]
    steps = sorted(range(1, 16), key=lambda d: -min(d, 16 - d))
    ring_partners = [(i, device(gz, i, core)) for i in [around(chip, d, 16) for d in steps]]
    crossed = [
        device(gz, t_last, other_core),
        device(gz, t_next, other_core),
        device(z_last, chip, other_core),
        device(z_next, chip, other_core),
    ]

    barrier = pltpu.get_barrier_semaphore()

    def greet(target):
        pl.semaphore_signal(barrier, inc=1, device_id=target, device_id_type=LOGICAL)

    loads = [pltpu.make_async_copy(links.at[mu], u.at[core, mu], load_sems.at[mu]) for mu in range(4)]
    constants = [
        pltpu.make_async_copy(momenta_hbm, momenta, load_sems.at[4]),
        pltpu.make_async_copy(sines_hbm.at[chip], sines.at[0], load_sems.at[5]),
        pltpu.make_async_copy(sines_hbm.at[chip + 16], sines.at[1], load_sems.at[6]),
        pltpu.make_async_copy(sines_hbm.at[2 * gz], sines.at[2], load_sems.at[7]),
        pltpu.make_async_copy(sines_hbm.at[2 * gz + 1], sines.at[3], load_sems.at[8]),
        pltpu.make_async_copy(table_hbm, table, load_sems.at[9]),
    ]
    for copy in loads[::-1] + constants[-1:]:
        copy.start()
    for _, target in ring_partners + plane_partners:
        greet(target)
    for target in crossed + [sibling]:
        greet(target)
    for copy in constants[:-1]:
        copy.start()

    def transfer(src, dst, send_sem, recv_sem, target):
        return pltpu.make_async_remote_copy(
            src_ref=src, dst_ref=dst, send_sem=send_sem, recv_sem=recv_sem, device_id=target, device_id_type=LOGICAL
        )

    def exchange(sends, recvs, ss, rs, slot, partners, me, neighbour):
        send, recv = sends.at[slot], recvs.at[slot]
        own = pl.ds(pl.multiple_of(me * 8, 8), 8)

        for index, target in partners:
            theirs = pl.ds(pl.multiple_of(index * 8, 8), 8)
            transfer(send.at[theirs], recv.at[own], ss.at[slot], rs.at[slot], target).start()
        recv[own] = send[own]
        part = pl.ds(0, 120)
        return transfer(send.at[part], recv.at[part], ss.at[slot], rs.at[slot], neighbour)

    def plane_exchange(slot):
        neighbour = device(z_next, chip, core)
        return exchange(plane_send, plane_recv, plane_ss, plane_rs, slot, plane_partners, gz, neighbour)

    def ring_exchange(slot):
        neighbour = device(gz, t_next, core)
        return exchange(ring_send, ring_recv, ring_ss, ring_rs, slot, ring_partners, chip, neighbour)

    def halo_transfers(it):
        mine = smooth.at[it, core]
        ss, rs = halo_ss, halo_rs
        to_sibling = transfer(mine, mine, ss.at[it, 0], rs.at[it, 0], sibling)
        groups = []
        for which, (src, dst, z, t_chip) in enumerate(
            (
                (mine.at[0], smooth_ta.at[it, core], gz, t_last),
                (mine.at[:, :, 0], smooth_za.at[it, core], z_last, chip),
                (mine.at[1], smooth_tb.at[it, core], gz, t_next),
                (mine.at[:, :, 1], smooth_zb.at[it, core], z_next, chip),
            )
        ):
            groups.append(
                [
                    transfer(src, dst, ss.at[it, 1 + 2 * which + h], rs.at[it, 1 + which], device(z, t_chip, h))
                    for h in range(2)
                ]
            )
        if it == ITERS - 1:
            groups[1] = [
                transfer(
                    mine.at[h, :, 0], smooth_za.at[it, core, h], ss.at[it, 3 + h], rs.at[it, 2],
                    device(z_last, chip, h),
                )
                for h in range(2)
            ]
        return to_sibling, groups

    def arrived(it, which, ref):
        transfer(ref.at[it], ref.at[it], halo_ss.at[it, 0], halo_rs.at[it, 1 + which], sibling).wait_recv()

    lane_core = lax.broadcasted_iota(jnp.int32, (8, 128), 0) * 0 + core
    first_half = lane_core == 0

    def own_half(fields):
        return [jnp.where(jnp.broadcast_to(first_half, one.shape), one, two) for one, two in zip(fields[:4], fields[4:])]

    for copy in loads:
        copy.wait()
    lines = [projected(load_matrix(u.at[core, mu])) for mu in range(4)]
    planes = []
    for f in range(8):
        x, y, z, t = [lines[mu][f] for mu in range(4)]
        inner = jnp.concatenate([jnp.zeros((1, 8, 128), F32), z[:1]], axis=0)
        total_here = ((behind_x(x) - x) + (behind_y(y) - y)) + (inner - (z + t))
        planes += [total_here[0], total_here[1], t[0], t[1], z[1]]
    constants[-1].wait()
    planes = right(jnp.concatenate(planes, axis=0), table)
    for f in range(8):
        five = [planes[40 * f + 8 * i : 40 * f + 8 * i + 8] for i in range(5)]
        for z in range(2):
            sum_send[f // 4, f % 4, z] = five[z]
            line_t_send[f // 4, f % 4, z] = five[2 + z]
        line_z_send[f // 4, f % 4] = five[4]
    sums[core] = sum_send[core]

    @pl.when(core == 0)
    def _():
        line_t[1] = line_t_send[0]

    pl.semaphore_wait(barrier, 35)
    sum_out = transfer(sum_send.at[other_core], sums.at[core], first_ss.at[0], first_rs.at[0], sibling)
    sum_in = transfer(sums.at[other_core], sums.at[other_core], first_ss.at[0], first_rs.at[0], sibling)
    t_inner = transfer(line_t_send.at[1], line_t.at[1], first_ss.at[1], first_rs.at[1], sibling)
    t_outer = [
        transfer(line_t_send.at[h], line_t.at[0], first_ss.at[2 + h], first_rs.at[2], device(gz, t_next, h))
        for h in range(2)
    ]
    z_outer = [
        transfer(line_z_send.at[h], line_z.at[core], first_ss.at[4 + h], first_rs.at[3], device(z_next, chip, h))
        for h in range(2)
    ]

    @pl.when(core == 1)
    def _():
        for copy in t_outer:
            copy.start()

    for copy in z_outer:
        copy.start()
    sum_out.start()

    @pl.when(core == 0)
    def _():
        t_inner.start()

    for copy in constants[:-1]:
        copy.wait()
    weights[...] = inverse_momenta(momenta[...], [sines[i] for i in range(4)])
    sum_in.wait_recv()

    @pl.when(core == 1)
    def _():
        t_inner.wait_recv()

    transfer(line_z, line_z, first_ss.at[4], first_rs.at[3], sibling).wait_recv()
    t_outer[0].wait_recv()
    fields = []
    for tl in range(2):
        fields.append([])
        for f in range(4):
            value = sums[tl, f] + line_t[tl, f]
            edge = jnp.stack([line_z[tl, f], jnp.zeros((8, 128), F32)])
            value = value + edge
            factor = 0.5 if f < 2 else jnp.where(jnp.broadcast_to(first_half, value.shape), 0.5, 1.0)
            fields[tl].append(value * factor)
    store_tiles(plane_send.at[0], plane_forward(fields, None))

    to_sibling = [
        transfer(
            links.at[mu, pl.ds(0, 12)], u.at[core, mu, pl.ds(0, 12)], edge_ss.at[5 + mu], edge_rs.at[0], sibling
        )
        for mu in range(4)
    ]
    from_sibling = transfer(
        u.at[other_core, :, pl.ds(0, 12)], u.at[other_core, :, pl.ds(0, 12)], edge_ss.at[0], edge_rs.at[0], sibling
    )
    t_edges = [
        transfer(
            links.at[3, pl.ds(0, 12)], edge_t.at[pl.ds(0, 12)], edge_ss.at[1 + h], edge_rs.at[1], device(gz, t_next, h)
        )
        for h in range(2)
    ]
    z_edges = [
        transfer(
            links.at[2, pl.ds(0, 12), 1], edge_z.at[core, pl.ds(0, 12)], edge_ss.at[3 + h], edge_rs.at[2],
            device(z_next, chip, h),
        )
        for h in range(2)
    ]

    def everything_left():
        sum_out.wait_send()
        for copy in z_outer + z_edges + to_sibling:
            copy.wait_send()

        @pl.when(core == 0)
        def _():
            t_inner.wait_send()

        @pl.when(core == 1)
        def _():
            for copy in t_outer + t_edges:
                copy.wait_send()

        for slot in range(2 * ITERS):
            for send, ss, rs in ((plane_send, plane_ss, plane_rs), (ring_send, ring_ss, ring_rs)):
                part = send.at[slot, pl.ds(0, 120)]
                transfer(part, part, ss.at[slot], rs.at[slot], sibling).wait_send()
        for it in range(ITERS - 1):
            to_other, groups = halo_transfers(it)
            for copy in [to_other] + [copy for group in groups for copy in group]:
                copy.wait_send()

    def beside(it, which):
        if it == 0:
            to_sibling[which].start()
            if which in (1, 2):
                z_edges[which - 1].start()
            else:

                @pl.when(core == 1)
                def _():
                    t_edges[which // 3].start()

    for it in range(ITERS):
        last = it == ITERS - 1
        copy = plane_exchange(2 * it)
        beside(it, 0)
        copy.wait_recv()
        store_tiles(ring_send.at[2 * it], fine_to_coarse(load_tiles(plane_recv.at[2 * it]), 4))
        copy = ring_exchange(2 * it)
        beside(it, 1)
        copy.wait_recv()
        tiles = fine_to_coarse(load_tiles(ring_recv.at[2 * it]), 1)
        tiles = [v * w for v, w in zip(tiles, load_tiles(weights))]
        store_tiles(ring_send.at[2 * it + 1], coarse_to_fine(tiles, 1))
        copy = ring_exchange(2 * it + 1)
        beside(it, 2)
        copy.wait_recv()
        store_tiles(plane_send.at[2 * it + 1], coarse_to_fine(load_tiles(ring_recv.at[2 * it + 1]), 4))
        copy = plane_exchange(2 * it + 1)
        beside(it, 3)
        copy.wait_recv()
        fields = plane_inverse(plane_recv[2 * it + 1], table)
        for tl in range(2):
            for f in range(4):
                smooth[it, core, tl, f] = fields[tl][f]
        to_other, (ahead_t, ahead_z_, after_t, after_z) = halo_transfers(it)
        if last:
            order = ahead_z_ + ahead_t[1:] + [to_other]
        else:
            order = [to_other] + ahead_z_ + after_z + ahead_t + after_t
        for copy in order:
            copy.start()
        if not last:
            from_sibling.wait_recv()
            transfer(
                edge_z.at[:, pl.ds(0, 12)], edge_z.at[:, pl.ds(0, 12)], edge_ss.at[0], edge_rs.at[2], sibling
            ).wait_recv()
            t_edges[0].wait_recv()
            for ref in [u.at[other_core, mu] for mu in range(4)] + [edge_t, edge_z.at[0], edge_z.at[1]]:
                store_matrix(ref.at[pl.ds(12, 6)], [cross_conj(*load_rows(ref))])
        theirs = smooth.at[it, other_core]
        transfer(theirs, theirs, halo_ss.at[it, 0], halo_rs.at[it, 0], sibling).wait_recv()

        def keep(slot, rows):
            store_matrix(gauge.at[slot], rows)

        for tl in range(2):
            keep(tl, gauge_rows([smooth[it, f // 4, tl, f % 4] for f in range(8)]))

        def turned_inside(where, target):
            rows = load_rows(gauge.at[where])
            own = completed(rows)
            for mu, shift in ((0, ahead_x), (1, ahead_y)):
                turned = product_dagger(product(rows, load_matrix(u.at[where, mu])), each(shift, own))
                store_matrix(target.at[mu], completed(turned))
            for mu in (2, 3):
                left = factor_t if last and mu == 3 else u.at[where, mu]
                store_matrix(left, product(rows, load_matrix(u.at[where, mu])))

        def turned_z(where, target, plane, following):
            rows = product_dagger(load_rows(u.at[where, 2, :, plane]), completed(following))
            store_matrix(target.at[2, :, plane], completed(rows))

        def turned_t(where, target, following):
            rows = product_dagger(load_rows(u.at[where, 3]), completed(load_rows(gauge.at[following])))
            store_matrix(target.at[3], completed(rows))

        def edge_gauges(ref, tl):
            return [[tuple(v[tl] for v in e) for e in row] for row in ref]

        if last:
            turned_inside(core, out)
            turned_z(core, out, 0, load_rows(gauge.at[core, :, 1]))
            everything_left()
            part = smooth_za.at[it, :, core]
            transfer(part, part, halo_ss.at[it, 0], halo_rs.at[it, 2], sibling).wait_recv()
            turned_z(core, out, 1, gauge_rows([smooth_za[it, f // 4, core, f % 4] for f in range(8)]))

            @pl.when(core == 0)
            def _():
                follow_t[...] = gauge[1]

            @pl.when(core == 1)
            def _():
                arrived(it, 0, smooth_ta)
                store_matrix(follow_t, gauge_rows([smooth_ta[it, f // 4, f % 4] for f in range(8)]))
        else:
            for tl in range(2):
                turned_inside(tl, u.at[tl])
            here = [completed(load_rows(gauge.at[tl])) for tl in range(2)]
            store_matrix(edge_t, product_dagger(load_matrix(edge_t), here[0]))
            for tl in range(2):
                edge = product_dagger(load_matrix(edge_z.at[tl]), each(lambda v: v[0], here[tl]))
                store_matrix(edge_z.at[tl], edge)
            turned_t(0, u.at[0], 1)
            for tl in range(2):
                turned_z(tl, u.at[tl], 0, load_rows(gauge.at[tl, :, 1]))
            even_t = own_half(projected(load_matrix(u.at[0, 3])))
            for tl in range(2):
                x, y = [own_half(projected(load_matrix(u.at[tl, mu]))) for mu in range(2)]
                z = own_half(projected(load_matrix(u.at[tl, 2, :, 0])))
                for f in range(4):
                    value = ((behind_x(x[f]) - x[f]) + (behind_y(y[f]) - y[f])) + jnp.stack([-z[f], z[f]])
                    sums[tl, f] = value + even_t[f] if tl else value - even_t[f]
            arrived(it, 1, smooth_za)
            edges = gauge_rows([smooth_za[it, f // 4, :, f % 4] for f in range(8)])
            for tl in range(2):
                turned_z(tl, u.at[tl], 1, edge_gauges(edges, tl))
            arrived(it, 3, smooth_zb)
            edges = gauge_rows([smooth_zb[it, f // 4, :, f % 4] for f in range(8)])
            z_edge = [
                own_half(projected(completed(product(edge_gauges(edges, tl), load_matrix(edge_z.at[tl])))))
                for tl in range(2)
            ]
            z_last_plane = [own_half(projected(load_matrix(u.at[tl, 2, :, 1]))) for tl in range(2)]
            arrived(it, 0, smooth_ta)
            keep(2, gauge_rows([smooth_ta[it, f // 4, f % 4] for f in range(8)]))
            turned_t(1, u.at[1], 2)
            odd_t = own_half(projected(load_matrix(u.at[1, 3])))
            arrived(it, 2, smooth_tb)
            edges = gauge_rows([smooth_tb[it, f // 4, f % 4] for f in range(8)])
            t_edge = own_half(projected(completed(product(edges, load_matrix(edge_t)))))
            fields = []
            for tl in range(2):
                fields.append([])
                for f in range(4):
                    value = sums[tl, f] + jnp.stack([z_edge[tl][f], -z_last_plane[tl][f]])
                    value = value - odd_t[f] if tl else value + t_edge[f]
                    factor = 0.5 if f < 2 else jnp.where(jnp.broadcast_to(first_half, value.shape), 0.5, 1.0)
                    fields[tl].append(value * factor)
            plane_send[2 * it + 2] = plane_forward(fields, table)

    to_other, (ahead_t, ahead_z_, after_t, after_z) = halo_transfers(ITERS - 1)
    for copy in [to_other] + ahead_z_ + ahead_t[1:]:
        copy.wait_send()


def closing_kernel(done, factor_t, follow_t, out, last_links, sems):
    pieces = [(mu, pl.ds(9 * half, 9)) for mu in range(4) for half in range(2)]
    copies = [
        pltpu.make_async_copy((last_links if mu == 3 else done.at[mu]).at[part], out.at[mu, part], sems.at[i])
        for i, (mu, part) in enumerate(pieces)
    ]
    for copy in copies[:6]:
        copy.start()
    store_matrix(last_links, completed(product_dagger(load_rows(factor_t), completed(load_rows(follow_t)))))
    for copy in copies[6:]:
        copy.start()
    for copy in copies:
        copy.wait()


def shards(links):
    constants = [jnp.asarray(t) for t in tables()]
    anywhere = pl.BlockSpec(memory_space=pl.ANY)
    vmem = pltpu.VMEM
    dma = pltpu.SemaphoreType.DMA
    slots = 2 * ITERS
    parts = pl.pallas_call(
        kernel,
        out_shape=[vmem((3, 18, 2, 8, 128), F32), vmem((12, 2, 8, 128), F32), vmem((12, 2, 8, 128), F32)],
        in_specs=[anywhere] * 4,
        out_specs=[pl.BlockSpec(memory_space=vmem)] * 3,
        scratch_shapes=[
            vmem((2, 4, 18, 2, 8, 128), F32),
            vmem((2, 18, 8, 128), F32),
            vmem((18, 2, 8, 128), F32),
            vmem((2, 4, 2, 8, 128), F32),
            vmem((2, 4, 2, 8, 128), F32),
            vmem((2, 4, 2, 8, 128), F32),
            vmem((2, 4, 2, 8, 128), F32),
            vmem((2, 4, 8, 128), F32),
            vmem((2, 4, 8, 128), F32),
            vmem((256, 128), BF16),
            vmem((16, 8, 128), F32),
            vmem((4, 8, 128), F32),
            vmem((128, 128), F32),
            vmem((slots, 128, 128), F32),
            vmem((slots, 128, 128), F32),
            vmem((slots, 128, 128), F32),
            vmem((slots, 128, 128), F32),
            vmem((ITERS, 2, 2, 4, 2, 8, 128), F32),
            vmem((ITERS, 2, 2, 4, 8, 128), F32),
            vmem((ITERS, 2, 2, 4, 8, 128), F32),
            vmem((ITERS, 2, 4, 2, 8, 128), F32),
            vmem((ITERS, 2, 4, 2, 8, 128), F32),
            vmem((3, 12, 2, 8, 128), F32),
            dma((10,)),
            dma((9,)),
            dma((3,)),
            dma((6,)),
            dma((4,)),
            dma((slots,)),
            dma((slots,)),
            dma((slots,)),
            dma((slots,)),
            dma((ITERS, 9)),
            dma((ITERS, 5)),
        ],
        compiler_params=pltpu.CompilerParams(
            collective_id=0, has_side_effects=True, vmem_limit_bytes=40 * 1024 * 1024
        ),
    )(*[pltpu.with_memory_space_constraint(a, pltpu.HBM) for a in [links.reshape(4, 18, 2, 8, 128)] + constants])
    result = pl.pallas_call(
        closing_kernel,
        out_shape=jax.ShapeDtypeStruct((4, 18, 2, 8, 128), F32),
        in_specs=[pl.BlockSpec(memory_space=vmem)] * 3,
        out_specs=anywhere,
        scratch_shapes=[vmem((18, 2, 8, 128), F32), dma((8,))],
        compiler_params=pltpu.CompilerParams(vmem_limit_bytes=40 * 1024 * 1024),
    )(*parts)
    return result.reshape(links.shape)


def solution(mesh):
    return jax.shard_map(
        shards,
        mesh=mesh,
        in_specs=(P(None, None, "gz", "ta", None),),
        out_specs=P(None, None, "gz", "ta", None),
        check_vma=False,
    )
```

```python
import functools
import math

import jax
import jax.numpy as jnp
import numpy as np
from jax import lax
from jax.experimental import pallas as pl
from jax.experimental.pallas import tpu as pltpu
from jax.sharding import PartitionSpec as P

ITERS = 2
STEP_SIZE = 0.08
LINE = 32
GZ = 16
TA = 32
PAIRS = ((0, 1), (0, 2), (1, 2))
LOGICAL = pl.DeviceIdType.LOGICAL
F32 = jnp.float32
BF16 = jnp.bfloat16


def halves(table):
    high = table.astype(jnp.bfloat16)
    return high, (table - high.astype(np.float64)).astype(jnp.bfloat16)


def tables():
    phase = 2.0 * np.pi * (np.outer(np.arange(LINE), np.arange(LINE)) % LINE) / LINE
    plane = np.kron(np.eye(4), (np.cos(phase) + np.sin(phase)) / np.sqrt(LINE))
    sines = 4.0 * np.sin(np.pi * np.arange(LINE) / LINE) ** 2
    row = np.arange(128)
    momenta = sines[row // 8 + 16 * (row % 2)][:, None] + np.tile(sines, 4)[None, :]
    tiles = np.broadcast_to(sines[:, None, None], (LINE, 8, 128))
    return (
        np.concatenate(halves(plane), axis=0),
        momenta.reshape(16, 8, 128).astype(np.float32),
        np.ascontiguousarray(tiles).astype(np.float32),
    )


def times(u, v):
    return (u[0] * v[0] - u[1] * v[1], u[0] * v[1] + u[1] * v[0])


def times_conj(u, v):
    return (u[0] * v[0] + u[1] * v[1], u[1] * v[0] - u[0] * v[1])


def plus(u, v):
    return (u[0] + v[0], u[1] + v[1])


def minus(u, v):
    return (u[0] - v[0], u[1] - v[1])


def conj(u):
    return (u[0], -u[1])


def scaled(u, factor):
    return (u[0] * factor, u[1] * factor)


def total(terms):
    return functools.reduce(plus, terms)


def product(left, right):
    return [[total([times(left[a][j], right[j][b]) for j in range(3)]) for b in range(3)] for a in range(len(left))]


def product_dagger(left, right):
    return [[total([times_conj(left[a][j], right[b][j]) for j in range(3)]) for b in range(3)] for a in range(len(left))]


def cross_conj(u, v):
    row = []
    for c in range(3):
        n, m = (c + 1) % 3, (c + 2) % 3
        row.append(conj(minus(times(u[n], v[m]), times(u[m], v[n]))))
    return row


def each(function, matrix):
    return [[(function(e[0]), function(e[1])) for e in row] for row in matrix]


def lanes(v):
    return lax.broadcasted_iota(jnp.int32, v.shape, v.ndim - 1)


def roll(v, shift, axis):
    return pltpu.roll(v, shift, axis)


def behind_x(v):
    moved = roll(v, 32, v.ndim - 1)
    return jnp.where(lanes(v) < 32, roll(moved, 1, v.ndim - 2), moved)


def ahead_x(v):
    moved = roll(v, 96, v.ndim - 1)
    return jnp.where(lanes(v) >= 96, roll(moved, 7, v.ndim - 2), moved)


def behind_y(v):
    return jnp.where(lanes(v) % 32 == 0, roll(v, 97, v.ndim - 1), roll(v, 1, v.ndim - 1))


def ahead_y(v):
    return jnp.where(lanes(v) % 32 == 31, roll(v, 31, v.ndim - 1), roll(v, 127, v.ndim - 1))


def behind_z(v, edge):
    return jnp.concatenate([edge[None], v[:1]], axis=0)


def ahead_z(v, edge):
    return jnp.concatenate([v[1:], edge[None]], axis=0)


def projected(u):
    third = (u[0][0][1] + u[1][1][1] + u[2][2][1]) * (1.0 / 3.0)
    return (
        [u[a][b][0] - u[b][a][0] for a, b in PAIRS]
        + [u[a][b][1] + u[b][a][1] for a, b in PAIRS]
        + [u[0][0][1] - third, u[1][1][1] - third]
    )


def block_transpose(planes):
    lane = lanes(planes[0])
    axis = planes[0].ndim - 1
    low = lane < 64
    even = (lane // 32) % 2 == 0
    first = [jnp.where(low, planes[p], roll(planes[p + 2], 64, axis)) for p in range(2)]
    second = [jnp.where(low, roll(planes[p], 64, axis), planes[p + 2]) for p in range(2)]
    out = []
    for one, two in (first, second):
        out.append(jnp.where(even, one, roll(two, 32, axis)))
        out.append(jnp.where(even, roll(one, 96, axis), two))
    return out


def rows_of(v):
    return lax.broadcasted_iota(jnp.int32, v.shape, v.ndim - 2)


def bit_exchange(one, two, stride):
    clear = lax.rem(lax.div(rows_of(one), stride), 2) == 0
    return (
        jnp.where(clear, one, roll(two, stride, one.ndim - 2)),
        jnp.where(clear, roll(one, 8 - stride, one.ndim - 2), two),
    )


def middle_exchange(v):
    pair = lax.div(rows_of(v), 2)
    return jnp.where(pair == 1, roll(v, 6, 0), jnp.where(pair == 2, roll(v, 2, 0), v))


def hartley(v):
    size = len(v)
    if size == 1:
        return v
    even, odd = hartley(v[0::2]), hartley(v[1::2])
    half = size // 2
    out = [None] * size
    for k in range(half):
        turned = odd[k]
        if k and 4 * k != size:
            angle = 2.0 * math.pi * k / size
            turned = odd[k] * math.cos(angle) + odd[half - k] * math.sin(angle)
        out[k], out[k + half] = even[k] + turned, even[k] - turned
    return out


def bit_clear(v, stride):
    return lax.rem(lax.div(rows_of(v), stride), 2) == 0


def rotated(v, stride):
    low = bit_clear(v[0], stride)
    out = list(v)
    for k in range(1, 16):
        if k != 8:
            angle = math.pi * k / 16
            out[k] = v[k] * jnp.where(low, 1.0, math.cos(angle)) + v[16 - k] * jnp.where(low, 0.0, math.sin(angle))
    return out


def butterflies(v, stride):
    low = bit_clear(v[0], stride)
    out = []
    for e in v:
        other = roll(e, stride, 0)
        if stride != 4:
            other = jnp.where(low, roll(e, 8 - stride, 0), other)
        out.append(other + jnp.where(low, e, -e))
    return out


def fine_to_coarse(v, stride):
    return butterflies(rotated(hartley(v), stride), stride)


def coarse_to_fine(v, stride):
    return hartley(rotated(butterflies(v, stride), stride))


def tiles_of(matrix):
    return [matrix[8 * i : 8 * i + 8] for i in range(16)]


def plane_forward(fields, table):
    parts = [block_transpose(fields[tl]) for tl in range(2)]
    tiles = [None] * 16
    for b in range(4):
        traded = [bit_exchange(parts[tl][b][0], parts[tl][b][1], 2) for tl in range(2)]
        for bit in range(2):
            tiles[8 * bit + b], tiles[8 * bit + 4 + b] = bit_exchange(traded[0][bit], traded[1][bit], 1)
    tiles = [middle_exchange(v) for v in coarse_to_fine(tiles, 4)]
    return tiles if table is None else right(jnp.concatenate(tiles, axis=0), table)


def plane_inverse(matrix, table):
    tiles = fine_to_coarse([middle_exchange(v) for v in tiles_of(right(matrix, table))], 4)
    blocks = [[None] * 4 for _ in range(2)]
    for b in range(4):
        pairs = [bit_exchange(tiles[8 * bit + b], tiles[8 * bit + 4 + b], 1) for bit in range(2)]
        for tl in range(2):
            blocks[tl][b] = jnp.stack(bit_exchange(pairs[0][tl], pairs[1][tl], 2))
    return [block_transpose(blocks[tl]) for tl in range(2)]


def split(v):
    high = v.astype(BF16)
    return high, (v - high.astype(F32)).astype(BF16)


def right(v, table):
    table_high, table_low = table[pl.ds(0, 128)], table[pl.ds(128, 128)]
    high, low = split(v)
    return jnp.dot(
        jnp.concatenate([high, low, high], axis=1),
        jnp.concatenate([table_high, table_high, table_low], axis=0),
        preferred_element_type=F32,
    )


def store_tiles(ref, tiles):
    for i, tile in enumerate(tiles):
        ref[pl.ds(8 * i, 8)] = tile


def load_tiles(ref):
    return [ref[pl.ds(8 * i, 8)] for i in range(16)]


def inverse_momenta(momenta, tiles):
    row = lax.broadcasted_iota(jnp.int32, (8, 128), 0)
    own = jnp.where(row < 4, tiles[0], tiles[1]) + jnp.where(lax.rem(lax.div(row, 2), 2) == 0, tiles[2], tiles[3])
    squares = momenta + own[None]
    positive = squares > 0.001
    return jnp.where(positive, (16.0 * STEP_SIZE / LINE**3) / jnp.where(positive, squares, 1.0), 0.0).reshape(128, 128)


def normalized(row):
    norm = functools.reduce(jnp.add, [e[0] * e[0] + e[1] * e[1] for e in row])
    scale = lax.rsqrt(norm)
    return [scaled(e, scale) for e in row]


def gauge_rows(fields):
    a, b, c = [(fields[i], fields[3 + i]) for i in range(3)]
    h0, h1 = fields[6], fields[7]
    h2 = -(h0 + h1)
    aa, bb, cc = [e[0] * e[0] + e[1] * e[1] for e in (a, b, c)]
    sixth = 1.0 / 6.0

    def turned(u, h):
        return (-(u[1] * h), u[0] * h)

    s01 = minus(turned(a, -h2), times_conj(b, c))
    s02 = plus(turned(b, -h1), times(a, c))
    s12 = minus(turned(c, -h0), times_conj(b, a))
    d0 = 1.0 - (h0 * h0 + aa + bb) * sixth
    d1 = 1.0 - (h1 * h1 + aa + cc) * sixth
    d2 = 1.0 - (h2 * h2 + bb + cc) * sixth

    def upper(u, s):
        return (0.5 * u[0] + s[0] * sixth, 0.5 * u[1] + s[1] * sixth)

    def lower(u, s):
        return (s[0] * sixth - 0.5 * u[0], 0.5 * u[1] - s[1] * sixth)

    inner = [
        [(d0, 0.5 * h0), upper(a, s01), upper(b, s02)],
        [lower(a, s01), (d1, 0.5 * h1), upper(c, s12)],
        [lower(b, s02), lower(c, s12), (d2, 0.5 * h2)],
    ]
    minus_a = (-a[0], a[1])
    p0 = [total([turned(inner[0][j], h0), times(a, inner[1][j]), times(b, inner[2][j])]) for j in range(3)]
    p1 = [total([times(minus_a, inner[0][j]), turned(inner[1][j], h1), times(c, inner[2][j])]) for j in range(3)]
    p0[0] = (p0[0][0] + 1.0, p0[0][1])
    p1[1] = (p1[1][0] + 1.0, p1[1][1])
    row0 = normalized(p0)
    overlap = total([times_conj(p1[j], row0[j]) for j in range(3)])
    row1 = normalized([minus(p1[j], times(overlap, row0[j])) for j in range(3)])
    return [row0, row1]


def completed(rows):
    return rows + [cross_conj(rows[0], rows[1])]


def load_matrix(ref):
    return [[(ref[2 * (3 * a + b)], ref[2 * (3 * a + b) + 1]) for b in range(3)] for a in range(3)]


def store_matrix(ref, matrix):
    for a, row in enumerate(matrix):
        for b, entry in enumerate(row):
            ref[2 * (3 * a + b)] = entry[0]
            ref[2 * (3 * a + b) + 1] = entry[1]


def load_rows(ref):
    return [[(ref[2 * (3 * a + b)], ref[2 * (3 * a + b) + 1]) for b in range(3)] for a in range(2)]


def kernel(
    links, table_hbm, momenta_hbm, sines_hbm, out, factor_t, follow_t,
    u, edge_z, edge_t, sum_send, sums, line_t_send, line_t, line_z_send, line_z, table, momenta, sines, weights,
    plane_send, plane_recv, ring_send, ring_recv, smooth, smooth_za, smooth_zb, smooth_ta, smooth_tb, gauge,
    load_sems, edge_ss, edge_rs, first_ss, first_rs, plane_ss, plane_rs, ring_ss, ring_rs, halo_ss, halo_rs,
):
    gz = lax.axis_index("gz")
    ta = lax.axis_index("ta")
    gz_x, gz_y = lax.div(gz, 4), lax.rem(gz, 4)
    chip, core = lax.div(ta, 2), lax.rem(ta, 2)
    other_core = 1 - core

    def device(z, t_chip, which):
        return z * TA + 2 * t_chip + which

    sibling = device(gz, chip, other_core)
    z_next, z_last = lax.rem(gz + 1, GZ), lax.rem(gz + GZ - 1, GZ)
    t_next, t_last = lax.rem(chip + 1, GZ), lax.rem(chip + GZ - 1, GZ)

    def around(place, step, size):
        return lax.rem(place + step, size)

    offsets = [(dx, dy) for dx in range(4) for dy in range(4) if dx or dy]
    offsets.sort(key=lambda o: -(min(o[0], 4 - o[0]) + min(o[1], 4 - o[1])))
    columns = [around(gz_x, dx, 4) for dx in range(4)]
    lines_y = [around(gz_y, dy, 4) for dy in range(4)]
    plane_partners = [(i, device(i, chip, core)) for i in [columns[dx] * 4 + lines_y[dy] for dx, dy in offsets]]
    steps = sorted(range(1, 16), key=lambda d: -min(d, 16 - d))
    ring_partners = [(i, device(gz, i, core)) for i in [around(chip, d, 16) for d in steps]]
    crossed = [
        device(gz, t_last, other_core),
        device(gz, t_next, other_core),
        device(z_last, chip, other_core),
        device(z_next, chip, other_core),
    ]

    barrier = pltpu.get_barrier_semaphore()

    def greet(target):
        pl.semaphore_signal(barrier, inc=1, device_id=target, device_id_type=LOGICAL)

    loads = [pltpu.make_async_copy(links.at[mu], u.at[core, mu], load_sems.at[mu]) for mu in range(4)]
    constants = [
        pltpu.make_async_copy(momenta_hbm, momenta, load_sems.at[4]),
        pltpu.make_async_copy(sines_hbm.at[chip], sines.at[0], load_sems.at[5]),
        pltpu.make_async_copy(sines_hbm.at[chip + 16], sines.at[1], load_sems.at[6]),
        pltpu.make_async_copy(sines_hbm.at[2 * gz], sines.at[2], load_sems.at[7]),
        pltpu.make_async_copy(sines_hbm.at[2 * gz + 1], sines.at[3], load_sems.at[8]),
        pltpu.make_async_copy(table_hbm, table, load_sems.at[9]),
    ]
    for copy in loads[::-1] + constants[-1:]:
        copy.start()
    for _, target in ring_partners + plane_partners:
        greet(target)
    for target in crossed + [sibling]:
        greet(target)
    for copy in constants[:-1]:
        copy.start()

    def transfer(src, dst, send_sem, recv_sem, target):
        return pltpu.make_async_remote_copy(
            src_ref=src, dst_ref=dst, send_sem=send_sem, recv_sem=recv_sem, device_id=target, device_id_type=LOGICAL
        )

    def exchange(sends, recvs, ss, rs, slot, partners, me, neighbour):
        send, recv = sends.at[slot], recvs.at[slot]
        own = pl.ds(pl.multiple_of(me * 8, 8), 8)

        for index, target in partners:
            theirs = pl.ds(pl.multiple_of(index * 8, 8), 8)
            transfer(send.at[theirs], recv.at[own], ss.at[slot], rs.at[slot], target).start()
        recv[own] = send[own]
        part = pl.ds(0, 120)
        return transfer(send.at[part], recv.at[part], ss.at[slot], rs.at[slot], neighbour)

    def plane_exchange(slot):
        neighbour = device(z_next, chip, core)
        return exchange(plane_send, plane_recv, plane_ss, plane_rs, slot, plane_partners, gz, neighbour)

    def ring_exchange(slot):
        neighbour = device(gz, t_next, core)
        return exchange(ring_send, ring_recv, ring_ss, ring_rs, slot, ring_partners, chip, neighbour)

    def halo_transfers(it):
        mine = smooth.at[it, core]
        ss, rs = halo_ss, halo_rs
        to_sibling = transfer(mine, mine, ss.at[it, 0], rs.at[it, 0], sibling)
        groups = []
        for which, (src, dst, z, t_chip) in enumerate(
            (
                (mine.at[0], smooth_ta.at[it, core], gz, t_last),
                (mine.at[:, :, 0], smooth_za.at[it, core], z_last, chip),
                (mine.at[1], smooth_tb.at[it, core], gz, t_next),
                (mine.at[:, :, 1], smooth_zb.at[it, core], z_next, chip),
            )
        ):
            groups.append(
                [
                    transfer(src, dst, ss.at[it, 1 + 2 * which + h], rs.at[it, 1 + which], device(z, t_chip, h))
                    for h in range(2)
                ]
            )
        if it == ITERS - 1:
            groups[1] = [
                transfer(
                    mine.at[h, :, 0], smooth_za.at[it, core, h], ss.at[it, 3 + h], rs.at[it, 2],
                    device(z_last, chip, h),
                )
                for h in range(2)
            ]
        return to_sibling, groups

    def arrived(it, which, ref):
        transfer(ref.at[it], ref.at[it], halo_ss.at[it, 0], halo_rs.at[it, 1 + which], sibling).wait_recv()

    lane_core = lax.broadcasted_iota(jnp.int32, (8, 128), 0) * 0 + core
    first_half = lane_core == 0

    def own_half(fields):
        return [jnp.where(jnp.broadcast_to(first_half, one.shape), one, two) for one, two in zip(fields[:4], fields[4:])]

    for copy in loads:
        copy.wait()
    lines = [projected(load_matrix(u.at[core, mu])) for mu in range(4)]
    planes = []
    for f in range(8):
        x, y, z, t = [lines[mu][f] for mu in range(4)]
        inner = jnp.concatenate([jnp.zeros((1, 8, 128), F32), z[:1]], axis=0)
        total_here = ((behind_x(x) - x) + (behind_y(y) - y)) + (inner - (z + t))
        planes += [total_here[0], total_here[1], t[0], t[1], z[1]]
    constants[-1].wait()
    planes = right(jnp.concatenate(planes, axis=0), table)
    for f in range(8):
        five = [planes[40 * f + 8 * i : 40 * f + 8 * i + 8] for i in range(5)]
        for z in range(2):
            sum_send[f // 4, f % 4, z] = five[z]
            line_t_send[f // 4, f % 4, z] = five[2 + z]
        line_z_send[f // 4, f % 4] = five[4]
    sums[core] = sum_send[core]

    @pl.when(core == 0)
    def _():
        line_t[1] = line_t_send[0]

    pl.semaphore_wait(barrier, 35)
    sum_out = transfer(sum_send.at[other_core], sums.at[core], first_ss.at[0], first_rs.at[0], sibling)
    sum_in = transfer(sums.at[other_core], sums.at[other_core], first_ss.at[0], first_rs.at[0], sibling)
    t_inner = transfer(line_t_send.at[1], line_t.at[1], first_ss.at[1], first_rs.at[1], sibling)
    t_outer = [
        transfer(line_t_send.at[h], line_t.at[0], first_ss.at[2 + h], first_rs.at[2], device(gz, t_next, h))
        for h in range(2)
    ]
    z_outer = [
        transfer(line_z_send.at[h], line_z.at[core], first_ss.at[4 + h], first_rs.at[3], device(z_next, chip, h))
        for h in range(2)
    ]

    @pl.when(core == 1)
    def _():
        for copy in t_outer:
            copy.start()

    for copy in z_outer:
        copy.start()
    sum_out.start()

    @pl.when(core == 0)
    def _():
        t_inner.start()

    for copy in constants[:-1]:
        copy.wait()
    weights[...] = inverse_momenta(momenta[...], [sines[i] for i in range(4)])
    sum_in.wait_recv()

    @pl.when(core == 1)
    def _():
        t_inner.wait_recv()

    transfer(line_z, line_z, first_ss.at[4], first_rs.at[3], sibling).wait_recv()
    t_outer[0].wait_recv()
    fields = []
    for tl in range(2):
        fields.append([])
        for f in range(4):
            value = sums[tl, f] + line_t[tl, f]
            edge = jnp.stack([line_z[tl, f], jnp.zeros((8, 128), F32)])
            value = value + edge
            factor = 0.5 if f < 2 else jnp.where(jnp.broadcast_to(first_half, value.shape), 0.5, 1.0)
            fields[tl].append(value * factor)
    store_tiles(plane_send.at[0], plane_forward(fields, None))

    to_sibling = [
        transfer(
            links.at[mu, pl.ds(0, 12)], u.at[core, mu, pl.ds(0, 12)], edge_ss.at[5 + mu], edge_rs.at[0], sibling
        )
        for mu in range(4)
    ]
    from_sibling = transfer(
        u.at[other_core, :, pl.ds(0, 12)], u.at[other_core, :, pl.ds(0, 12)], edge_ss.at[0], edge_rs.at[0], sibling
    )
    t_edges = [
        transfer(
            links.at[3, pl.ds(0, 12)], edge_t.at[pl.ds(0, 12)], edge_ss.at[1 + h], edge_rs.at[1], device(gz, t_next, h)
        )
        for h in range(2)
    ]
    z_edges = [
        transfer(
            links.at[2, pl.ds(0, 12), 1], edge_z.at[core, pl.ds(0, 12)], edge_ss.at[3 + h], edge_rs.at[2],
            device(z_next, chip, h),
        )
        for h in range(2)
    ]

    def everything_left():
        sum_out.wait_send()
        for copy in z_outer + z_edges + to_sibling:
            copy.wait_send()

        @pl.when(core == 0)
        def _():
            t_inner.wait_send()

        @pl.when(core == 1)
        def _():
            for copy in t_outer + t_edges:
                copy.wait_send()

        for slot in range(2 * ITERS):
            for send, ss, rs in ((plane_send, plane_ss, plane_rs), (ring_send, ring_ss, ring_rs)):
                part = send.at[slot, pl.ds(0, 120)]
                transfer(part, part, ss.at[slot], rs.at[slot], sibling).wait_send()
        for it in range(ITERS - 1):
            to_other, groups = halo_transfers(it)
            for copy in [to_other] + [copy for group in groups for copy in group]:
                copy.wait_send()

    def beside(it, which):
        if it == 0:
            to_sibling[which].start()
            if which in (1, 2):
                z_edges[which - 1].start()
            else:

                @pl.when(core == 1)
                def _():
                    t_edges[which // 3].start()

    for it in range(ITERS):
        last = it == ITERS - 1
        copy = plane_exchange(2 * it)
        beside(it, 0)
        copy.wait_recv()
        store_tiles(ring_send.at[2 * it], fine_to_coarse(load_tiles(plane_recv.at[2 * it]), 4))
        copy = ring_exchange(2 * it)
        beside(it, 1)
        copy.wait_recv()
        tiles = fine_to_coarse(load_tiles(ring_recv.at[2 * it]), 1)
        tiles = [v * w for v, w in zip(tiles, load_tiles(weights))]
        store_tiles(ring_send.at[2 * it + 1], coarse_to_fine(tiles, 1))
        copy = ring_exchange(2 * it + 1)
        beside(it, 2)
        copy.wait_recv()
        store_tiles(plane_send.at[2 * it + 1], coarse_to_fine(load_tiles(ring_recv.at[2 * it + 1]), 4))
        copy = plane_exchange(2 * it + 1)
        beside(it, 3)
        copy.wait_recv()
        fields = plane_inverse(plane_recv[2 * it + 1], table)
        for tl in range(2):
            for f in range(4):
                smooth[it, core, tl, f] = fields[tl][f]
        to_other, (ahead_t, ahead_z_, after_t, after_z) = halo_transfers(it)
        if last:
            order = ahead_z_ + ahead_t[1:] + [to_other]
        else:
            order = ahead_z_ + after_z + ahead_t + after_t + [to_other]
        for copy in order:
            copy.start()
        if not last:
            from_sibling.wait_recv()
            transfer(
                edge_z.at[:, pl.ds(0, 12)], edge_z.at[:, pl.ds(0, 12)], edge_ss.at[0], edge_rs.at[2], sibling
            ).wait_recv()
            t_edges[0].wait_recv()
            for ref in [u.at[other_core, mu] for mu in range(4)] + [edge_t, edge_z.at[0], edge_z.at[1]]:
                store_matrix(ref.at[pl.ds(12, 6)], [cross_conj(*load_rows(ref))])
        theirs = smooth.at[it, other_core]
        transfer(theirs, theirs, halo_ss.at[it, 0], halo_rs.at[it, 0], sibling).wait_recv()

        def keep(slot, rows):
            store_matrix(gauge.at[slot], rows)

        for tl in range(2):
            keep(tl, gauge_rows([smooth[it, f // 4, tl, f % 4] for f in range(8)]))

        def turned_inside(where, target):
            rows = load_rows(gauge.at[where])
            own = completed(rows)
            for mu, shift in ((0, ahead_x), (1, ahead_y)):
                turned = product_dagger(product(rows, load_matrix(u.at[where, mu])), each(shift, own))
                store_matrix(target.at[mu], completed(turned))
            for mu in (2, 3):
                left = factor_t if last and mu == 3 else u.at[where, mu]
                store_matrix(left, product(rows, load_matrix(u.at[where, mu])))

        def turned_z(where, target, plane, following):
            rows = product_dagger(load_rows(u.at[where, 2, :, plane]), completed(following))
            store_matrix(target.at[2, :, plane], completed(rows))

        def turned_t(where, target, following):
            rows = product_dagger(load_rows(u.at[where, 3]), completed(load_rows(gauge.at[following])))
            store_matrix(target.at[3], completed(rows))

        def edge_gauges(ref, tl):
            return [[tuple(v[tl] for v in e) for e in row] for row in ref]

        if last:
            turned_inside(core, out)
            turned_z(core, out, 0, load_rows(gauge.at[core, :, 1]))
            everything_left()
            part = smooth_za.at[it, :, core]
            transfer(part, part, halo_ss.at[it, 0], halo_rs.at[it, 2], sibling).wait_recv()
            turned_z(core, out, 1, gauge_rows([smooth_za[it, f // 4, core, f % 4] for f in range(8)]))

            @pl.when(core == 0)
            def _():
                follow_t[...] = gauge[1]

            @pl.when(core == 1)
            def _():
                arrived(it, 0, smooth_ta)
                store_matrix(follow_t, gauge_rows([smooth_ta[it, f // 4, f % 4] for f in range(8)]))
        else:
            for tl in range(2):
                turned_inside(tl, u.at[tl])
            here = [completed(load_rows(gauge.at[tl])) for tl in range(2)]
            store_matrix(edge_t, product_dagger(load_matrix(edge_t), here[0]))
            for tl in range(2):
                edge = product_dagger(load_matrix(edge_z.at[tl]), each(lambda v: v[0], here[tl]))
                store_matrix(edge_z.at[tl], edge)
            turned_t(0, u.at[0], 1)
            for tl in range(2):
                turned_z(tl, u.at[tl], 0, load_rows(gauge.at[tl, :, 1]))
            even_t = own_half(projected(load_matrix(u.at[0, 3])))
            for tl in range(2):
                x, y = [own_half(projected(load_matrix(u.at[tl, mu]))) for mu in range(2)]
                z = own_half(projected(load_matrix(u.at[tl, 2, :, 0])))
                for f in range(4):
                    value = ((behind_x(x[f]) - x[f]) + (behind_y(y[f]) - y[f])) + jnp.stack([-z[f], z[f]])
                    sums[tl, f] = value + even_t[f] if tl else value - even_t[f]
            arrived(it, 1, smooth_za)
            edges = gauge_rows([smooth_za[it, f // 4, :, f % 4] for f in range(8)])
            for tl in range(2):
                turned_z(tl, u.at[tl], 1, edge_gauges(edges, tl))
            arrived(it, 3, smooth_zb)
            edges = gauge_rows([smooth_zb[it, f // 4, :, f % 4] for f in range(8)])
            z_edge = [
                own_half(projected(completed(product(edge_gauges(edges, tl), load_matrix(edge_z.at[tl])))))
                for tl in range(2)
            ]
            z_last_plane = [own_half(projected(load_matrix(u.at[tl, 2, :, 1]))) for tl in range(2)]
            arrived(it, 0, smooth_ta)
            keep(2, gauge_rows([smooth_ta[it, f // 4, f % 4] for f in range(8)]))
            turned_t(1, u.at[1], 2)
            odd_t = own_half(projected(load_matrix(u.at[1, 3])))
            arrived(it, 2, smooth_tb)
            edges = gauge_rows([smooth_tb[it, f // 4, f % 4] for f in range(8)])
            t_edge = own_half(projected(completed(product(edges, load_matrix(edge_t)))))
            fields = []
            for tl in range(2):
                fields.append([])
                for f in range(4):
                    value = sums[tl, f] + jnp.stack([z_edge[tl][f], -z_last_plane[tl][f]])
                    value = value - odd_t[f] if tl else value + t_edge[f]
                    factor = 0.5 if f < 2 else jnp.where(jnp.broadcast_to(first_half, value.shape), 0.5, 1.0)
                    fields[tl].append(value * factor)
            plane_send[2 * it + 2] = plane_forward(fields, table)

    to_other, (ahead_t, ahead_z_, after_t, after_z) = halo_transfers(ITERS - 1)
    for copy in [to_other] + ahead_z_ + ahead_t[1:]:
        copy.wait_send()


def closing_kernel(done, factor_t, follow_t, out, last_links, sems):
    pieces = [(mu, pl.ds(9 * half, 9)) for mu in range(4) for half in range(2)]
    copies = [
        pltpu.make_async_copy((last_links if mu == 3 else done.at[mu]).at[part], out.at[mu, part], sems.at[i])
        for i, (mu, part) in enumerate(pieces)
    ]
    for copy in copies[:6]:
        copy.start()
    store_matrix(last_links, completed(product_dagger(load_rows(factor_t), completed(load_rows(follow_t)))))
    for copy in copies[6:]:
        copy.start()
    for copy in copies:
        copy.wait()


def shards(links):
    constants = [jnp.asarray(t) for t in tables()]
    anywhere = pl.BlockSpec(memory_space=pl.ANY)
    vmem = pltpu.VMEM
    dma = pltpu.SemaphoreType.DMA
    slots = 2 * ITERS
    parts = pl.pallas_call(
        kernel,
        out_shape=[vmem((3, 18, 2, 8, 128), F32), vmem((12, 2, 8, 128), F32), vmem((12, 2, 8, 128), F32)],
        in_specs=[anywhere] * 4,
        out_specs=[pl.BlockSpec(memory_space=vmem)] * 3,
        scratch_shapes=[
            vmem((2, 4, 18, 2, 8, 128), F32),
            vmem((2, 18, 8, 128), F32),
            vmem((18, 2, 8, 128), F32),
            vmem((2, 4, 2, 8, 128), F32),
            vmem((2, 4, 2, 8, 128), F32),
            vmem((2, 4, 2, 8, 128), F32),
            vmem((2, 4, 2, 8, 128), F32),
            vmem((2, 4, 8, 128), F32),
            vmem((2, 4, 8, 128), F32),
            vmem((256, 128), BF16),
            vmem((16, 8, 128), F32),
            vmem((4, 8, 128), F32),
            vmem((128, 128), F32),
            vmem((slots, 128, 128), F32),
            vmem((slots, 128, 128), F32),
            vmem((slots, 128, 128), F32),
            vmem((slots, 128, 128), F32),
            vmem((ITERS, 2, 2, 4, 2, 8, 128), F32),
            vmem((ITERS, 2, 2, 4, 8, 128), F32),
            vmem((ITERS, 2, 2, 4, 8, 128), F32),
            vmem((ITERS, 2, 4, 2, 8, 128), F32),
            vmem((ITERS, 2, 4, 2, 8, 128), F32),
            vmem((3, 12, 2, 8, 128), F32),
            dma((10,)),
            dma((9,)),
            dma((3,)),
            dma((6,)),
            dma((4,)),
            dma((slots,)),
            dma((slots,)),
            dma((slots,)),
            dma((slots,)),
            dma((ITERS, 9)),
            dma((ITERS, 5)),
        ],
        compiler_params=pltpu.CompilerParams(
            collective_id=0, has_side_effects=True, vmem_limit_bytes=40 * 1024 * 1024
        ),
    )(*[pltpu.with_memory_space_constraint(a, pltpu.HBM) for a in [links.reshape(4, 18, 2, 8, 128)] + constants])
    result = pl.pallas_call(
        closing_kernel,
        out_shape=jax.ShapeDtypeStruct((4, 18, 2, 8, 128), F32),
        in_specs=[pl.BlockSpec(memory_space=vmem)] * 3,
        out_specs=anywhere,
        scratch_shapes=[vmem((18, 2, 8, 128), F32), dma((8,))],
        compiler_params=pltpu.CompilerParams(vmem_limit_bytes=40 * 1024 * 1024),
    )(*parts)
    return result.reshape(links.shape)


def solution(mesh):
    return jax.shard_map(
        shards,
        mesh=mesh,
        in_specs=(P(None, None, "gz", "ta", None),),
        out_specs=P(None, None, "gz", "ta", None),
        check_vma=False,
    )
```

```python
import functools
import math

import jax
import jax.numpy as jnp
import numpy as np
from jax import lax
from jax.experimental import pallas as pl
from jax.experimental.pallas import tpu as pltpu
from jax.sharding import PartitionSpec as P

ITERS = 2
STEP_SIZE = 0.08
LINE = 32
GZ = 16
TA = 32
PAIRS = ((0, 1), (0, 2), (1, 2))
LOGICAL = pl.DeviceIdType.LOGICAL
F32 = jnp.float32
BF16 = jnp.bfloat16


def halves(table):
    high = table.astype(jnp.bfloat16)
    return high, (table - high.astype(np.float64)).astype(jnp.bfloat16)


def tables():
    phase = 2.0 * np.pi * (np.outer(np.arange(LINE), np.arange(LINE)) % LINE) / LINE
    plane = np.kron(np.eye(4), (np.cos(phase) + np.sin(phase)) / np.sqrt(LINE))
    sines = 4.0 * np.sin(np.pi * np.arange(LINE) / LINE) ** 2
    row = np.arange(128)
    momenta = sines[row // 8 + 16 * (row % 2)][:, None] + np.tile(sines, 4)[None, :]
    tiles = np.broadcast_to(sines[:, None, None], (LINE, 8, 128))
    return (
        np.concatenate(halves(plane), axis=0),
        momenta.reshape(16, 8, 128).astype(np.float32),
        np.ascontiguousarray(tiles).astype(np.float32),
    )


def times(u, v):
    return (u[0] * v[0] - u[1] * v[1], u[0] * v[1] + u[1] * v[0])


def times_conj(u, v):
    return (u[0] * v[0] + u[1] * v[1], u[1] * v[0] - u[0] * v[1])


def plus(u, v):
    return (u[0] + v[0], u[1] + v[1])


def minus(u, v):
    return (u[0] - v[0], u[1] - v[1])


def conj(u):
    return (u[0], -u[1])


def scaled(u, factor):
    return (u[0] * factor, u[1] * factor)


def total(terms):
    return functools.reduce(plus, terms)


def product(left, right):
    return [[total([times(left[a][j], right[j][b]) for j in range(3)]) for b in range(3)] for a in range(len(left))]


def product_dagger(left, right):
    return [[total([times_conj(left[a][j], right[b][j]) for j in range(3)]) for b in range(3)] for a in range(len(left))]


def cross_conj(u, v):
    row = []
    for c in range(3):
        n, m = (c + 1) % 3, (c + 2) % 3
        row.append(conj(minus(times(u[n], v[m]), times(u[m], v[n]))))
    return row


def each(function, matrix):
    return [[(function(e[0]), function(e[1])) for e in row] for row in matrix]


def lanes(v):
    return lax.broadcasted_iota(jnp.int32, v.shape, v.ndim - 1)


def roll(v, shift, axis):
    return pltpu.roll(v, shift, axis)


def behind_x(v):
    moved = roll(v, 32, v.ndim - 1)
    return jnp.where(lanes(v) < 32, roll(moved, 1, v.ndim - 2), moved)


def ahead_x(v):
    moved = roll(v, 96, v.ndim - 1)
    return jnp.where(lanes(v) >= 96, roll(moved, 7, v.ndim - 2), moved)


def behind_y(v):
    return jnp.where(lanes(v) % 32 == 0, roll(v, 97, v.ndim - 1), roll(v, 1, v.ndim - 1))


def ahead_y(v):
    return jnp.where(lanes(v) % 32 == 31, roll(v, 31, v.ndim - 1), roll(v, 127, v.ndim - 1))


def behind_z(v, edge):
    return jnp.concatenate([edge[None], v[:1]], axis=0)


def ahead_z(v, edge):
    return jnp.concatenate([v[1:], edge[None]], axis=0)


def projected(u):
    third = (u[0][0][1] + u[1][1][1] + u[2][2][1]) * (1.0 / 3.0)
    return (
        [u[a][b][0] - u[b][a][0] for a, b in PAIRS]
        + [u[a][b][1] + u[b][a][1] for a, b in PAIRS]
        + [u[0][0][1] - third, u[1][1][1] - third]
    )


def block_transpose(planes):
    lane = lanes(planes[0])
    axis = planes[0].ndim - 1
    low = lane < 64
    even = (lane // 32) % 2 == 0
    first = [jnp.where(low, planes[p], roll(planes[p + 2], 64, axis)) for p in range(2)]
    second = [jnp.where(low, roll(planes[p], 64, axis), planes[p + 2]) for p in range(2)]
    out = []
    for one, two in (first, second):
        out.append(jnp.where(even, one, roll(two, 32, axis)))
        out.append(jnp.where(even, roll(one, 96, axis), two))
    return out


def rows_of(v):
    return lax.broadcasted_iota(jnp.int32, v.shape, v.ndim - 2)


def bit_exchange(one, two, stride):
    clear = lax.rem(lax.div(rows_of(one), stride), 2) == 0
    return (
        jnp.where(clear, one, roll(two, stride, one.ndim - 2)),
        jnp.where(clear, roll(one, 8 - stride, one.ndim - 2), two),
    )


def middle_exchange(v):
    pair = lax.div(rows_of(v), 2)
    return jnp.where(pair == 1, roll(v, 6, 0), jnp.where(pair == 2, roll(v, 2, 0), v))


def hartley(v):
    size = len(v)
    if size == 1:
        return v
    even, odd = hartley(v[0::2]), hartley(v[1::2])
    half = size // 2
    out = [None] * size
    for k in range(half):
        turned = odd[k]
        if k and 4 * k != size:
            angle = 2.0 * math.pi * k / size
            turned = odd[k] * math.cos(angle) + odd[half - k] * math.sin(angle)
        out[k], out[k + half] = even[k] + turned, even[k] - turned
    return out


def bit_clear(v, stride):
    return lax.rem(lax.div(rows_of(v), stride), 2) == 0


def rotated(v, stride):
    low = bit_clear(v[0], stride)
    out = list(v)
    for k in range(1, 16):
        if k != 8:
            angle = math.pi * k / 16
            out[k] = v[k] * jnp.where(low, 1.0, math.cos(angle)) + v[16 - k] * jnp.where(low, 0.0, math.sin(angle))
    return out


def butterflies(v, stride):
    low = bit_clear(v[0], stride)
    out = []
    for e in v:
        other = roll(e, stride, 0)
        if stride != 4:
            other = jnp.where(low, roll(e, 8 - stride, 0), other)
        out.append(other + jnp.where(low, e, -e))
    return out


def fine_to_coarse(v, stride):
    return butterflies(rotated(hartley(v), stride), stride)


def coarse_to_fine(v, stride):
    return hartley(rotated(butterflies(v, stride), stride))


def tiles_of(matrix):
    return [matrix[8 * i : 8 * i + 8] for i in range(16)]


def plane_forward(fields, table):
    parts = [block_transpose(fields[tl]) for tl in range(2)]
    tiles = [None] * 16
    for b in range(4):
        traded = [bit_exchange(parts[tl][b][0], parts[tl][b][1], 2) for tl in range(2)]
        for bit in range(2):
            tiles[8 * bit + b], tiles[8 * bit + 4 + b] = bit_exchange(traded[0][bit], traded[1][bit], 1)
    tiles = [middle_exchange(v) for v in coarse_to_fine(tiles, 4)]
    return tiles if table is None else right(jnp.concatenate(tiles, axis=0), table)


def plane_inverse(matrix, table):
    tiles = fine_to_coarse([middle_exchange(v) for v in tiles_of(right(matrix, table))], 4)
    blocks = [[None] * 4 for _ in range(2)]
    for b in range(4):
        pairs = [bit_exchange(tiles[8 * bit + b], tiles[8 * bit + 4 + b], 1) for bit in range(2)]
        for tl in range(2):
            blocks[tl][b] = jnp.stack(bit_exchange(pairs[0][tl], pairs[1][tl], 2))
    return [block_transpose(blocks[tl]) for tl in range(2)]


def split(v):
    high = v.astype(BF16)
    return high, (v - high.astype(F32)).astype(BF16)


def right(v, table):
    table_high, table_low = table[pl.ds(0, 128)], table[pl.ds(128, 128)]
    high, low = split(v)
    return jnp.dot(
        jnp.concatenate([high, low, high], axis=1),
        jnp.concatenate([table_high, table_high, table_low], axis=0),
        preferred_element_type=F32,
    )


def store_tiles(ref, tiles):
    for i, tile in enumerate(tiles):
        ref[pl.ds(8 * i, 8)] = tile


def load_tiles(ref):
    return [ref[pl.ds(8 * i, 8)] for i in range(16)]


def inverse_momenta(momenta, tiles):
    row = lax.broadcasted_iota(jnp.int32, (8, 128), 0)
    own = jnp.where(row < 4, tiles[0], tiles[1]) + jnp.where(lax.rem(lax.div(row, 2), 2) == 0, tiles[2], tiles[3])
    squares = momenta + own[None]
    positive = squares > 0.001
    return jnp.where(positive, (16.0 * STEP_SIZE / LINE**3) / jnp.where(positive, squares, 1.0), 0.0).reshape(128, 128)


def normalized(row):
    norm = functools.reduce(jnp.add, [e[0] * e[0] + e[1] * e[1] for e in row])
    scale = lax.rsqrt(norm)
    return [scaled(e, scale) for e in row]


def gauge_rows(fields):
    a, b, c = [(fields[i], fields[3 + i]) for i in range(3)]
    h0, h1 = fields[6], fields[7]
    h2 = -(h0 + h1)
    aa, bb, cc = [e[0] * e[0] + e[1] * e[1] for e in (a, b, c)]
    sixth = 1.0 / 6.0

    def turned(u, h):
        return (-(u[1] * h), u[0] * h)

    s01 = minus(turned(a, -h2), times_conj(b, c))
    s02 = plus(turned(b, -h1), times(a, c))
    s12 = minus(turned(c, -h0), times_conj(b, a))
    d0 = 1.0 - (h0 * h0 + aa + bb) * sixth
    d1 = 1.0 - (h1 * h1 + aa + cc) * sixth
    d2 = 1.0 - (h2 * h2 + bb + cc) * sixth

    def upper(u, s):
        return (0.5 * u[0] + s[0] * sixth, 0.5 * u[1] + s[1] * sixth)

    def lower(u, s):
        return (s[0] * sixth - 0.5 * u[0], 0.5 * u[1] - s[1] * sixth)

    inner = [
        [(d0, 0.5 * h0), upper(a, s01), upper(b, s02)],
        [lower(a, s01), (d1, 0.5 * h1), upper(c, s12)],
        [lower(b, s02), lower(c, s12), (d2, 0.5 * h2)],
    ]
    minus_a = (-a[0], a[1])
    p0 = [total([turned(inner[0][j], h0), times(a, inner[1][j]), times(b, inner[2][j])]) for j in range(3)]
    p1 = [total([times(minus_a, inner[0][j]), turned(inner[1][j], h1), times(c, inner[2][j])]) for j in range(3)]
    p0[0] = (p0[0][0] + 1.0, p0[0][1])
    p1[1] = (p1[1][0] + 1.0, p1[1][1])
    row0 = normalized(p0)
    overlap = total([times_conj(p1[j], row0[j]) for j in range(3)])
    row1 = normalized([minus(p1[j], times(overlap, row0[j])) for j in range(3)])
    return [row0, row1]


def completed(rows):
    return rows + [cross_conj(rows[0], rows[1])]


def load_matrix(ref):
    return [[(ref[2 * (3 * a + b)], ref[2 * (3 * a + b) + 1]) for b in range(3)] for a in range(3)]


def store_matrix(ref, matrix):
    for a, row in enumerate(matrix):
        for b, entry in enumerate(row):
            ref[2 * (3 * a + b)] = entry[0]
            ref[2 * (3 * a + b) + 1] = entry[1]


def load_rows(ref):
    return [[(ref[2 * (3 * a + b)], ref[2 * (3 * a + b) + 1]) for b in range(3)] for a in range(2)]


def kernel(
    links, table_hbm, momenta_hbm, sines_hbm, out, factor_t, follow_t,
    u, edge_z, edge_t, sum_send, sums, line_t_send, line_t, line_z_send, line_z, table, momenta, sines, weights,
    plane_send, plane_recv, ring_send, ring_recv, smooth, smooth_za, smooth_zb, smooth_ta, smooth_tb, gauge,
    load_sems, edge_ss, edge_rs, first_ss, first_rs, plane_ss, plane_rs, ring_ss, ring_rs, halo_ss, halo_rs,
):
    gz = lax.axis_index("gz")
    ta = lax.axis_index("ta")
    gz_x, gz_y = lax.div(gz, 4), lax.rem(gz, 4)
    chip, core = lax.div(ta, 2), lax.rem(ta, 2)
    other_core = 1 - core

    def device(z, t_chip, which):
        return z * TA + 2 * t_chip + which

    sibling = device(gz, chip, other_core)
    z_next, z_last = lax.rem(gz + 1, GZ), lax.rem(gz + GZ - 1, GZ)
    t_next, t_last = lax.rem(chip + 1, GZ), lax.rem(chip + GZ - 1, GZ)

    def around(place, step, size):
        return lax.rem(place + step, size)

    offsets = [(dx, dy) for dx in range(4) for dy in range(4) if dx or dy]
    offsets.sort(key=lambda o: -(min(o[0], 4 - o[0]) + min(o[1], 4 - o[1])))
    sign = 1 - 2 * core
    columns = [around(gz_x + 4, dx * sign, 4) for dx in range(4)]
    lines_y = [around(gz_y + 4, dy * sign, 4) for dy in range(4)]
    plane_partners = [(i, device(i, chip, core)) for i in [columns[dx] * 4 + lines_y[dy] for dx, dy in offsets]]
    steps = sorted(range(1, 16), key=lambda d: -min(d, 16 - d))
    ring_partners = [(i, device(gz, i, core)) for i in [around(chip + 16, d * sign, 16) for d in steps]]
    crossed = [
        device(gz, t_last, other_core),
        device(gz, t_next, other_core),
        device(z_last, chip, other_core),
        device(z_next, chip, other_core),
    ]

    barrier = pltpu.get_barrier_semaphore()

    def greet(target):
        pl.semaphore_signal(barrier, inc=1, device_id=target, device_id_type=LOGICAL)

    loads = [pltpu.make_async_copy(links.at[mu], u.at[core, mu], load_sems.at[mu]) for mu in range(4)]
    constants = [
        pltpu.make_async_copy(momenta_hbm, momenta, load_sems.at[4]),
        pltpu.make_async_copy(sines_hbm.at[chip], sines.at[0], load_sems.at[5]),
        pltpu.make_async_copy(sines_hbm.at[chip + 16], sines.at[1], load_sems.at[6]),
        pltpu.make_async_copy(sines_hbm.at[2 * gz], sines.at[2], load_sems.at[7]),
        pltpu.make_async_copy(sines_hbm.at[2 * gz + 1], sines.at[3], load_sems.at[8]),
        pltpu.make_async_copy(table_hbm, table, load_sems.at[9]),
    ]
    for copy in loads[::-1] + constants[-1:]:
        copy.start()
    for _, target in ring_partners + plane_partners:
        greet(target)
    for target in crossed + [sibling]:
        greet(target)
    for copy in constants[:-1]:
        copy.start()

    def transfer(src, dst, send_sem, recv_sem, target):
        return pltpu.make_async_remote_copy(
            src_ref=src, dst_ref=dst, send_sem=send_sem, recv_sem=recv_sem, device_id=target, device_id_type=LOGICAL
        )

    def exchange(sends, recvs, ss, rs, slot, partners, me, neighbour):
        send, recv = sends.at[slot], recvs.at[slot]
        own = pl.ds(pl.multiple_of(me * 8, 8), 8)

        for index, target in partners:
            theirs = pl.ds(pl.multiple_of(index * 8, 8), 8)
            transfer(send.at[theirs], recv.at[own], ss.at[slot], rs.at[slot], target).start()
        recv[own] = send[own]
        part = pl.ds(0, 120)
        return transfer(send.at[part], recv.at[part], ss.at[slot], rs.at[slot], neighbour)

    def plane_exchange(slot):
        neighbour = device(z_next, chip, core)
        return exchange(plane_send, plane_recv, plane_ss, plane_rs, slot, plane_partners, gz, neighbour)

    def ring_exchange(slot):
        neighbour = device(gz, t_next, core)
        return exchange(ring_send, ring_recv, ring_ss, ring_rs, slot, ring_partners, chip, neighbour)

    def halo_transfers(it):
        mine = smooth.at[it, core]
        ss, rs = halo_ss, halo_rs
        to_sibling = transfer(mine, mine, ss.at[it, 0], rs.at[it, 0], sibling)
        groups = []
        for which, (src, dst, z, t_chip) in enumerate(
            (
                (mine.at[0], smooth_ta.at[it, core], gz, t_last),
                (mine.at[:, :, 0], smooth_za.at[it, core], z_last, chip),
                (mine.at[1], smooth_tb.at[it, core], gz, t_next),
                (mine.at[:, :, 1], smooth_zb.at[it, core], z_next, chip),
            )
        ):
            groups.append(
                [
                    transfer(src, dst, ss.at[it, 1 + 2 * which + h], rs.at[it, 1 + which], device(z, t_chip, h))
                    for h in range(2)
                ]
            )
        if it == ITERS - 1:
            groups[1] = [
                transfer(
                    mine.at[h, :, 0], smooth_za.at[it, core, h], ss.at[it, 3 + h], rs.at[it, 2],
                    device(z_last, chip, h),
                )
                for h in range(2)
            ]
        return to_sibling, groups

    def arrived(it, which, ref):
        transfer(ref.at[it], ref.at[it], halo_ss.at[it, 0], halo_rs.at[it, 1 + which], sibling).wait_recv()

    lane_core = lax.broadcasted_iota(jnp.int32, (8, 128), 0) * 0 + core
    first_half = lane_core == 0

    def own_half(fields):
        return [jnp.where(jnp.broadcast_to(first_half, one.shape), one, two) for one, two in zip(fields[:4], fields[4:])]

    for copy in loads:
        copy.wait()
    lines = [projected(load_matrix(u.at[core, mu])) for mu in range(4)]
    planes = []
    for f in range(8):
        x, y, z, t = [lines[mu][f] for mu in range(4)]
        inner = jnp.concatenate([jnp.zeros((1, 8, 128), F32), z[:1]], axis=0)
        total_here = ((behind_x(x) - x) + (behind_y(y) - y)) + (inner - (z + t))
        planes += [total_here[0], total_here[1], t[0], t[1], z[1]]
    constants[-1].wait()
    planes = right(jnp.concatenate(planes, axis=0), table)
    for f in range(8):
        five = [planes[40 * f + 8 * i : 40 * f + 8 * i + 8] for i in range(5)]
        for z in range(2):
            sum_send[f // 4, f % 4, z] = five[z]
            line_t_send[f // 4, f % 4, z] = five[2 + z]
        line_z_send[f // 4, f % 4] = five[4]
    sums[core] = sum_send[core]

    @pl.when(core == 0)
    def _():
        line_t[1] = line_t_send[0]

    pl.semaphore_wait(barrier, 35)
    sum_out = transfer(sum_send.at[other_core], sums.at[core], first_ss.at[0], first_rs.at[0], sibling)
    sum_in = transfer(sums.at[other_core], sums.at[other_core], first_ss.at[0], first_rs.at[0], sibling)
    t_inner = transfer(line_t_send.at[1], line_t.at[1], first_ss.at[1], first_rs.at[1], sibling)
    t_outer = [
        transfer(line_t_send.at[h], line_t.at[0], first_ss.at[2 + h], first_rs.at[2], device(gz, t_next, h))
        for h in range(2)
    ]
    z_outer = [
        transfer(line_z_send.at[h], line_z.at[core], first_ss.at[4 + h], first_rs.at[3], device(z_next, chip, h))
        for h in range(2)
    ]

    @pl.when(core == 1)
    def _():
        for copy in t_outer:
            copy.start()

    for copy in z_outer:
        copy.start()
    sum_out.start()

    @pl.when(core == 0)
    def _():
        t_inner.start()

    for copy in constants[:-1]:
        copy.wait()
    weights[...] = inverse_momenta(momenta[...], [sines[i] for i in range(4)])
    sum_in.wait_recv()

    @pl.when(core == 1)
    def _():
        t_inner.wait_recv()

    transfer(line_z, line_z, first_ss.at[4], first_rs.at[3], sibling).wait_recv()
    t_outer[0].wait_recv()
    fields = []
    for tl in range(2):
        fields.append([])
        for f in range(4):
            value = sums[tl, f] + line_t[tl, f]
            edge = jnp.stack([line_z[tl, f], jnp.zeros((8, 128), F32)])
            value = value + edge
            factor = 0.5 if f < 2 else jnp.where(jnp.broadcast_to(first_half, value.shape), 0.5, 1.0)
            fields[tl].append(value * factor)
    store_tiles(plane_send.at[0], plane_forward(fields, None))

    to_sibling = [
        transfer(
            links.at[mu, pl.ds(0, 12)], u.at[core, mu, pl.ds(0, 12)], edge_ss.at[5 + mu], edge_rs.at[0], sibling
        )
        for mu in range(4)
    ]
    from_sibling = transfer(
        u.at[other_core, :, pl.ds(0, 12)], u.at[other_core, :, pl.ds(0, 12)], edge_ss.at[0], edge_rs.at[0], sibling
    )
    t_edges = [
        transfer(
            links.at[3, pl.ds(0, 12)], edge_t.at[pl.ds(0, 12)], edge_ss.at[1 + h], edge_rs.at[1], device(gz, t_next, h)
        )
        for h in range(2)
    ]
    z_edges = [
        transfer(
            links.at[2, pl.ds(0, 12), 1], edge_z.at[core, pl.ds(0, 12)], edge_ss.at[3 + h], edge_rs.at[2],
            device(z_next, chip, h),
        )
        for h in range(2)
    ]

    def everything_left():
        sum_out.wait_send()
        for copy in z_outer + z_edges + to_sibling:
            copy.wait_send()

        @pl.when(core == 0)
        def _():
            t_inner.wait_send()

        @pl.when(core == 1)
        def _():
            for copy in t_outer + t_edges:
                copy.wait_send()

        for slot in range(2 * ITERS):
            for send, ss, rs in ((plane_send, plane_ss, plane_rs), (ring_send, ring_ss, ring_rs)):
                part = send.at[slot, pl.ds(0, 120)]
                transfer(part, part, ss.at[slot], rs.at[slot], sibling).wait_send()
        for it in range(ITERS - 1):
            to_other, groups = halo_transfers(it)
            for copy in [to_other] + [copy for group in groups for copy in group]:
                copy.wait_send()

    def beside(it, which):
        if it == 0:
            to_sibling[which].start()
            if which in (1, 2):
                z_edges[which - 1].start()
            else:

                @pl.when(core == 1)
                def _():
                    t_edges[which // 3].start()

    for it in range(ITERS):
        last = it == ITERS - 1
        copy = plane_exchange(2 * it)
        beside(it, 0)
        copy.wait_recv()
        store_tiles(ring_send.at[2 * it], fine_to_coarse(load_tiles(plane_recv.at[2 * it]), 4))
        copy = ring_exchange(2 * it)
        beside(it, 1)
        copy.wait_recv()
        tiles = fine_to_coarse(load_tiles(ring_recv.at[2 * it]), 1)
        tiles = [v * w for v, w in zip(tiles, load_tiles(weights))]
        store_tiles(ring_send.at[2 * it + 1], coarse_to_fine(tiles, 1))
        copy = ring_exchange(2 * it + 1)
        beside(it, 2)
        copy.wait_recv()
        store_tiles(plane_send.at[2 * it + 1], coarse_to_fine(load_tiles(ring_recv.at[2 * it + 1]), 4))
        copy = plane_exchange(2 * it + 1)
        beside(it, 3)
        copy.wait_recv()
        fields = plane_inverse(plane_recv[2 * it + 1], table)
        for tl in range(2):
            for f in range(4):
                smooth[it, core, tl, f] = fields[tl][f]
        to_other, (ahead_t, ahead_z_, after_t, after_z) = halo_transfers(it)
        if last:
            order = ahead_z_ + ahead_t[1:] + [to_other]
        else:
            order = ahead_z_ + after_z + [to_other] + ahead_t + after_t
        for copy in order:
            copy.start()
        theirs = smooth.at[it, other_core]
        transfer(theirs, theirs, halo_ss.at[it, 0], halo_rs.at[it, 0], sibling).wait_recv()

        def keep(slot, rows):
            store_matrix(gauge.at[slot], rows)

        for tl in range(2):
            keep(tl, gauge_rows([smooth[it, f // 4, tl, f % 4] for f in range(8)]))

        def turned_inside(where, target):
            rows = load_rows(gauge.at[where])
            own = completed(rows)
            for mu, shift in ((0, ahead_x), (1, ahead_y)):
                turned = product_dagger(product(rows, load_matrix(u.at[where, mu])), each(shift, own))
                store_matrix(target.at[mu], completed(turned))
            for mu in (2, 3):
                left = factor_t if last and mu == 3 else u.at[where, mu]
                store_matrix(left, product(rows, load_matrix(u.at[where, mu])))

        def turned_z(where, target, plane, following):
            rows = product_dagger(load_rows(u.at[where, 2, :, plane]), completed(following))
            store_matrix(target.at[2, :, plane], completed(rows))

        def turned_t(where, target, following):
            rows = product_dagger(load_rows(u.at[where, 3]), completed(load_rows(gauge.at[following])))
            store_matrix(target.at[3], completed(rows))

        def edge_gauges(ref, tl):
            return [[tuple(v[tl] for v in e) for e in row] for row in ref]

        if last:
            turned_inside(core, out)
            turned_z(core, out, 0, load_rows(gauge.at[core, :, 1]))
            everything_left()
            part = smooth_za.at[it, :, core]
            transfer(part, part, halo_ss.at[it, 0], halo_rs.at[it, 2], sibling).wait_recv()
            turned_z(core, out, 1, gauge_rows([smooth_za[it, f // 4, core, f % 4] for f in range(8)]))

            @pl.when(core == 0)
            def _():
                follow_t[...] = gauge[1]

            @pl.when(core == 1)
            def _():
                arrived(it, 0, smooth_ta)
                store_matrix(follow_t, gauge_rows([smooth_ta[it, f // 4, f % 4] for f in range(8)]))
        else:
            from_sibling.wait_recv()
            transfer(
                edge_z.at[:, pl.ds(0, 12)], edge_z.at[:, pl.ds(0, 12)], edge_ss.at[0], edge_rs.at[2], sibling
            ).wait_recv()
            t_edges[0].wait_recv()
            missing = [completed(load_rows(u.at[other_core, mu])) for mu in range(4)]
            for mu in range(4):
                store_matrix(u.at[other_core, mu], missing[mu])
            for tl in range(2):
                turned_inside(tl, u.at[tl])
            here = [completed(load_rows(gauge.at[tl])) for tl in range(2)]
            store_matrix(edge_t, product_dagger(completed(load_rows(edge_t)), here[0]))
            for tl in range(2):
                edge = product_dagger(completed(load_rows(edge_z.at[tl])), each(lambda v: v[0], here[tl]))
                store_matrix(edge_z.at[tl], edge)
            turned_t(0, u.at[0], 1)
            for tl in range(2):
                turned_z(tl, u.at[tl], 0, load_rows(gauge.at[tl, :, 1]))
            even_t = own_half(projected(load_matrix(u.at[0, 3])))
            for tl in range(2):
                x, y = [own_half(projected(load_matrix(u.at[tl, mu]))) for mu in range(2)]
                z = own_half(projected(load_matrix(u.at[tl, 2, :, 0])))
                for f in range(4):
                    value = ((behind_x(x[f]) - x[f]) + (behind_y(y[f]) - y[f])) + jnp.stack([-z[f], z[f]])
                    sums[tl, f] = value + even_t[f] if tl else value - even_t[f]
            arrived(it, 1, smooth_za)
            edges = gauge_rows([smooth_za[it, f // 4, :, f % 4] for f in range(8)])
            for tl in range(2):
                turned_z(tl, u.at[tl], 1, edge_gauges(edges, tl))
            arrived(it, 3, smooth_zb)
            edges = gauge_rows([smooth_zb[it, f // 4, :, f % 4] for f in range(8)])
            z_edge = [
                own_half(projected(completed(product(edge_gauges(edges, tl), load_matrix(edge_z.at[tl])))))
                for tl in range(2)
            ]
            z_last_plane = [own_half(projected(load_matrix(u.at[tl, 2, :, 1]))) for tl in range(2)]
            arrived(it, 0, smooth_ta)
            keep(2, gauge_rows([smooth_ta[it, f // 4, f % 4] for f in range(8)]))
            turned_t(1, u.at[1], 2)
            odd_t = own_half(projected(load_matrix(u.at[1, 3])))
            arrived(it, 2, smooth_tb)
            edges = gauge_rows([smooth_tb[it, f // 4, f % 4] for f in range(8)])
            t_edge = own_half(projected(completed(product(edges, load_matrix(edge_t)))))
            fields = []
            for tl in range(2):
                fields.append([])
                for f in range(4):
                    value = sums[tl, f] + jnp.stack([z_edge[tl][f], -z_last_plane[tl][f]])
                    value = value - odd_t[f] if tl else value + t_edge[f]
                    factor = 0.5 if f < 2 else jnp.where(jnp.broadcast_to(first_half, value.shape), 0.5, 1.0)
                    fields[tl].append(value * factor)
            plane_send[2 * it + 2] = plane_forward(fields, table)

    to_other, (ahead_t, ahead_z_, after_t, after_z) = halo_transfers(ITERS - 1)
    for copy in [to_other] + ahead_z_ + ahead_t[1:]:
        copy.wait_send()


def closing_kernel(done, factor_t, follow_t, out, last_links, sems):
    pieces = [(mu, pl.ds(9 * half, 9)) for mu in range(4) for half in range(2)]
    copies = [
        pltpu.make_async_copy((last_links if mu == 3 else done.at[mu]).at[part], out.at[mu, part], sems.at[i])
        for i, (mu, part) in enumerate(pieces)
    ]
    for copy in copies[:6]:
        copy.start()
    store_matrix(last_links, completed(product_dagger(load_rows(factor_t), completed(load_rows(follow_t)))))
    for copy in copies[6:]:
        copy.start()
    for copy in copies:
        copy.wait()


def shards(links):
    constants = [jnp.asarray(t) for t in tables()]
    anywhere = pl.BlockSpec(memory_space=pl.ANY)
    vmem = pltpu.VMEM
    dma = pltpu.SemaphoreType.DMA
    slots = 2 * ITERS
    parts = pl.pallas_call(
        kernel,
        out_shape=[vmem((3, 18, 2, 8, 128), F32), vmem((12, 2, 8, 128), F32), vmem((12, 2, 8, 128), F32)],
        in_specs=[anywhere] * 4,
        out_specs=[pl.BlockSpec(memory_space=vmem)] * 3,
        scratch_shapes=[
            vmem((2, 4, 18, 2, 8, 128), F32),
            vmem((2, 18, 8, 128), F32),
            vmem((18, 2, 8, 128), F32),
            vmem((2, 4, 2, 8, 128), F32),
            vmem((2, 4, 2, 8, 128), F32),
            vmem((2, 4, 2, 8, 128), F32),
            vmem((2, 4, 2, 8, 128), F32),
            vmem((2, 4, 8, 128), F32),
            vmem((2, 4, 8, 128), F32),
            vmem((256, 128), BF16),
            vmem((16, 8, 128), F32),
            vmem((4, 8, 128), F32),
            vmem((128, 128), F32),
            vmem((slots, 128, 128), F32),
            vmem((slots, 128, 128), F32),
            vmem((slots, 128, 128), F32),
            vmem((slots, 128, 128), F32),
            vmem((ITERS, 2, 2, 4, 2, 8, 128), F32),
            vmem((ITERS, 2, 2, 4, 8, 128), F32),
            vmem((ITERS, 2, 2, 4, 8, 128), F32),
            vmem((ITERS, 2, 4, 2, 8, 128), F32),
            vmem((ITERS, 2, 4, 2, 8, 128), F32),
            vmem((3, 12, 2, 8, 128), F32),
            dma((10,)),
            dma((9,)),
            dma((3,)),
            dma((6,)),
            dma((4,)),
            dma((slots,)),
            dma((slots,)),
            dma((slots,)),
            dma((slots,)),
            dma((ITERS, 9)),
            dma((ITERS, 5)),
        ],
        compiler_params=pltpu.CompilerParams(
            collective_id=0, has_side_effects=True, vmem_limit_bytes=40 * 1024 * 1024
        ),
    )(*[pltpu.with_memory_space_constraint(a, pltpu.HBM) for a in [links.reshape(4, 18, 2, 8, 128)] + constants])
    result = pl.pallas_call(
        closing_kernel,
        out_shape=jax.ShapeDtypeStruct((4, 18, 2, 8, 128), F32),
        in_specs=[pl.BlockSpec(memory_space=vmem)] * 3,
        out_specs=anywhere,
        scratch_shapes=[vmem((18, 2, 8, 128), F32), dma((8,))],
        compiler_params=pltpu.CompilerParams(vmem_limit_bytes=40 * 1024 * 1024),
    )(*parts)
    return result.reshape(links.shape)


def solution(mesh):
    return jax.shard_map(
        shards,
        mesh=mesh,
        in_specs=(P(None, None, "gz", "ta", None),),
        out_specs=P(None, None, "gz", "ta", None),
        check_vma=False,
    )
```
